128 devices in a mesh: seq: 32 (over x, y, z_hi), tp: 4 (over z_lo, core).
Axes of the slice: x: 4, y: 4, z: 4 (z_hi: 2, z_lo: 2; z = z_hi * 2 + z_lo), core: 2. Of those that a mesh axis runs over, the one named last changes fastest.
Arguments:
- layer_in: bfloat16 [8192, 4096], P('seq'), may hold values from -24 to 24
- w_value: bfloat16 [4096, 4096], P(None, 'tp'), may hold values from -0.09375 to 0.09375
- short_taps: float32 [7, 4096], P(None, 'tp'), may hold values from -2 to 2
- long_filters: float32 [2, 4096, 8192], P(None, ('tp', 'seq')), may hold values from -0.046875 to 0.046875
- gate_proj: bfloat16 [8192, 4096], P('seq', 'tp'), may hold values from -6 to 6
- grad_out: bfloat16 [8192, 4096], P('seq', 'tp'), may hold values from -8 to 8
Outputs:
- grad_input: bfloat16 [8192, 4096], P('seq', 'tp')
- grad_weight: float32 [4096, 4096], P('seq', 'tp')
- grad_taps: float32 [7, 4096], P(None, 'tp')
- grad_filters: float32 [2, 4096, 8192], P(None, ('tp', 'seq'))
- grad_gate: bfloat16 [8192, 4096], P('seq', 'tp')
The draws below stay inside these ranges and needn't reach their ends.
All inputs are finite; a program needn't handle non-finite values.
Results may differ from the reference program's by a relative error of at most 0.0062.
Values may be sent and summed in bfloat16 or wider, within the bound.
No kernel may reach another device: no remote copies, remote signals or barrier semaphores. Data moves between devices by JAX's collectives and lax.ppermute only.
A program may use at most 128 MiB of HBM per device.

```python
import math
import jax
import jax.numpy as jnp
from jax import lax

D = 4096
TAPS = 7
TOKENS = 8192


def draw_layer_in(key, part):
    key = jax.random.fold_in(key, 11)
    first_key, second_key = jax.random.split(key)
    base_draw = jnp.clip(jax.random.normal(first_key, (TOKENS, D), jnp.float32), -4.0, 4.0)
    rise_log = math.log(3.0)
    jitter = jax.random.uniform(second_key, (TOKENS, 1), jnp.float32, 0.0, math.log(2.0))
    ramp_log = rise_log * jnp.arange(TOKENS, dtype=jnp.float32)[:, None] / (TOKENS - 1)
    return (base_draw * jnp.exp(ramp_log + jitter)).astype(jnp.bfloat16)


def draw_grad_out(key, part):
    key = jax.random.fold_in(key, 23)
    base_draw = 0.5 + 0.5 * jnp.clip(jax.random.normal(key, (TOKENS, D), jnp.float32), -4.0, 4.0)
    rise_log = math.log(3.0)
    ramp_log = rise_log * jnp.arange(TOKENS, dtype=jnp.float32)[:, None] / (TOKENS - 1)
    return (base_draw * jnp.exp(ramp_log)).astype(jnp.bfloat16)


def level_of(key, dims, cuts, smallest, high):
    gain, own = 1.0, jax.random.fold_in(key, 6)
    for axis_at, parts in cuts:
        steps = jnp.exp(jax.random.uniform(jax.random.fold_in(own, axis_at), (parts,), jnp.float32, smallest / len(cuts), high / len(cuts)))
        gain = gain * jnp.repeat(steps, dims[axis_at] // parts).reshape([-1 if axis == axis_at else 1 for axis in range(len(dims))])
    return gain


def noise(own_key, dims, spread, bound, shards=(), kind=jnp.bfloat16):
    array = spread * jax.random.normal(own_key, dims, jnp.float32)
    if shards:
        array = array * level_of(own_key, dims, shards, -0.22, 0.18)
    return jnp.clip(array, -bound, bound).astype(kind)


def setup_inputs(seed: int = 0) -> dict:
    key_of = jax.random.split(jax.random.key(seed), 7)
    return {
        "layer_in": draw_layer_in(jax.random.fold_in(key_of[6], 71), 0),
        "w_value": noise(key_of[1], (D, D), D ** -0.5, 0.09375, ((1, 4),)),
        "short_taps": noise(key_of[2], (TAPS, D), TAPS ** -0.5, 2.0, ((1, 4),), jnp.float32),
        "long_filters": noise(key_of[3], (2, D, TOKENS), (2 * TOKENS) ** -0.5, 0.046875, ((1, 128),), jnp.float32),
        "gate_proj": noise(key_of[4], (TOKENS, D), 1.5, 6.0, ((0, 32), (1, 4))),
        "grad_out": draw_grad_out(jax.random.fold_in(key_of[6], 71), 0),
    }


block_width = 128


def settle(value):
    return lax.optimization_barrier(value.astype(jnp.bfloat16)).astype(jnp.float32)


def silu_slope(value):
    sig_part = jax.nn.sigmoid(value)
    return sig_part * (1.0 + value * (1.0 - sig_part))


def wrap_kernel(filters):
    forward = filters[0]
    backward = filters[1]
    lead_tap = forward[:, :1] + backward[:, :1]
    zero_col = jnp.zeros_like(lead_tap)
    return jnp.concatenate([lead_tap, forward[:, 1:], zero_col, jnp.flip(backward[:, 1:], axis=1)], axis=1)


def mixer_block(inputs):
    values, gate_rows, grad_rows, tap_rows, filters = inputs
    length = values.shape[1]
    fft_length = 2 * length
    tap_reach = TAPS // 2
    value_pad = jnp.pad(values.astype(jnp.float32), ((0, 0), (tap_reach, tap_reach)))
    conv_sum = sum(tap_rows[offset][:, None] * value_pad[:, offset:offset + length] for offset in range(TAPS))
    short_conv = settle(conv_sum)
    pooled = jnp.sum(jax.nn.silu(short_conv), axis=1) / length
    gate_sig = jax.nn.sigmoid(gate_rows.astype(jnp.float32))
    slope_in = settle(grad_rows.astype(jnp.float32) * gate_sig)
    spec_short = jnp.fft.rfft(short_conv, n=fft_length, axis=1)
    spec_slope = jnp.fft.rfft(slope_in, n=fft_length, axis=1)
    spec_kernel = jnp.fft.rfft(wrap_kernel(filters), n=fft_length, axis=1)
    long_out = jnp.fft.irfft(spec_short * spec_kernel, n=fft_length, axis=1)[:, :length]
    long_slope = jnp.fft.irfft(jnp.conj(spec_kernel) * spec_slope, n=fft_length, axis=1)[:, :length]
    lag_grads = jnp.fft.irfft(jnp.conj(spec_short) * spec_slope, n=fft_length, axis=1)
    mixed_out = settle(long_out + pooled[:, None])
    grad_gate = (grad_rows.astype(jnp.float32) * mixed_out * gate_sig * (1.0 - gate_sig)).astype(jnp.bfloat16)
    mean_grad = jnp.sum(slope_in, axis=1)
    slope_back = settle(long_slope + (mean_grad / length)[:, None] * silu_slope(short_conv))
    slope_pad = jnp.pad(slope_back, ((0, 0), (tap_reach, tap_reach)))
    grad_values = sum(tap_rows[offset][:, None] * slope_pad[:, 2 * tap_reach - offset:2 * tap_reach - offset + length] for offset in range(TAPS))
    grad_values = grad_values.astype(jnp.bfloat16)
    grad_taps = jnp.stack([jnp.sum(slope_back * value_pad[:, offset:offset + length], axis=1) for offset in range(TAPS)])
    reverse_part = jnp.concatenate([lag_grads[:, :1], jnp.flip(lag_grads[:, length + 1:], axis=1)], axis=1)
    grad_filters = jnp.stack([lag_grads[:, :length], reverse_part])
    return grad_values, grad_gate, grad_taps, grad_filters


def reference(layer_in, w_value, short_taps, long_filters, gate_proj, grad_out):
    values = jnp.dot(layer_in, w_value, preferred_element_type=jnp.float32).astype(jnp.bfloat16)
    block_count = D // block_width

    def columns(matrix):
        return matrix.T.reshape(block_count, block_width, TOKENS)

    tap_blocks = short_taps.reshape(TAPS, block_count, block_width).transpose(1, 0, 2)
    filter_blocks = long_filters.reshape(2, block_count, block_width, TOKENS).transpose(1, 0, 2, 3)
    block_values, block_gates, block_taps, block_filters = lax.map(
        mixer_block, (columns(values), columns(gate_proj), columns(grad_out), tap_blocks, filter_blocks))
    grad_v = block_values.reshape(D, TOKENS).T
    grad_gate = block_gates.reshape(D, TOKENS).T
    grad_taps = block_taps.transpose(1, 0, 2).reshape(TAPS, D)
    grad_filters = block_filters.transpose(1, 0, 2, 3).reshape(2, D, TOKENS)
    grad_input = jnp.dot(grad_v, w_value.T, preferred_element_type=jnp.float32).astype(jnp.bfloat16)
    grad_weight = jnp.dot(layer_in.T, grad_v, preferred_element_type=jnp.float32)
    return grad_input, grad_weight, grad_taps, grad_filters, grad_gate
```

```python
import functools
import math

import jax
import jax.numpy as jnp
import ml_dtypes
import numpy as np
from jax import lax
from jax.experimental import pallas as pl
from jax.experimental.pallas import tpu as pltpu
from jax.sharding import PartitionSpec as P

LANES = 128
ROWS = 64
LENGTH = ROWS * LANES
TAPS = 7
REACH = TAPS // 2
BATCH = 4


def halves(table):
    high = table.astype(ml_dtypes.bfloat16)
    low = (table - high.astype(np.float64)).astype(ml_dtypes.bfloat16)
    return high, low


@functools.lru_cache(maxsize=None)
def tables(blocks):
    half = np.arange(ROWS) + 0.5
    natural = np.arange(ROWS)
    split = (2 * np.arange(blocks)[None, :] + np.arange(2)[:, None]).reshape(-1)

    def first(order):
        turn = 2.0 * math.pi / LANES * np.outer(half, order)
        return halves(np.concatenate([np.cos(turn), -np.sin(turn)], axis=0))

    def last(order):
        turn = 2.0 * math.pi / LANES * np.outer(order, half)
        return halves(np.concatenate([np.cos(turn), -np.sin(turn)], axis=1) / LENGTH)

    split_high, split_low = first(split)
    nat_high, nat_low = first(natural)
    first_split = np.concatenate([split_high, split_low], axis=1)
    first_nat = np.concatenate([nat_high, nat_low, nat_high, nat_low], axis=1)
    inv_split_high, inv_split_low = last(split)
    inv_nat_high, inv_nat_low = last(natural)
    last_split = np.concatenate([inv_split_high, inv_split_high, inv_split_low], axis=1)
    last_nat = np.concatenate([inv_nat_high, inv_nat_high, inv_nat_low], axis=1)
    twist = 2.0 * math.pi / (2 * LENGTH) * np.outer(half, np.arange(LANES))
    twist = np.stack([np.cos(twist), -np.sin(twist)]).astype(np.float32)
    grid = 2.0 * math.pi / LANES * np.outer(np.arange(LANES), np.arange(LANES))
    cos, sin = np.cos(grid), np.sin(grid)

    def stacked(table):
        high, low = halves(table)
        return np.concatenate([high, high, low], axis=0)

    forward = np.block([[cos, -sin], [sin, cos]])
    mirror = np.block([[cos, sin], [sin, -cos]])
    inverse = np.block([[cos, sin], [-sin, cos]])
    pair = np.concatenate([stacked(forward), stacked(mirror)], axis=0)
    both = np.concatenate([stacked(inverse), stacked(np.block([[cos, sin], [sin, -cos]]))], axis=1)
    return {
        "first_split": first_split, "first_nat": first_nat, "twist": twist, "forward": stacked(forward), "pair": pair,
        "inverse": stacked(inverse), "both": both, "last_split": last_split, "last_nat": last_nat,
    }


def cut(value):
    high = value.astype(jnp.bfloat16)
    low = (value - high.astype(jnp.float32)).astype(jnp.bfloat16)
    return high, low


def store_parts(ref, row, col, real, imag):
    real_high, real_low = cut(real)
    imag_high, imag_low = cut(imag)
    parts = (real_high, imag_high, real_low, imag_low, real_high, imag_high)
    for at, part in enumerate(parts):
        ref[row:row + ROWS, col + at * LANES:col + (at + 1) * LANES] = part


def shifted(early, late, step):
    if step == 0:
        return early, late
    lane = lax.broadcasted_iota(jnp.int32, early.shape, 1)
    row = lax.broadcasted_iota(jnp.int32, early.shape, 0)
    count = early.shape[0]
    turned_early = pltpu.roll(early, (-step) % LANES, 1)
    turned_late = pltpu.roll(late, (-step) % LANES, 1)
    if step > 0:
        keep = lane < LANES - step
        beyond = jnp.where(row == count - 1, 0.0, pltpu.roll(turned_early, count - 1, 0))
        return jnp.where(keep, turned_early, turned_late), jnp.where(keep, turned_late, beyond)
    keep = lane >= -step
    before = jnp.where(row == 0, 0.0, pltpu.roll(turned_late, 1, 0))
    return jnp.where(keep, turned_early, before), jnp.where(keep, turned_late, turned_early)


def dot(left, right):
    return jnp.dot(left, right, preferred_element_type=jnp.float32)


QUADS = [[4 * q + place for place in range(4)] for q in range(8)]
LEAGUES = [[4 * q + 2 * pair + z for q in range(8) for z in range(2)] for pair in range(2)]
PLANES = [[2 * j + z for j in range(16)] for z in range(2)]


def twisted(array, col, twist_ref):
    real = array[:ROWS, col * LANES:(col + 1) * LANES]
    imag = array[ROWS:, col * LANES:(col + 1) * LANES]
    return real * twist_ref[0] - imag * twist_ref[1], real * twist_ref[1] + imag * twist_ref[0]


def untwisted(array, twist_ref):
    real, imag = array[:, :LANES], array[:, LANES:]
    return jnp.concatenate(
        [real * twist_ref[0] + imag * twist_ref[1], imag * twist_ref[0] - real * twist_ref[1]], axis=0)


def finish(table_ref, one, two):
    high, low = cut(jnp.concatenate([one, two], axis=1))
    return dot(table_ref[...], jnp.concatenate([high, low, high], axis=0))


def spectra_kernel(filters_ref, first_nat_ref, twist_ref, pair_ref, out_ref, kernel_buf):
    for q in range(BATCH):
        at = (pl.program_id(0) % (8 // BATCH)) * BATCH + q
        plus = filters_ref[0, 0, pl.ds(at, ROWS, stride=8), :]
        minus = filters_ref[1, 0, pl.ds(at, ROWS, stride=8), :]
        high, low = cut(jnp.concatenate([plus, minus], axis=1))
        section = dot(first_nat_ref[...], jnp.concatenate([high, high, low, low], axis=0))
        store_parts(kernel_buf, q * ROWS, 0, *twisted(section, 0, twist_ref))
        store_parts(kernel_buf, q * ROWS, 6 * LANES, *twisted(section, 1, twist_ref))
    out_ref[...] = dot(kernel_buf[...], pair_ref[...])


def lag_kernel(lag_ref, twist_ref, both_ref, last_nat_ref, out_ref):
    parts = lag_ref[...]
    unmixed = dot(jnp.concatenate([parts, parts[:, :2 * LANES]], axis=1), both_ref[...])
    for q in range(BATCH):
        at = (pl.program_id(0) % (8 // BATCH)) * BATCH + q
        rows = slice(q * ROWS, (q + 1) * ROWS)
        pair = finish(last_nat_ref, untwisted(unmixed[rows, :2 * LANES], twist_ref),
                      untwisted(unmixed[rows, 2 * LANES:], twist_ref))
        out_ref[0, 0, pl.ds(at, ROWS, stride=8), :] = pair[:, :LANES]
        out_ref[1, 0, pl.ds(at, ROWS, stride=8), :] = pair[:, LANES:]


def mixer_kernel(
    taps_ref, arrived_ref, spectra_ref, first_split_ref, twist_ref, forward_ref, inverse_ref, last_split_ref,
    back_ref, lag_ref,
    values_buf, slopes_buf, back_buf, mixed_buf, taps_buf, extra_buf, signal_buf, product_buf,
):
    blocks, width = arrived_ref.shape[0], arrived_ref.shape[1] // 2
    step = pl.program_id(0)

    @pl.when(step == 0)
    def _():
        for h in range(2):
            part = slice(h * LANES, (h + 1) * LANES)
            values_buf[h] = arrived_ref[:, :width, part].astype(jnp.float32).reshape(blocks * width, LANES)
            slopes_buf[h] = arrived_ref[:, width:, part].astype(jnp.float32).reshape(blocks * width, LANES)

    pooled = []
    for q in range(BATCH):
        c = step * BATCH + q
        early = values_buf[0, pl.ds(c, blocks, stride=width), :]
        late = values_buf[1, pl.ds(c, blocks, stride=width), :]
        sum_early, sum_late = None, None
        for k in range(TAPS):
            one, two = shifted(early, late, k - REACH)
            tap = taps_ref[k, c]
            sum_early = tap * one if k == 0 else sum_early + tap * one
            sum_late = tap * two if k == 0 else sum_late + tap * two
        short = jnp.concatenate([sum_early, sum_late], axis=0).astype(jnp.bfloat16)
        conv = short.astype(jnp.float32)
        slope = jnp.concatenate(
            [slopes_buf[h, pl.ds(c, blocks, stride=width), :] for h in range(2)], axis=0)
        sig = jax.nn.sigmoid(conv)
        pooled.append(jnp.sum(conv * sig, keepdims=True) / LENGTH)
        mean_grad = jnp.sum(slope, keepdims=True) / LENGTH
        extra_buf[q] = mean_grad * (sig * (1.0 + conv * (1.0 - sig)))
        both = jnp.concatenate([short, slope.astype(jnp.bfloat16)], axis=1)
        section = dot(first_split_ref[...], jnp.concatenate([both, both], axis=0))
        store_parts(signal_buf, q * ROWS, 0, *twisted(section, 0, twist_ref))
        store_parts(signal_buf, (BATCH + q) * ROWS, 0, *twisted(section, 1, twist_ref))

    spec = dot(signal_buf[...], forward_ref[...])
    for q in range(BATCH):
        rows = slice(q * ROWS, (q + 1) * ROWS)
        slope_rows = slice((BATCH + q) * ROWS, (BATCH + q + 1) * ROWS)
        short_re, short_im = spec[rows, :LANES], spec[rows, LANES:]
        slope_re, slope_im = spec[slope_rows, :LANES], spec[slope_rows, LANES:]
        filt_re, filt_im = spectra_ref[rows, :LANES], spectra_ref[rows, LANES:]
        store_parts(product_buf, (2 * q) * ROWS, 0,
                    short_re * filt_re - short_im * filt_im, short_re * filt_im + short_im * filt_re)
        store_parts(product_buf, (2 * q + 1) * ROWS, 0,
                    slope_re * filt_re + slope_im * filt_im, slope_im * filt_re - slope_re * filt_im)
        real_high, real_low = cut(slope_re * short_re + slope_im * short_im)
        imag_high, imag_low = cut(slope_im * short_re - slope_re * short_im)
        for at, part in enumerate((real_high, imag_high, real_low, imag_low)):
            lag_ref[rows, at * LANES:(at + 1) * LANES] = part

    unmixed = dot(product_buf[...], inverse_ref[...])
    for q in range(BATCH):
        c = step * BATCH + q
        rows = 2 * q * ROWS
        long_pair = finish(last_split_ref, untwisted(unmixed[rows:rows + ROWS], twist_ref),
                           untwisted(unmixed[rows + ROWS:rows + 2 * ROWS], twist_ref))
        mixed = long_pair[:, :LANES] + pooled[q]
        slope_back = (long_pair[:, LANES:] + extra_buf[q]).astype(jnp.bfloat16).astype(jnp.float32)
        early = values_buf[0, pl.ds(c, blocks, stride=width), :]
        late = values_buf[1, pl.ds(c, blocks, stride=width), :]
        sum_early, sum_late = None, None
        for k in range(TAPS):
            one, two = shifted(slope_back[:blocks], slope_back[blocks:], REACH - k)
            tap = taps_ref[k, c]
            sum_early = tap * one if k == 0 else sum_early + tap * one
            sum_late = tap * two if k == 0 else sum_late + tap * two
            taps_buf[k, pl.ds(c, 1), :] = jnp.sum(one * early + two * late, axis=0, keepdims=True)
        for h, part in enumerate((sum_early, sum_late)):
            back_buf[h, pl.ds(c, blocks, stride=width), :] = part
            mixed_buf[h, pl.ds(c, blocks, stride=width), :] = mixed[h * blocks:(h + 1) * blocks]

    @pl.when(step == pl.num_programs(0) - 1)
    def _():
        for q in range(blocks // 4):
            for place in range(4):
                rows = slice((4 * q + place) * width, (4 * q + place + 1) * width)
                for h in range(2):
                    part = back_buf[h, rows, :].astype(jnp.bfloat16)
                    lanes = slice((2 * place + h) * LANES, (2 * place + h + 1) * LANES)
                    back_ref[2 * q, :, lanes] = part
                    back_ref[2 * q + 1, :, lanes] = part
                    at = 8 + 2 * (place // 2) + h
                    back_ref[2 * q + place % 2, :, at * LANES:(at + 1) * LANES] = (
                        mixed_buf[h, rows, :].astype(jnp.bfloat16))
        lane = lax.broadcasted_iota(jnp.int32, (width, LANES), 1)
        packed = jnp.zeros((width, LANES), jnp.float32)
        for k in range(TAPS):
            rest = jnp.sum(taps_buf[k], axis=1, keepdims=True)
            for p in range(3):
                piece = rest.astype(jnp.bfloat16).astype(jnp.float32)
                packed = jnp.where(lane == 8 * p + k, piece, packed)
                rest = rest - piece
        for d in range(blocks // 2):
            back_ref[d, :, 12 * LANES:] = packed.astype(jnp.bfloat16)


def whole(shape):
    return pl.BlockSpec(shape, lambda *_: (0,) * len(shape))


def call(kernel, name, flops, nbytes, vmem=16, **kwargs):
    return pl.pallas_call(
        kernel, name=name,
        compiler_params=pltpu.CompilerParams(
            dimension_semantics=("arbitrary",), vmem_limit_bytes=vmem * 1024 * 1024),
        cost_estimate=pl.CostEstimate(flops=flops, bytes_accessed=nbytes, transcendentals=0), **kwargs)


def tables_of(names, blocks=LENGTH // 256):
    chosen = [jnp.asarray(tables(blocks)[name]) for name in names]
    return chosen, [whole(table.shape) for table in chosen]


PER_TILE = pl.BlockSpec((2, 1, ROWS * 8, LANES), lambda i: (0, i // (8 // BATCH), 0, 0))


def spectra_of(filters):
    width = filters.shape[1]
    tiles = width // 8
    view = filters.reshape(2, tiles, 8, ROWS, LANES).transpose(0, 1, 3, 2, 4).reshape(2, tiles, ROWS * 8, LANES)
    consts, specs = tables_of(("first_nat", "twist", "pair"))
    return call(
        spectra_kernel, "spectra", 3_000_000_000, 5_000_000, vmem=56,
        grid=(width // BATCH,), in_specs=[PER_TILE] + specs,
        out_specs=pl.BlockSpec((BATCH * ROWS, 2 * LANES), lambda i: (i, 0)),
        out_shape=jax.ShapeDtypeStruct((width * ROWS, 2 * LANES), jnp.float32),
        scratch_shapes=[pltpu.VMEM((BATCH * ROWS, 12 * LANES), jnp.bfloat16)],
    )(view, *consts)


def filter_grads(lag):
    width = lag.shape[0] // ROWS
    tiles = width // 8
    consts, specs = tables_of(("twist", "both", "last_nat"))
    out = call(
        lag_kernel, "filter_grads", 3_000_000_000, 5_000_000,
        grid=(width // BATCH,),
        in_specs=[pl.BlockSpec((BATCH * ROWS, 4 * LANES), lambda i: (i, 0))] + specs,
        out_specs=PER_TILE,
        out_shape=jax.ShapeDtypeStruct((2, tiles, ROWS * 8, LANES), jnp.float32),
    )(lag, *consts)
    return out.reshape(2, tiles, ROWS, 8, LANES).transpose(0, 1, 3, 2, 4).reshape(2, width, LENGTH)


def mixer(own_taps, arrived, spectra):
    blocks, width, span = arrived.shape[0], arrived.shape[1] // 2, arrived.shape[2]
    consts, specs = tables_of(("first_split", "twist", "forward", "inverse", "last_split"))
    back_shape = (blocks // 2, width, 6 * span + LANES)
    rows = (2, blocks * width, LANES)
    return call(
        mixer_kernel, "mixer", 3_000_000_000, 8_000_000, vmem=56,
        grid=(width // BATCH,),
        in_specs=[pl.BlockSpec(memory_space=pltpu.SMEM), whole(arrived.shape),
                  pl.BlockSpec((BATCH * ROWS, 2 * LANES), lambda i: (i, 0))] + specs,
        out_specs=[whole(back_shape), pl.BlockSpec((BATCH * ROWS, 4 * LANES), lambda i: (i, 0))],
        out_shape=[
            jax.ShapeDtypeStruct(back_shape, jnp.bfloat16),
            jax.ShapeDtypeStruct((width * ROWS, 4 * LANES), jnp.bfloat16),
        ],
        scratch_shapes=[
            pltpu.VMEM(rows, jnp.float32),
            pltpu.VMEM(rows, jnp.float32),
            pltpu.VMEM(rows, jnp.float32),
            pltpu.VMEM(rows, jnp.float32),
            pltpu.VMEM((TAPS, width, LANES), jnp.float32),
            pltpu.VMEM((BATCH, ROWS, LANES), jnp.float32),
            pltpu.VMEM((2 * BATCH * ROWS, 6 * LANES), jnp.bfloat16),
            pltpu.VMEM((2 * BATCH * ROWS, 6 * LANES), jnp.bfloat16),
        ],
    )(own_taps, arrived, spectra, *consts)


STREAMS = 4


def send_kernel(rows_ref, *refs):
    weight_refs, (gate_ref, grad_ref, out_ref, total_ref) = refs[:STREAMS], refs[STREAMS:]
    blocks, width, span = out_ref.shape[0], out_ref.shape[1] // 2, out_ref.shape[2]
    step, steps = pl.program_id(0), pl.num_programs(0)
    count = blocks * gate_ref.shape[1] // total_ref.shape[1]
    sig = jax.nn.sigmoid(gate_ref[...].astype(jnp.float32))
    slopes = (grad_ref[...].astype(jnp.float32) * sig).T.astype(jnp.bfloat16)
    out_ref[pl.ds(step * count, count), width:, :] = slopes.reshape(count, width, span)
    part = weight_refs[0].shape[0]
    term = dot(rows_ref[:, :part], weight_refs[0][...])
    for j in range(1, STREAMS):
        term = term + dot(rows_ref[:, j * part:(j + 1) * part], weight_refs[j][...])

    @pl.when(step == 0)
    def _():
        total_ref[...] = term

    @pl.when((step > 0) & (step < steps - 1))
    def _():
        total_ref[...] += term

    @pl.when(step == steps - 1)
    def _():
        total = total_ref[...] + term
        out_ref[:, :width, :] = total.T.astype(jnp.bfloat16).reshape(blocks, width, span)


def sends(layer_in, w_value, gate, grads, count, steps=4):
    span, depth = layer_in.shape
    channels = w_value.shape[1]
    width = channels // count
    block = pl.BlockSpec((span, channels // steps), lambda i: (0, i))
    streams = [pl.BlockSpec((depth // (steps * STREAMS), channels), functools.partial(lambda j, i: (STREAMS * i + j, 0), j))
               for j in range(STREAMS)]
    return call(
        send_kernel, "sends", 2 * span * depth * channels, 12_500_000, vmem=56, grid=(steps,),
        in_specs=[pl.BlockSpec((span, depth // steps), lambda i: (0, i))] + streams + [block, block],
        out_specs=whole((count, 2 * width, span)),
        out_shape=jax.ShapeDtypeStruct((count, 2 * width, span), jnp.bfloat16),
        scratch_shapes=[pltpu.VMEM((span, channels), jnp.float32)],
    )(layer_in, *[w_value] * STREAMS, gate, grads)


def quarter_kernel(place_ref, rows_ref, others_ref, same_ref, cross_ref, other_ref):
    z = place_ref[0] % 2
    for y in range(4):
        to = slice(y * LANES, (y + 1) * LANES)
        own = pl.ds(pl.multiple_of((2 * y + z) * LANES, LANES), LANES)
        same_ref[:, to] = rows_ref[:, own]
        other_ref[:, to] = others_ref[:, own]
        cross_ref[:, to] = rows_ref[:, pl.ds(pl.multiple_of((2 * y + 1 - z) * LANES, LANES), LANES)]


def quarters_of(place, layer_in):
    span, depth = layer_in.shape
    quarter = jax.ShapeDtypeStruct((span, depth // 4), jnp.bfloat16)
    return call(
        quarter_kernel, "quarters", 0, 5_000_000,
        grid_spec=pltpu.PrefetchScalarGridSpec(
            num_scalar_prefetch=1, grid=(2,),
            in_specs=[pl.BlockSpec((span, depth // 4), lambda i, place: (0, 2 * (place[1] % 2) + i)),
                      pl.BlockSpec((span, depth // 4), lambda i, place: (0, 2 - 2 * (place[1] % 2) + i))],
            out_specs=[pl.BlockSpec((span, 4 * LANES), lambda i, place: (0, i))] * 3),
        out_shape=[quarter] * 3,
    )(place, layer_in, layer_in)


def share_kernel(place_ref, back_ref, *refs):
    mine, other, out_ref = refs[:4], refs[4:8], refs[8]
    core = place_ref[1] % 2
    span = mine[0].shape[0]
    for half, rows in ((core, mine), (1 - core, other)):
        for two in range(4):
            lanes = slice(two * 256, (two + 1) * 256)
            product = None
            for j in range(4):
                at = pl.multiple_of((place_ref[0] ^ j) * span, span)
                term = dot(back_ref[:, pl.ds(at, span)], rows[j][:, lanes])
                product = term if product is None else product + term
            product = product.astype(jnp.bfloat16)
            out_ref[half * 8 + 2 * two] = product[:, :LANES]
            out_ref[half * 8 + 2 * two + 1] = product[:, LANES:]


def shares(place, back, mine, other):
    span, depth = mine[0].shape
    rows = back.shape[0]
    return call(
        share_kernel, "shares", 16 * rows * span * depth, 7_000_000, vmem=24, grid=(1,),
        in_specs=[pl.BlockSpec(memory_space=pltpu.SMEM), pl.BlockSpec((rows, 4 * span), lambda i: (0, 0))]
        + [whole(part.shape) for part in mine + other],
        out_specs=whole((16, rows, LANES)),
        out_shape=jax.ShapeDtypeStruct((16, rows, LANES), jnp.bfloat16),
    )(place, back, *mine, *other)


def merge(pair, mine, mate):
    first, second = jnp.where(pair == 0, mine, mate), jnp.where(pair == 0, mate, mine)
    half = mine.shape[0] // 2
    return jnp.concatenate([first[:half], second[:half], first[half:], second[half:]], axis=0)


def weight_kernel(place_ref, shares_ref, taps_ref, mate_ref, weight_ref, tap_sums_ref):
    for x in range(4):
        rows, lanes = slice(x * LANES, (x + 1) * LANES), slice(x * 2 * LANES, (x + 1) * 2 * LANES)
        totals = []
        for pair in range(2):
            total = shares_ref[pair, rows, :].astype(jnp.float32)
            for j in range(pair + 2, shares_ref.shape[0], 2):
                total = total + shares_ref[j, rows, :].astype(jnp.float32)
            totals.append(total)
        weight_ref[:, lanes] = merge(0, *totals).T
        packed = merge(place_ref[0] // 2, taps_ref[rows, :].astype(jnp.float32), mate_ref[rows, :].astype(jnp.float32)).T
        tap_sums_ref[:, lanes] = (packed[16:24] + packed[8:16] + packed[0:8])[:TAPS]


def close_weight(place, parts, back, mate):
    count, rows, span = parts.shape
    channels = 2 * rows
    return call(
        weight_kernel, "close_weight", 2_000_000, 3_000_000, grid=(1,),
        in_specs=[pl.BlockSpec(memory_space=pltpu.SMEM), whole(parts.shape),
                  pl.BlockSpec((rows, LANES), lambda i: (0, 12)), pl.BlockSpec((rows, LANES), lambda i: (0, 4))],
        out_specs=[whole((span, channels)), whole((TAPS, channels))],
        out_shape=[jax.ShapeDtypeStruct((span, channels), jnp.float32),
                   jax.ShapeDtypeStruct((TAPS, channels), jnp.float32)],
    )(place, parts, back, mate)


def input_kernel(place_ref, back_ref, mate_ref, weight_ref, send_ref, keep_ref, own_buf):
    @pl.when(pl.program_id(0) == 0)
    def _():
        pair = place_ref[0] // 2
        for at in range(8):
            rows = slice(at * 64, (at + 1) * 64)
            own_buf[pl.ds(pl.multiple_of(at * LANES + pair * 64, 64), 64), :] = back_ref[rows, :]
            own_buf[pl.ds(pl.multiple_of(at * LANES + (1 - pair) * 64, 64), 64), :] = mate_ref[rows, :]

    term = dot(weight_ref[...], own_buf[...])

    @pl.when(pl.program_id(0) < 2)
    def _():
        send_ref[0] = term.astype(jnp.bfloat16)

    @pl.when(pl.program_id(0) >= 2)
    def _():
        keep_ref[0] = term


def input_terms(place, back, mate, w_value):
    depth, channels = w_value.shape
    rows, span = depth // 4, 256
    return call(
        input_kernel, "input_terms", 2 * span * depth * channels, 12_000_000, vmem=24,
        grid_spec=pltpu.PrefetchScalarGridSpec(
            num_scalar_prefetch=1, grid=(4,),
            in_specs=[pl.BlockSpec((channels // 2, span), lambda i, place: (0, place[0])),
                      pl.BlockSpec((channels // 2, span), lambda i, place: (0, 0)),
                      pl.BlockSpec((rows, channels), lambda i, place: (place[1] ^ ((2 * i + 1 - i // 2) % 4), 0))],
            out_specs=[pl.BlockSpec((1, rows, span), lambda i, place: (jnp.minimum(i, 1), 0, 0)),
                       pl.BlockSpec((1, rows, span), lambda i, place: (jnp.maximum(i - 2, 0), 0, 0))],
            scratch_shapes=[pltpu.VMEM((channels, span), jnp.bfloat16)]),
        out_shape=[jax.ShapeDtypeStruct((2, rows, span), jnp.bfloat16),
                   jax.ShapeDtypeStruct((2, rows, span), jnp.float32)],
    )(place, back, mate, w_value)


def close_kernel(keep_ref, core_ref, chip_ref, out_ref):
    total = keep_ref[0] + core_ref[0].astype(jnp.float32) + chip_ref[...].astype(jnp.float32)
    out_ref[...] = total.T.astype(jnp.bfloat16)


def close_input(keep, core, chip):
    rows, span = chip.shape
    first = pl.BlockSpec((1, 512, span), lambda i: (0, i, 0))
    return call(
        close_kernel, "close_input", 1_000_000, 3_000_000, grid=(rows // 512,),
        in_specs=[first, first, pl.BlockSpec((512, span), lambda i: (i, 0))],
        out_specs=pl.BlockSpec((span, 512), lambda i: (0, i)),
        out_shape=jax.ShapeDtypeStruct((span, rows), jnp.bfloat16))(keep, core, chip)


def gate_kernel(place_ref, mixed_ref, mate_ref, gate_ref, grad_ref, out_ref):
    mixed = merge(place_ref[0] // 2, mixed_ref[...].astype(jnp.float32), mate_ref[...].astype(jnp.float32)).T
    sig = jax.nn.sigmoid(gate_ref[...].astype(jnp.float32))
    out_ref[...] = (grad_ref[...].astype(jnp.float32) * mixed * sig * (1.0 - sig)).astype(jnp.bfloat16)


def gate_grad(place, back, mate, gate, grads):
    span, channels = gate.shape
    block = pl.BlockSpec((span, channels // 4), lambda i, place: (0, i))
    return call(
        gate_kernel, "gate_grad", 2_000_000, 2_500_000,
        grid_spec=pltpu.PrefetchScalarGridSpec(
            num_scalar_prefetch=1, grid=(4,),
            in_specs=[pl.BlockSpec((LANES, span), lambda i, place: (i, 4 + place[0] // 2)),
                      pl.BlockSpec((LANES, span), lambda i, place: (i, 1)), block, block],
            out_specs=block),
        out_shape=jax.ShapeDtypeStruct(gate.shape, jnp.bfloat16))(place, back, mate, gate, grads)


def local(layer_in, w_value, short_taps, long_filters, gate_proj, grad_out):
    seq_count = lax.axis_size("seq")
    seq_at, tp_at = lax.axis_index("seq"), lax.axis_index("tp")
    span, depth = layer_in.shape
    channels = w_value.shape[1]
    width = channels // seq_count
    quad_at = seq_at % 4
    place = jnp.stack([quad_at, tp_at]).astype(jnp.int32)
    cores, chips = [(0, 1), (1, 0), (2, 3), (3, 2)], [(0, 2), (2, 0), (1, 3), (3, 1)]

    def exchange(value, index_groups=None):
        return lax.all_to_all(
            value, "seq", split_axis=0, concat_axis=0, axis_index_groups=index_groups, tiled=True)

    def mates(value, step):
        return lax.ppermute(value, "seq", [(s, s ^ step) for s in range(seq_count)])

    outgoing = sends(layer_in, w_value, gate_proj, grad_out, seq_count)
    rows_in, outgoing = lax.optimization_barrier((layer_in, outgoing))
    arrived = exchange(outgoing)
    same, cross, other = quarters_of(place, rows_in)
    mine = [same, mates(cross, 1), mates(same, 2), mates(cross, 3)]
    other = [other] + [lax.ppermute(part, "tp", cores) for part in mine[1:]]
    spectra = spectra_of(long_filters)

    own_taps = lax.dynamic_slice_in_dim(short_taps, seq_at * width, width, 1)
    back, lag = mixer(own_taps, arrived, spectra)
    back, mine = lax.optimization_barrier((back, mine))
    back = exchange(back, LEAGUES).reshape(channels // 2, back.shape[2])
    grad_filters = filter_grads(lag)
    back, grad_filters, other = lax.optimization_barrier((back, grad_filters, other))
    mate = mates(jnp.concatenate([
        lax.dynamic_slice_in_dim(back, (quad_at ^ 2) * span, span, 1),
        lax.dynamic_slice_in_dim(back, 4 * span + (1 - quad_at // 2) * span, span, 1),
        back[:, 6 * span:]], axis=1), 2)

    parts = exchange(shares(place, back, mine, other), PLANES)
    send, keep = input_terms(place, back, mate, w_value)
    core = lax.ppermute(send, "tp", cores)
    chip = lax.ppermute((keep[1] + core[1].astype(jnp.float32)).astype(jnp.bfloat16), "tp", chips)
    grad_input = close_input(keep, core, chip)
    grad_gate = gate_grad(place, back, mate, gate_proj, grad_out)
    grad_weight, grad_taps = close_weight(place, parts, back, mate)
    return (grad_input, grad_weight, grad_taps, grad_filters, grad_gate)


def solution(mesh):
    in_specs = (
        P("seq", None),
        P(None, "tp"),
        P(None, "tp"),
        P(None, ("tp", "seq"), None),
        P("seq", "tp"),
        P("seq", "tp"),
    )
    out_specs = (
        P("seq", "tp"),
        P("seq", "tp"),
        P(None, "tp"),
        P(None, ("tp", "seq"), None),
        P("seq", "tp"),
    )
    return jax.shard_map(local, mesh=mesh, in_specs=in_specs, out_specs=out_specs, check_vma=False)
```

```python
import functools
import math

import jax
import jax.numpy as jnp
import ml_dtypes
import numpy as np
from jax import lax
from jax.experimental import pallas as pl
from jax.experimental.pallas import tpu as pltpu
from jax.sharding import PartitionSpec as P

LANES = 128
ROWS = 64
LENGTH = ROWS * LANES
TAPS = 7
REACH = TAPS // 2
BATCH = 4
GROUP, GROUPS = 2, 4


def halves(table):
    high = table.astype(ml_dtypes.bfloat16)
    low = (table - high.astype(np.float64)).astype(ml_dtypes.bfloat16)
    return high, low


@functools.lru_cache(maxsize=None)
def tables(blocks):
    half = np.arange(ROWS) + 0.5
    natural = np.arange(ROWS)
    split = (2 * np.arange(blocks)[None, :] + np.arange(2)[:, None]).reshape(-1)

    def first(order):
        turn = 2.0 * math.pi / LANES * np.outer(half, order)
        return halves(np.concatenate([np.cos(turn), -np.sin(turn)], axis=0))

    def last(order):
        turn = 2.0 * math.pi / LANES * np.outer(order, half)
        return halves(np.concatenate([np.cos(turn), -np.sin(turn)], axis=1) / LENGTH)

    split_high, split_low = first(split)
    nat_high, nat_low = first(natural)
    first_split = np.concatenate([split_high, split_low], axis=1)
    first_nat = np.concatenate([nat_high, nat_low, nat_high, nat_low], axis=1)
    inv_split_high, inv_split_low = last(split)
    inv_nat_high, inv_nat_low = last(natural)
    last_split = np.concatenate([inv_split_high, inv_split_high, inv_split_low], axis=1)
    last_nat = np.concatenate([inv_nat_high, inv_nat_high, inv_nat_low], axis=1)
    twist = 2.0 * math.pi / (2 * LENGTH) * np.outer(half, np.arange(LANES))
    twist = np.stack([np.cos(twist), -np.sin(twist)]).astype(np.float32)
    grid = 2.0 * math.pi / LANES * np.outer(np.arange(LANES), np.arange(LANES))
    cos, sin = np.cos(grid), np.sin(grid)

    def stacked(table):
        high, low = halves(table)
        return np.concatenate([high, high, low], axis=0)

    forward = np.block([[cos, -sin], [sin, cos]])
    mirror = np.block([[cos, sin], [sin, -cos]])
    inverse = np.block([[cos, sin], [-sin, cos]])
    pair = np.concatenate([stacked(forward), stacked(mirror)], axis=0)
    both = np.concatenate([stacked(inverse), stacked(np.block([[cos, sin], [sin, -cos]]))], axis=1)
    return {
        "first_split": first_split, "first_nat": first_nat, "twist": twist, "forward": stacked(forward), "pair": pair,
        "inverse": stacked(inverse), "both": both, "last_split": last_split, "last_nat": last_nat,
    }


def cut(value):
    high = value.astype(jnp.bfloat16)
    low = (value - high.astype(jnp.float32)).astype(jnp.bfloat16)
    return high, low


def store_parts(ref, row, col, real, imag):
    real_high, real_low = cut(real)
    imag_high, imag_low = cut(imag)
    parts = (real_high, imag_high, real_low, imag_low, real_high, imag_high)
    for at, part in enumerate(parts):
        ref[row:row + ROWS, col + at * LANES:col + (at + 1) * LANES] = part


def shifted(early, late, step):
    if step == 0:
        return early, late
    lane = lax.broadcasted_iota(jnp.int32, early.shape, 1)
    row = lax.broadcasted_iota(jnp.int32, early.shape, 0)
    count = early.shape[0]
    turned_early = pltpu.roll(early, (-step) % LANES, 1)
    turned_late = pltpu.roll(late, (-step) % LANES, 1)
    if step > 0:
        keep = lane < LANES - step
        beyond = jnp.where(row == count - 1, 0.0, pltpu.roll(turned_early, count - 1, 0))
        return jnp.where(keep, turned_early, turned_late), jnp.where(keep, turned_late, beyond)
    keep = lane >= -step
    before = jnp.where(row == 0, 0.0, pltpu.roll(turned_late, 1, 0))
    return jnp.where(keep, turned_early, before), jnp.where(keep, turned_late, turned_early)


def dot(left, right):
    return jnp.dot(left, right, preferred_element_type=jnp.float32)


Y_OF = ((1, 2), (0, 3))
QUADS = [[(x * 4 + Y_OF[odd][pair]) * 2 + z for pair in range(2) for z in range(2)] for x in range(4) for odd in range(2)]
LEAGUES = [[quad[2 * pair + z] for quad in QUADS for z in range(2)] for pair in range(2)]
PLANES = [[2 * j + z for j in range(16)] for z in range(2)]
MATE = 6


def twisted(array, col, twist_ref):
    real = array[:ROWS, col * LANES:(col + 1) * LANES]
    imag = array[ROWS:, col * LANES:(col + 1) * LANES]
    return real * twist_ref[0] - imag * twist_ref[1], real * twist_ref[1] + imag * twist_ref[0]


def untwisted(array, twist_ref):
    real, imag = array[:, :LANES], array[:, LANES:]
    return jnp.concatenate(
        [real * twist_ref[0] + imag * twist_ref[1], imag * twist_ref[0] - real * twist_ref[1]], axis=0)


def finish(table_ref, one, two):
    high, low = cut(jnp.concatenate([one, two], axis=1))
    return dot(table_ref[...], jnp.concatenate([high, low, high], axis=0))


def spectra_kernel(filters_ref, first_nat_ref, twist_ref, pair_ref, out_ref, kernel_buf):
    for q in range(BATCH):
        at = (pl.program_id(0) % (8 // BATCH)) * BATCH + q
        plus = filters_ref[0, 0, pl.ds(at, ROWS, stride=8), :]
        minus = filters_ref[1, 0, pl.ds(at, ROWS, stride=8), :]
        high, low = cut(jnp.concatenate([plus, minus], axis=1))
        section = dot(first_nat_ref[...], jnp.concatenate([high, high, low, low], axis=0))
        store_parts(kernel_buf, q * ROWS, 0, *twisted(section, 0, twist_ref))
        store_parts(kernel_buf, q * ROWS, 6 * LANES, *twisted(section, 1, twist_ref))
    out_ref[...] = dot(kernel_buf[...], pair_ref[...])


def lag_kernel(lag_ref, twist_ref, both_ref, last_nat_ref, out_ref):
    parts = lag_ref[...]
    unmixed = dot(jnp.concatenate([parts, parts[:, :2 * LANES]], axis=1), both_ref[...])
    for q in range(BATCH):
        at = (pl.program_id(0) % (8 // BATCH)) * BATCH + q
        rows = slice(q * ROWS, (q + 1) * ROWS)
        pair = finish(last_nat_ref, untwisted(unmixed[rows, :2 * LANES], twist_ref),
                      untwisted(unmixed[rows, 2 * LANES:], twist_ref))
        out_ref[0, 0, pl.ds(at, ROWS, stride=8), :] = pair[:, :LANES]
        out_ref[1, 0, pl.ds(at, ROWS, stride=8), :] = pair[:, LANES:]


def mixer_kernel(
    taps_ref, arrived_ref, spectra_ref, first_split_ref, twist_ref, forward_ref, inverse_ref, last_split_ref,
    back_ref, lag_ref,
    values_buf, slopes_buf, back_buf, mixed_buf, taps_buf, extra_buf, signal_buf, product_buf,
):
    blocks, width = arrived_ref.shape[0], arrived_ref.shape[1] // 2
    step = pl.program_id(0)

    @pl.when(step == 0)
    def _():
        for h in range(2):
            part = slice(h * LANES, (h + 1) * LANES)
            values_buf[h] = arrived_ref[:, :width, part].astype(jnp.float32).reshape(blocks * width, LANES)
            slopes_buf[h] = arrived_ref[:, width:, part].astype(jnp.float32).reshape(blocks * width, LANES)

    pooled = {}

    def start(g):
        for q in range(g * GROUP, (g + 1) * GROUP):
            c = step * GROUP * GROUPS + q
            early = values_buf[0, pl.ds(c, blocks, stride=width), :]
            late = values_buf[1, pl.ds(c, blocks, stride=width), :]
            sum_early, sum_late = None, None
            for k in range(TAPS):
                one, two = shifted(early, late, k - REACH)
                tap = taps_ref[k, c]
                sum_early = tap * one if k == 0 else sum_early + tap * one
                sum_late = tap * two if k == 0 else sum_late + tap * two
            short = jnp.concatenate([sum_early, sum_late], axis=0).astype(jnp.bfloat16)
            conv = short.astype(jnp.float32)
            slope = jnp.concatenate(
                [slopes_buf[h, pl.ds(c, blocks, stride=width), :] for h in range(2)], axis=0)
            sig = jax.nn.sigmoid(conv)
            pooled[q] = jnp.sum(conv * sig, keepdims=True) / LENGTH
            mean_grad = jnp.sum(slope, keepdims=True) / LENGTH
            extra_buf[q] = mean_grad * (sig * (1.0 + conv * (1.0 - sig)))
            both = jnp.concatenate([short, slope.astype(jnp.bfloat16)], axis=1)
            section = dot(first_split_ref[...], jnp.concatenate([both, both], axis=0))
            store_parts(signal_buf, 2 * q * ROWS, 0, *twisted(section, 0, twist_ref))
            store_parts(signal_buf, (2 * q + 1) * ROWS, 0, *twisted(section, 1, twist_ref))

    def multiply(g):
        base = 2 * g * GROUP * ROWS
        spec = dot(signal_buf[base:base + 2 * GROUP * ROWS], forward_ref[...])
        for q in range(GROUP):
            short, slope = spec[2 * q * ROWS:(2 * q + 1) * ROWS], spec[(2 * q + 1) * ROWS:(2 * q + 2) * ROWS]
            rows = slice((g * GROUP + q) * ROWS, (g * GROUP + q + 1) * ROWS)
            short_re, short_im = short[:, :LANES], short[:, LANES:]
            slope_re, slope_im = slope[:, :LANES], slope[:, LANES:]
            filt_re, filt_im = spectra_ref[rows, :LANES], spectra_ref[rows, LANES:]
            store_parts(product_buf, base + 2 * q * ROWS, 0,
                        short_re * filt_re - short_im * filt_im, short_re * filt_im + short_im * filt_re)
            store_parts(product_buf, base + (2 * q + 1) * ROWS, 0,
                        slope_re * filt_re + slope_im * filt_im, slope_im * filt_re - slope_re * filt_im)
            real_high, real_low = cut(slope_re * short_re + slope_im * short_im)
            imag_high, imag_low = cut(slope_im * short_re - slope_re * short_im)
            for at, part in enumerate((real_high, imag_high, real_low, imag_low)):
                lag_ref[rows, at * LANES:(at + 1) * LANES] = part

    def end(g):
        base = 2 * g * GROUP * ROWS
        unmixed = dot(product_buf[base:base + 2 * GROUP * ROWS], inverse_ref[...])
        for q in range(GROUP):
            c = step * GROUP * GROUPS + g * GROUP + q
            rows = 2 * q * ROWS
            long_pair = finish(last_split_ref, untwisted(unmixed[rows:rows + ROWS], twist_ref),
                               untwisted(unmixed[rows + ROWS:rows + 2 * ROWS], twist_ref))
            mixed = long_pair[:, :LANES] + pooled[g * GROUP + q]
            slope_back = long_pair[:, LANES:] + extra_buf[g * GROUP + q]
            slope_back = slope_back.astype(jnp.bfloat16).astype(jnp.float32)
            early = values_buf[0, pl.ds(c, blocks, stride=width), :]
            late = values_buf[1, pl.ds(c, blocks, stride=width), :]
            sum_early, sum_late = None, None
            for k in range(TAPS):
                one, two = shifted(slope_back[:blocks], slope_back[blocks:], REACH - k)
                tap = taps_ref[k, c]
                sum_early = tap * one if k == 0 else sum_early + tap * one
                sum_late = tap * two if k == 0 else sum_late + tap * two
                taps_buf[k, pl.ds(c, 1), :] = jnp.sum(one * early + two * late, axis=0, keepdims=True)
            for h, part in enumerate((sum_early, sum_late)):
                back_buf[h, pl.ds(c, blocks, stride=width), :] = part
                mixed_buf[h, pl.ds(c, blocks, stride=width), :] = mixed[h * blocks:(h + 1) * blocks]

    for turn in range(GROUPS + 2):
        if turn >= 2:
            end(turn - 2)
        if 1 <= turn <= GROUPS:
            multiply(turn - 1)
        if turn < GROUPS:
            start(turn)

    @pl.when(step == pl.num_programs(0) - 1)
    def _():
        for q, quad in enumerate(QUADS):
            for place, s in enumerate(quad):
                rows = slice(s * width, (s + 1) * width)
                for h in range(2):
                    part = back_buf[h, rows, :].astype(jnp.bfloat16)
                    lanes = slice((2 * place + h) * LANES, (2 * place + h + 1) * LANES)
                    back_ref[2 * q, :, lanes] = part
                    back_ref[2 * q + 1, :, lanes] = part
                    at = 8 + 2 * (place // 2) + h
                    back_ref[2 * q + place % 2, :, at * LANES:(at + 1) * LANES] = (
                        mixed_buf[h, rows, :].astype(jnp.bfloat16))
        lane = lax.broadcasted_iota(jnp.int32, (width, LANES), 1)
        packed = jnp.zeros((width, LANES), jnp.float32)
        for k in range(TAPS):
            rest = jnp.sum(taps_buf[k], axis=1, keepdims=True)
            for p in range(3):
                piece = rest.astype(jnp.bfloat16).astype(jnp.float32)
                packed = jnp.where(lane == 8 * p + k, piece, packed)
                rest = rest - piece
        for d in range(blocks // 2):
            back_ref[d, :, 12 * LANES:] = packed.astype(jnp.bfloat16)


def whole(shape):
    return pl.BlockSpec(shape, lambda *_: (0,) * len(shape))


def call(kernel, name, flops, nbytes, vmem=16, **kwargs):
    return pl.pallas_call(
        kernel, name=name,
        compiler_params=pltpu.CompilerParams(vmem_limit_bytes=vmem * 1024 * 1024),
        cost_estimate=pl.CostEstimate(flops=flops, bytes_accessed=nbytes, transcendentals=0), **kwargs)


def tables_of(names, blocks=LENGTH // 256):
    chosen = [jnp.asarray(tables(blocks)[name]) for name in names]
    return chosen, [whole(table.shape) for table in chosen]


PER_TILE = pl.BlockSpec((2, 1, ROWS * 8, LANES), lambda i: (0, i // (8 // BATCH), 0, 0))


def spectra_of(filters):
    width = filters.shape[1]
    tiles = width // 8
    view = filters.reshape(2, tiles, 8, ROWS, LANES).transpose(0, 1, 3, 2, 4).reshape(2, tiles, ROWS * 8, LANES)
    consts, specs = tables_of(("first_nat", "twist", "pair"))
    return call(
        spectra_kernel, "spectra", 3_000_000_000, 5_000_000, vmem=56,
        grid=(width // BATCH,), in_specs=[PER_TILE] + specs,
        out_specs=pl.BlockSpec((BATCH * ROWS, 2 * LANES), lambda i: (i, 0)),
        out_shape=jax.ShapeDtypeStruct((width * ROWS, 2 * LANES), jnp.float32),
        scratch_shapes=[pltpu.VMEM((BATCH * ROWS, 12 * LANES), jnp.bfloat16)],
    )(view, *consts)


def filter_grads(lag):
    width = lag.shape[0] // ROWS
    tiles = width // 8
    consts, specs = tables_of(("twist", "both", "last_nat"))
    out = call(
        lag_kernel, "filter_grads", 3_000_000_000, 5_000_000,
        grid=(width // BATCH,),
        in_specs=[pl.BlockSpec((BATCH * ROWS, 4 * LANES), lambda i: (i, 0))] + specs,
        out_specs=PER_TILE,
        out_shape=jax.ShapeDtypeStruct((2, tiles, ROWS * 8, LANES), jnp.float32),
    )(lag, *consts)
    return out.reshape(2, tiles, ROWS, 8, LANES).transpose(0, 1, 3, 2, 4).reshape(2, width, LENGTH)


def mixer(own_taps, arrived, spectra):
    blocks, width, span = arrived.shape[0], arrived.shape[1] // 2, arrived.shape[2]
    consts, specs = tables_of(("first_split", "twist", "forward", "inverse", "last_split"))
    back_shape = (blocks // 2, width, 6 * span + LANES)
    rows, batch = (2, blocks * width, LANES), GROUP * GROUPS
    return call(
        mixer_kernel, "mixer", 3_000_000_000, 8_000_000, vmem=56,
        grid=(width // batch,),
        in_specs=[pl.BlockSpec(memory_space=pltpu.SMEM), whole(arrived.shape),
                  pl.BlockSpec((batch * ROWS, 2 * LANES), lambda i: (i, 0))] + specs,
        out_specs=[whole(back_shape), pl.BlockSpec((batch * ROWS, 4 * LANES), lambda i: (i, 0))],
        out_shape=[
            jax.ShapeDtypeStruct(back_shape, jnp.bfloat16),
            jax.ShapeDtypeStruct((width * ROWS, 4 * LANES), jnp.bfloat16),
        ],
        scratch_shapes=[
            pltpu.VMEM(rows, jnp.float32),
            pltpu.VMEM(rows, jnp.float32),
            pltpu.VMEM(rows, jnp.float32),
            pltpu.VMEM(rows, jnp.float32),
            pltpu.VMEM((TAPS, width, LANES), jnp.float32),
            pltpu.VMEM((batch, ROWS, LANES), jnp.float32),
            pltpu.VMEM((2 * batch * ROWS, 6 * LANES), jnp.bfloat16),
            pltpu.VMEM((2 * batch * ROWS, 6 * LANES), jnp.bfloat16),
        ],
    )(own_taps, arrived, spectra, *consts)


STREAMS = 4


def send_kernel(rows_ref, *refs):
    weight_refs, (gate_ref, grad_ref, out_ref, total_ref) = refs[:STREAMS], refs[STREAMS:]
    blocks, width, span = out_ref.shape[0], out_ref.shape[1] // 2, out_ref.shape[2]
    step, steps = pl.program_id(0), pl.num_programs(0)
    count = blocks * gate_ref.shape[1] // total_ref.shape[1]
    sig = jax.nn.sigmoid(gate_ref[...].astype(jnp.float32))
    slopes = (grad_ref[...].astype(jnp.float32) * sig).T.astype(jnp.bfloat16)
    out_ref[pl.ds(step * count, count), width:, :] = slopes.reshape(count, width, span)
    part = weight_refs[0].shape[0]
    term = dot(rows_ref[:, :part], weight_refs[0][...])
    for j in range(1, STREAMS):
        term = term + dot(rows_ref[:, j * part:(j + 1) * part], weight_refs[j][...])

    @pl.when(step == 0)
    def _():
        total_ref[...] = term

    @pl.when((step > 0) & (step < steps - 1))
    def _():
        total_ref[...] += term

    @pl.when(step == steps - 1)
    def _():
        total = total_ref[...] + term
        out_ref[:, :width, :] = total.T.astype(jnp.bfloat16).reshape(blocks, width, span)


def sends(layer_in, w_value, gate, grads, count, steps=4):
    span, depth = layer_in.shape
    channels = w_value.shape[1]
    width = channels // count
    block = pl.BlockSpec((span, channels // steps), lambda i: (0, i))
    streams = [pl.BlockSpec((depth // (steps * STREAMS), channels), functools.partial(lambda j, i: (STREAMS * i + j, 0), j))
               for j in range(STREAMS)]
    return call(
        send_kernel, "sends", 2 * span * depth * channels, 12_500_000, vmem=56, grid=(steps,),
        in_specs=[pl.BlockSpec((span, depth // steps), lambda i: (0, i))] + streams + [block, block],
        out_specs=whole((count, 2 * width, span)),
        out_shape=jax.ShapeDtypeStruct((count, 2 * width, span), jnp.bfloat16),
        scratch_shapes=[pltpu.VMEM((span, channels), jnp.float32)],
    )(layer_in, *[w_value] * STREAMS, gate, grads)


def quarter_kernel(place_ref, rows_ref, others_ref, same_ref, cross_ref, other_ref):
    z = place_ref[0] % 2
    for y in range(4):
        to = slice(y * LANES, (y + 1) * LANES)
        own = pl.ds(pl.multiple_of((2 * y + z) * LANES, LANES), LANES)
        same_ref[:, to] = rows_ref[:, own]
        other_ref[:, to] = others_ref[:, own]
        cross_ref[:, to] = rows_ref[:, pl.ds(pl.multiple_of((2 * y + 1 - z) * LANES, LANES), LANES)]


def quarters_of(place, layer_in):
    span, depth = layer_in.shape
    quarter = jax.ShapeDtypeStruct((span, depth // 4), jnp.bfloat16)
    return call(
        quarter_kernel, "quarters", 0, 5_000_000,
        grid_spec=pltpu.PrefetchScalarGridSpec(
            num_scalar_prefetch=1, grid=(2,),
            in_specs=[pl.BlockSpec((span, depth // 4), lambda i, place: (0, 2 * (place[1] % 2) + i)),
                      pl.BlockSpec((span, depth // 4), lambda i, place: (0, 2 - 2 * (place[1] % 2) + i))],
            out_specs=[pl.BlockSpec((span, 4 * LANES), lambda i, place: (0, i))] * 3),
        out_shape=[quarter] * 3,
    )(place, layer_in, layer_in)


def quad_place():
    seq_at = lax.axis_index("seq")
    return seq_at // 4 % 2 * 2 + seq_at % 2


def share_kernel(back_ref, *refs):
    parts, (out_ref, back_buf, rows_buf, out_buf, in_sem, out_sem) = refs[:8], refs[8:]
    span = rows_buf.shape[1]
    loads = [pltpu.make_async_copy(back_ref.at[:, pl.ds(0, 4 * span)], back_buf, in_sem.at[8])]
    loads += [pltpu.make_async_copy(part, rows_buf.at[n], in_sem.at[n]) for n, part in enumerate(parts)]
    for load in loads:
        load.start()
    loads[0].wait()
    stores = []
    for half in range(2):
        for load in loads[1 + 4 * half:5 + 4 * half]:
            load.wait()
        first = 8 * (half ^ (lax.axis_index("tp") % 2))
        for two in range(4):
            lanes = slice(two * 256, (two + 1) * 256)
            product = None
            for j in range(4):
                at = pl.multiple_of((quad_place() ^ j) * span, span)
                term = dot(back_buf[:, pl.ds(at, span)], rows_buf[4 * half + j, :, lanes])
                product = term if product is None else product + term
            product = product.astype(jnp.bfloat16)
            n = 4 * half + two
            out_buf[2 * n] = product[:, :LANES]
            out_buf[2 * n + 1] = product[:, LANES:]
            store = pltpu.make_async_copy(
                out_buf.at[pl.ds(2 * n, 2)], out_ref.at[pl.ds(first + 2 * two, 2)], out_sem.at[n])
            store.start()
            stores.append(store)
    for store in stores:
        store.wait()


def shares(back, mine, other):
    span, depth = mine[0].shape
    rows = back.shape[0]
    return call(
        share_kernel, "shares", 16 * rows * span * depth, 7_000_000, vmem=32,
        in_specs=[pl.BlockSpec(memory_space=pl.ANY)] * 9,
        out_specs=pl.BlockSpec(memory_space=pl.ANY),
        out_shape=jax.ShapeDtypeStruct((16, rows, LANES), jnp.bfloat16),
        scratch_shapes=[
            pltpu.VMEM((rows, 4 * span), jnp.bfloat16), pltpu.VMEM((8, span, depth), jnp.bfloat16),
            pltpu.VMEM((16, rows, LANES), jnp.bfloat16),
            pltpu.SemaphoreType.DMA((9,)), pltpu.SemaphoreType.DMA((8,))],
    )(back, *mine, *other)


def merge(pair, mine, mate):
    first, second = jnp.where(pair == 0, mine, mate), jnp.where(pair == 0, mate, mine)
    half = mine.shape[0] // 2
    return jnp.concatenate([first[half:], first[:half], second[:half], second[half:]], axis=0)


def weight_kernel(shares_ref, taps_ref, mate_ref, weight_ref, tap_sums_ref):
    for x in range(4):
        rows, lanes = slice(x * LANES, (x + 1) * LANES), slice(x * 2 * LANES, (x + 1) * 2 * LANES)
        totals = []
        for pair in range(2):
            terms = [shares_ref[j, rows, :].astype(jnp.float32) for j in range(16) if j % 4 // 2 == pair]
            totals.append(sum(terms[1:], terms[0]))
        weight_ref[:, lanes] = merge(0, *totals).T
        packed = merge(quad_place() // 2, taps_ref[rows, :].astype(jnp.float32), mate_ref[rows, :].astype(jnp.float32)).T
        tap_sums_ref[:, lanes] = (packed[16:24] + packed[8:16] + packed[0:8])[:TAPS]


def close_weight(parts, back, mate):
    count, rows, span = parts.shape
    channels = 2 * rows
    return call(
        weight_kernel, "close_weight", 2_000_000, 3_000_000, grid=(1,),
        in_specs=[whole(parts.shape),
                  pl.BlockSpec((rows, LANES), lambda i: (0, 12)), pl.BlockSpec((rows, LANES), lambda i: (0, 2))],
        out_specs=[whole((span, channels)), whole((TAPS, channels))],
        out_shape=[jax.ShapeDtypeStruct((span, channels), jnp.float32),
                   jax.ShapeDtypeStruct((TAPS, channels), jnp.float32)],
    )(parts, back, mate)


def input_kernel(place_ref, back_ref, mate_ref, *refs):
    weight_refs, (send_ref, keep_ref, own_buf) = refs[:STREAMS], refs[STREAMS:]

    @pl.when(pl.program_id(0) == 0)
    def _():
        pair = place_ref[0] // 2
        for x in range(4):
            for odd, mine, other in ((0, 1 + pair, 2 - pair), (1, 3 * pair, 3 - 3 * pair)):
                rows = slice((2 * x + odd) * 64, (2 * x + odd + 1) * 64)
                own_buf[pl.ds(pl.multiple_of((4 * x + mine) * 64, 64), 64), :] = back_ref[rows, :]
                own_buf[pl.ds(pl.multiple_of((4 * x + other) * 64, 64), 64), :] = mate_ref[rows, :]

    size = weight_refs[0].shape[0]
    terms = [dot(weight_ref[...], own_buf[...]) for weight_ref in weight_refs]

    @pl.when(pl.program_id(0) < 2)
    def _():
        for n, term in enumerate(terms):
            send_ref[0, n * size:(n + 1) * size] = term.astype(jnp.bfloat16)

    @pl.when(pl.program_id(0) >= 2)
    def _():
        for n, term in enumerate(terms):
            keep_ref[0, n * size:(n + 1) * size] = term


def input_terms(place, back, mate, w_value):
    depth, channels = w_value.shape
    rows, span = depth // 4, 256

    def stream(n):
        return pl.BlockSpec(
            (rows // STREAMS, channels),
            lambda i, place: (STREAMS * (place[1] ^ ((2 * i + 1 - i // 2) % 4)) + n, 0))

    return call(
        input_kernel, "input_terms", 2 * span * depth * channels, 12_000_000, vmem=56,
        grid_spec=pltpu.PrefetchScalarGridSpec(
            num_scalar_prefetch=1, grid=(4,),
            in_specs=[pl.BlockSpec((channels // 2, span), lambda i, place: (0, place[0])),
                      pl.BlockSpec((channels // 2, span), lambda i, place: (0, 0))] + [stream(n) for n in range(STREAMS)],
            out_specs=[pl.BlockSpec((1, rows, span), lambda i, place: (jnp.minimum(i, 1), 0, 0)),
                       pl.BlockSpec((1, rows, span), lambda i, place: (jnp.maximum(i - 2, 0), 0, 0))],
            scratch_shapes=[pltpu.VMEM((channels, span), jnp.bfloat16)]),
        out_shape=[jax.ShapeDtypeStruct((2, rows, span), jnp.bfloat16),
                   jax.ShapeDtypeStruct((2, rows, span), jnp.float32)],
    )(place, back, mate, *[w_value] * STREAMS)


def close_kernel(keep_ref, core_ref, chip_ref, out_ref):
    total = keep_ref[0] + core_ref[0].astype(jnp.float32) + chip_ref[...].astype(jnp.float32)
    out_ref[...] = total.T.astype(jnp.bfloat16)


def close_input(keep, core, chip):
    rows, span = chip.shape
    first = pl.BlockSpec((1, 512, span), lambda i: (0, i, 0))
    return call(
        close_kernel, "close_input", 1_000_000, 3_000_000, grid=(rows // 512,),
        in_specs=[first, first, pl.BlockSpec((512, span), lambda i: (i, 0))],
        out_specs=pl.BlockSpec((span, 512), lambda i: (0, i)),
        out_shape=jax.ShapeDtypeStruct((span, rows), jnp.bfloat16))(keep, core, chip)


def gate_kernel(place_ref, mixed_ref, mate_ref, gate_ref, grad_ref, out_ref):
    mixed = merge(place_ref[0] // 2, mixed_ref[...].astype(jnp.float32), mate_ref[...].astype(jnp.float32)).T
    sig = jax.nn.sigmoid(gate_ref[...].astype(jnp.float32))
    out_ref[...] = (grad_ref[...].astype(jnp.float32) * mixed * sig * (1.0 - sig)).astype(jnp.bfloat16)


def gate_grad(place, back, mate, gate, grads):
    span, channels = gate.shape
    block = pl.BlockSpec((span, channels // 4), lambda i, place: (0, i))
    return call(
        gate_kernel, "gate_grad", 2_000_000, 2_500_000,
        grid_spec=pltpu.PrefetchScalarGridSpec(
            num_scalar_prefetch=1, grid=(4,),
            in_specs=[pl.BlockSpec((LANES, span), lambda i, place: (i, 4 + place[0] // 2)),
                      pl.BlockSpec((LANES, span), lambda i, place: (i, 0)), block, block],
            out_specs=block),
        out_shape=jax.ShapeDtypeStruct(gate.shape, jnp.bfloat16))(place, back, mate, gate, grads)


def local(layer_in, w_value, short_taps, long_filters, gate_proj, grad_out):
    seq_count = lax.axis_size("seq")
    seq_at, tp_at = lax.axis_index("seq"), lax.axis_index("tp")
    span, depth = layer_in.shape
    channels = w_value.shape[1]
    width = channels // seq_count
    quad_at = quad_place()
    place = jnp.stack([quad_at, tp_at]).astype(jnp.int32)
    cores, chips = [(0, 1), (1, 0), (2, 3), (3, 2)], [(0, 2), (2, 0), (1, 3), (3, 1)]

    def exchange(value, index_groups=None):
        return lax.all_to_all(
            value, "seq", split_axis=0, concat_axis=0, axis_index_groups=index_groups, tiled=True)

    def mates(value):
        return lax.ppermute(value, "seq", [(s, s ^ MATE) for s in range(seq_count)])

    outgoing = sends(layer_in, w_value, gate_proj, grad_out, seq_count)
    rows_in, outgoing = lax.optimization_barrier((layer_in, outgoing))
    arrived = exchange(outgoing)
    same, cross, other = quarters_of(place, rows_in)
    spectra = spectra_of(long_filters)
    same, cross, spectra = lax.optimization_barrier((same, cross, spectra))

    def across(value, flip):
        return lax.ppermute(
            value, ("seq", "tp"), [(4 * s + t, 4 * (s ^ flip) + (t ^ 2)) for s in range(seq_count) for t in range(4)])

    mine = [same, across(cross, 1), mates(same), across(cross, 1 ^ MATE)]
    other = [other] + [lax.ppermute(part, "tp", cores) for part in mine[1:]]

    own_taps = lax.dynamic_slice_in_dim(short_taps, seq_at * width, width, 1)
    back, lag = mixer(own_taps, arrived, spectra)
    back, mine = lax.optimization_barrier((back, mine))
    back = exchange(back, LEAGUES).reshape(channels // 2, back.shape[2])
    grad_filters = filter_grads(lag)
    back, grad_filters, other = lax.optimization_barrier((back, grad_filters, other))
    mate = mates(lax.dynamic_slice_in_dim(back, (quad_at ^ 2) * span, span, 1))
    mate_rest = jnp.concatenate([
        lax.dynamic_slice_in_dim(back, 4 * span + (1 - quad_at // 2) * span, span, 1), back[:, 6 * span:]], axis=1)
    outgoing = shares(back, mine, other)
    outgoing, mate, mate_rest = lax.optimization_barrier((outgoing, mate, mate_rest))
    mate_rest = mates(mate_rest)
    parts = exchange(outgoing, PLANES)

    send, keep = input_terms(place, back, mate, w_value)
    core = lax.ppermute(send, "tp", cores)
    chip = lax.ppermute((keep[1] + core[1].astype(jnp.float32)).astype(jnp.bfloat16), "tp", chips)
    grad_input = close_input(keep, core, chip)
    grad_gate = gate_grad(place, back, mate_rest, gate_proj, grad_out)
    parts, grad_input, grad_gate = lax.optimization_barrier((parts, grad_input, grad_gate))
    grad_weight, grad_taps = close_weight(parts, back, mate_rest)
    return (grad_input, grad_weight, grad_taps, grad_filters, grad_gate)


def solution(mesh):
    in_specs = (
        P("seq", None),
        P(None, "tp"),
        P(None, "tp"),
        P(None, ("tp", "seq"), None),
        P("seq", "tp"),
        P("seq", "tp"),
    )
    out_specs = (
        P("seq", "tp"),
        P("seq", "tp"),
        P(None, "tp"),
        P(None, ("tp", "seq"), None),
        P("seq", "tp"),
    )
    return jax.shard_map(local, mesh=mesh, in_specs=in_specs, out_specs=out_specs, check_vma=False)
```

```python
import functools
import math

import jax
import jax.numpy as jnp
import ml_dtypes
import numpy as np
from jax import lax
from jax.experimental import pallas as pl
from jax.experimental.pallas import tpu as pltpu
from jax.sharding import PartitionSpec as P

LANES = 128
ROWS = 64
LENGTH = ROWS * LANES
TAPS = 7
REACH = TAPS // 2
BATCH = 4
GROUP, GROUPS = 2, 8


def halves(table):
    high = table.astype(ml_dtypes.bfloat16)
    low = (table - high.astype(np.float64)).astype(ml_dtypes.bfloat16)
    return high, low


@functools.lru_cache(maxsize=None)
def tables(blocks):
    half = np.arange(ROWS) + 0.5
    natural = np.arange(ROWS)
    split = (2 * np.arange(blocks)[None, :] + np.arange(2)[:, None]).reshape(-1)

    def first(order):
        turn = 2.0 * math.pi / LANES * np.outer(half, order)
        return halves(np.concatenate([np.cos(turn), -np.sin(turn)], axis=0))

    def last(order):
        turn = 2.0 * math.pi / LANES * np.outer(order, half)
        return halves(np.concatenate([np.cos(turn), -np.sin(turn)], axis=1) / LENGTH)

    split_high, split_low = first(split)
    nat_high, nat_low = first(natural)
    first_split = np.concatenate([split_high, split_low], axis=1)
    first_nat = np.concatenate([nat_high, nat_low, nat_high, nat_low], axis=1)
    inv_split_high, inv_split_low = last(split)
    inv_nat_high, inv_nat_low = last(natural)
    last_split = np.concatenate([inv_split_high, inv_split_high, inv_split_low], axis=1)
    last_nat = np.concatenate([inv_nat_high, inv_nat_high, inv_nat_low], axis=1)
    twist = 2.0 * math.pi / (2 * LENGTH) * np.outer(half, np.arange(LANES))
    twist = np.stack([np.cos(twist), -np.sin(twist)]).astype(np.float32)
    grid = 2.0 * math.pi / LANES * np.outer(np.arange(LANES), np.arange(LANES))
    cos, sin = np.cos(grid), np.sin(grid)

    def stacked(table):
        high, low = halves(table)
        return np.concatenate([high, high, low], axis=0)

    forward = np.block([[cos, -sin], [sin, cos]])
    mirror = np.block([[cos, sin], [sin, -cos]])
    inverse = np.block([[cos, sin], [-sin, cos]])
    pair = np.concatenate([stacked(forward), stacked(mirror)], axis=0)
    both = np.concatenate([stacked(inverse), stacked(np.block([[cos, sin], [sin, -cos]]))], axis=1)
    return {
        "first_split": first_split, "first_nat": first_nat, "twist": twist, "forward": stacked(forward), "pair": pair,
        "inverse": stacked(inverse), "both": both, "last_split": last_split, "last_nat": last_nat,
    }


def cut(value):
    high = value.astype(jnp.bfloat16)
    low = (value - high.astype(jnp.float32)).astype(jnp.bfloat16)
    return high, low


def store_parts(ref, row, col, real, imag):
    real_high, real_low = cut(real)
    imag_high, imag_low = cut(imag)
    parts = (real_high, imag_high, real_low, imag_low, real_high, imag_high)
    for at, part in enumerate(parts):
        ref[row:row + ROWS, col + at * LANES:col + (at + 1) * LANES] = part


def shifted(early, late, step):
    if step == 0:
        return early, late
    lane = lax.broadcasted_iota(jnp.int32, early.shape, 1)
    row = lax.broadcasted_iota(jnp.int32, early.shape, 0)
    count = early.shape[0]
    turned_early = pltpu.roll(early, (-step) % LANES, 1)
    turned_late = pltpu.roll(late, (-step) % LANES, 1)
    if step > 0:
        keep = lane < LANES - step
        beyond = jnp.where(row == count - 1, 0.0, pltpu.roll(turned_early, count - 1, 0))
        return jnp.where(keep, turned_early, turned_late), jnp.where(keep, turned_late, beyond)
    keep = lane >= -step
    before = jnp.where(row == 0, 0.0, pltpu.roll(turned_late, 1, 0))
    return jnp.where(keep, turned_early, before), jnp.where(keep, turned_late, turned_early)


def dot(left, right):
    return jnp.dot(left, right, preferred_element_type=jnp.float32)


Y_OF = ((1, 2), (0, 3))
QUADS = [[(x * 4 + Y_OF[odd][pair]) * 2 + z for pair in range(2) for z in range(2)] for x in range(4) for odd in range(2)]
LEAGUES = [[quad[2 * pair + z] for quad in QUADS for z in range(2)] for pair in range(2)]
PLANES = [[2 * j + z for j in range(16)] for z in range(2)]
MATE = 6


def twisted(array, col, twist_ref):
    real = array[:ROWS, col * LANES:(col + 1) * LANES]
    imag = array[ROWS:, col * LANES:(col + 1) * LANES]
    return real * twist_ref[0] - imag * twist_ref[1], real * twist_ref[1] + imag * twist_ref[0]


def untwisted(array, twist_ref):
    real, imag = array[:, :LANES], array[:, LANES:]
    return jnp.concatenate(
        [real * twist_ref[0] + imag * twist_ref[1], imag * twist_ref[0] - real * twist_ref[1]], axis=0)


def finish(table_ref, one, two):
    high, low = cut(jnp.concatenate([one, two], axis=1))
    return dot(table_ref[...], jnp.concatenate([high, low, high], axis=0))


def spectra_kernel(filters_ref, first_nat_ref, twist_ref, pair_ref, out_ref, kernel_buf):
    for q in range(BATCH):
        at = (pl.program_id(0) % (8 // BATCH)) * BATCH + q
        plus = filters_ref[0, 0, pl.ds(at, ROWS, stride=8), :]
        minus = filters_ref[1, 0, pl.ds(at, ROWS, stride=8), :]
        high, low = cut(jnp.concatenate([plus, minus], axis=1))
        section = dot(first_nat_ref[...], jnp.concatenate([high, high, low, low], axis=0))
        store_parts(kernel_buf, q * ROWS, 0, *twisted(section, 0, twist_ref))
        store_parts(kernel_buf, q * ROWS, 6 * LANES, *twisted(section, 1, twist_ref))
    out_ref[...] = dot(kernel_buf[...], pair_ref[...])


def lag_kernel(lag_ref, twist_ref, both_ref, last_nat_ref, out_ref):
    parts = lag_ref[...]
    unmixed = dot(jnp.concatenate([parts, parts[:, :2 * LANES]], axis=1), both_ref[...])
    for q in range(BATCH):
        at = (pl.program_id(0) % (8 // BATCH)) * BATCH + q
        rows = slice(q * ROWS, (q + 1) * ROWS)
        pair = finish(last_nat_ref, untwisted(unmixed[rows, :2 * LANES], twist_ref),
                      untwisted(unmixed[rows, 2 * LANES:], twist_ref))
        out_ref[0, 0, pl.ds(at, ROWS, stride=8), :] = pair[:, :LANES]
        out_ref[1, 0, pl.ds(at, ROWS, stride=8), :] = pair[:, LANES:]


def mixer_kernel(
    taps_ref, arrived_ref, spectra_ref, first_split_ref, twist_ref, forward_ref, inverse_ref, last_split_ref,
    back_ref, lag_ref,
    values_buf, slopes_buf, back_buf, mixed_buf, taps_buf, extra_buf, signal_buf, product_buf,
):
    blocks, width = arrived_ref.shape[0], arrived_ref.shape[1] // 2
    step = pl.program_id(0)

    @pl.when(step == 0)
    def _():
        for h in range(2):
            part = slice(h * LANES, (h + 1) * LANES)
            values_buf[h] = arrived_ref[:, :width, part].astype(jnp.float32).reshape(blocks * width, LANES)
            slopes_buf[h] = arrived_ref[:, width:, part].astype(jnp.float32).reshape(blocks * width, LANES)

    pooled = {}

    def start(g):
        for q in range(g * GROUP, (g + 1) * GROUP):
            c = step * GROUP * GROUPS + q
            early = values_buf[0, pl.ds(c, blocks, stride=width), :]
            late = values_buf[1, pl.ds(c, blocks, stride=width), :]
            sum_early, sum_late = None, None
            for k in range(TAPS):
                one, two = shifted(early, late, k - REACH)
                tap = taps_ref[k, c]
                sum_early = tap * one if k == 0 else sum_early + tap * one
                sum_late = tap * two if k == 0 else sum_late + tap * two
            short = jnp.concatenate([sum_early, sum_late], axis=0).astype(jnp.bfloat16)
            conv = short.astype(jnp.float32)
            slope = jnp.concatenate(
                [slopes_buf[h, pl.ds(c, blocks, stride=width), :] for h in range(2)], axis=0)
            sig = jax.nn.sigmoid(conv)
            pooled[q] = jnp.sum(conv * sig, keepdims=True) / LENGTH
            mean_grad = jnp.sum(slope, keepdims=True) / LENGTH
            extra_buf[q] = mean_grad * (sig * (1.0 + conv * (1.0 - sig)))
            both = jnp.concatenate([short, slope.astype(jnp.bfloat16)], axis=1)
            section = dot(first_split_ref[...], jnp.concatenate([both, both], axis=0))
            store_parts(signal_buf, 2 * q * ROWS, 0, *twisted(section, 0, twist_ref))
            store_parts(signal_buf, (2 * q + 1) * ROWS, 0, *twisted(section, 1, twist_ref))

    def multiply(g):
        base = 2 * g * GROUP * ROWS
        spec = dot(signal_buf[base:base + 2 * GROUP * ROWS], forward_ref[...])
        for q in range(GROUP):
            short, slope = spec[2 * q * ROWS:(2 * q + 1) * ROWS], spec[(2 * q + 1) * ROWS:(2 * q + 2) * ROWS]
            rows = slice((g * GROUP + q) * ROWS, (g * GROUP + q + 1) * ROWS)
            short_re, short_im = short[:, :LANES], short[:, LANES:]
            slope_re, slope_im = slope[:, :LANES], slope[:, LANES:]
            filt_re, filt_im = spectra_ref[rows, :LANES], spectra_ref[rows, LANES:]
            store_parts(product_buf, base + 2 * q * ROWS, 0,
                        short_re * filt_re - short_im * filt_im, short_re * filt_im + short_im * filt_re)
            store_parts(product_buf, base + (2 * q + 1) * ROWS, 0,
                        slope_re * filt_re + slope_im * filt_im, slope_im * filt_re - slope_re * filt_im)
            real_high, real_low = cut(slope_re * short_re + slope_im * short_im)
            imag_high, imag_low = cut(slope_im * short_re - slope_re * short_im)
            for at, part in enumerate((real_high, imag_high, real_low, imag_low)):
                lag_ref[rows, at * LANES:(at + 1) * LANES] = part

    def end(g):
        base = 2 * g * GROUP * ROWS
        unmixed = dot(product_buf[base:base + 2 * GROUP * ROWS], inverse_ref[...])
        for q in range(GROUP):
            c = step * GROUP * GROUPS + g * GROUP + q
            rows = 2 * q * ROWS
            long_pair = finish(last_split_ref, untwisted(unmixed[rows:rows + ROWS], twist_ref),
                               untwisted(unmixed[rows + ROWS:rows + 2 * ROWS], twist_ref))
            mixed = long_pair[:, :LANES] + pooled[g * GROUP + q]
            slope_back = long_pair[:, LANES:] + extra_buf[g * GROUP + q]
            slope_back = slope_back.astype(jnp.bfloat16).astype(jnp.float32)
            early = values_buf[0, pl.ds(c, blocks, stride=width), :]
            late = values_buf[1, pl.ds(c, blocks, stride=width), :]
            sum_early, sum_late = None, None
            for k in range(TAPS):
                one, two = shifted(slope_back[:blocks], slope_back[blocks:], REACH - k)
                tap = taps_ref[k, c]
                sum_early = tap * one if k == 0 else sum_early + tap * one
                sum_late = tap * two if k == 0 else sum_late + tap * two
                taps_buf[k, pl.ds(c, 1), :] = jnp.sum(one * early + two * late, axis=0, keepdims=True)
            for h, part in enumerate((sum_early, sum_late)):
                back_buf[h, pl.ds(c, blocks, stride=width), :] = part
                mixed_buf[h, pl.ds(c, blocks, stride=width), :] = mixed[h * blocks:(h + 1) * blocks]

    for turn in range(GROUPS + 2):
        if turn >= 2:
            end(turn - 2)
        if 1 <= turn <= GROUPS:
            multiply(turn - 1)
        if turn < GROUPS:
            start(turn)

    @pl.when(step == pl.num_programs(0) - 1)
    def _():
        for q, quad in enumerate(QUADS):
            for place, s in enumerate(quad):
                rows = slice(s * width, (s + 1) * width)
                for h in range(2):
                    part = back_buf[h, rows, :].astype(jnp.bfloat16)
                    lanes = slice((2 * place + h) * LANES, (2 * place + h + 1) * LANES)
                    back_ref[2 * q, :, lanes] = part
                    back_ref[2 * q + 1, :, lanes] = part
                    at = 8 + 2 * (place // 2) + h
                    back_ref[2 * q + place % 2, :, at * LANES:(at + 1) * LANES] = (
                        mixed_buf[h, rows, :].astype(jnp.bfloat16))
        lane = lax.broadcasted_iota(jnp.int32, (width, LANES), 1)
        packed = jnp.zeros((width, LANES), jnp.float32)
        for k in range(TAPS):
            rest = jnp.sum(taps_buf[k], axis=1, keepdims=True)
            for p in range(3):
                piece = rest.astype(jnp.bfloat16).astype(jnp.float32)
                packed = jnp.where(lane == 8 * p + k, piece, packed)
                rest = rest - piece
        for d in range(blocks // 2):
            back_ref[d, :, 12 * LANES:] = packed.astype(jnp.bfloat16)


def whole(shape):
    return pl.BlockSpec(shape, lambda *_: (0,) * len(shape))


def call(kernel, name, flops, nbytes, vmem=16, **kwargs):
    return pl.pallas_call(
        kernel, name=name,
        compiler_params=pltpu.CompilerParams(vmem_limit_bytes=vmem * 1024 * 1024),
        cost_estimate=pl.CostEstimate(flops=flops, bytes_accessed=nbytes, transcendentals=0), **kwargs)


def tables_of(names, blocks=LENGTH // 256):
    chosen = [jnp.asarray(tables(blocks)[name]) for name in names]
    return chosen, [whole(table.shape) for table in chosen]


PER_TILE = pl.BlockSpec((2, 1, ROWS * 8, LANES), lambda i: (0, i // (8 // BATCH), 0, 0))


def spectra_of(filters):
    width = filters.shape[1]
    tiles = width // 8
    view = filters.reshape(2, tiles, 8, ROWS, LANES).transpose(0, 1, 3, 2, 4).reshape(2, tiles, ROWS * 8, LANES)
    consts, specs = tables_of(("first_nat", "twist", "pair"))
    return call(
        spectra_kernel, "spectra", 3_000_000_000, 5_000_000, vmem=56,
        grid=(width // BATCH,), in_specs=[PER_TILE] + specs,
        out_specs=pl.BlockSpec((BATCH * ROWS, 2 * LANES), lambda i: (i, 0)),
        out_shape=jax.ShapeDtypeStruct((width * ROWS, 2 * LANES), jnp.float32),
        scratch_shapes=[pltpu.VMEM((BATCH * ROWS, 12 * LANES), jnp.bfloat16)],
    )(view, *consts)


def filter_grads(lag):
    width = lag.shape[0] // ROWS
    tiles = width // 8
    consts, specs = tables_of(("twist", "both", "last_nat"))
    out = call(
        lag_kernel, "filter_grads", 3_000_000_000, 5_000_000,
        grid=(width // BATCH,),
        in_specs=[pl.BlockSpec((BATCH * ROWS, 4 * LANES), lambda i: (i, 0))] + specs,
        out_specs=PER_TILE,
        out_shape=jax.ShapeDtypeStruct((2, tiles, ROWS * 8, LANES), jnp.float32),
    )(lag, *consts)
    return out.reshape(2, tiles, ROWS, 8, LANES).transpose(0, 1, 3, 2, 4).reshape(2, width, LENGTH)


def mixer(own_taps, arrived, spectra):
    blocks, width, span = arrived.shape[0], arrived.shape[1] // 2, arrived.shape[2]
    consts, specs = tables_of(("first_split", "twist", "forward", "inverse", "last_split"))
    back_shape = (blocks // 2, width, 6 * span + LANES)
    rows, batch = (2, blocks * width, LANES), GROUP * GROUPS
    return call(
        mixer_kernel, "mixer", 100_000_000, 1_000_000, vmem=56,
        grid=(width // batch,),
        in_specs=[pl.BlockSpec(memory_space=pltpu.SMEM), whole(arrived.shape),
                  pl.BlockSpec((batch * ROWS, 2 * LANES), lambda i: (i, 0))] + specs,
        out_specs=[whole(back_shape), pl.BlockSpec((batch * ROWS, 4 * LANES), lambda i: (i, 0))],
        out_shape=[
            jax.ShapeDtypeStruct(back_shape, jnp.bfloat16),
            jax.ShapeDtypeStruct((width * ROWS, 4 * LANES), jnp.bfloat16),
        ],
        scratch_shapes=[
            pltpu.VMEM(rows, jnp.float32),
            pltpu.VMEM(rows, jnp.float32),
            pltpu.VMEM(rows, jnp.float32),
            pltpu.VMEM(rows, jnp.float32),
            pltpu.VMEM((TAPS, width, LANES), jnp.float32),
            pltpu.VMEM((batch, ROWS, LANES), jnp.float32),
            pltpu.VMEM((2 * batch * ROWS, 6 * LANES), jnp.bfloat16),
            pltpu.VMEM((2 * batch * ROWS, 6 * LANES), jnp.bfloat16),
        ],
    )(own_taps, arrived, spectra, *consts)


STREAMS = 4


def send_kernel(rows_ref, *refs):
    weight_refs, (gate_ref, grad_ref, out_ref, total_ref) = refs[:STREAMS], refs[STREAMS:]
    blocks, width, span = out_ref.shape[0], out_ref.shape[1] // 2, out_ref.shape[2]
    step, steps = pl.program_id(0), pl.num_programs(0)
    count = blocks * gate_ref.shape[1] // total_ref.shape[1]
    sig = jax.nn.sigmoid(gate_ref[...].astype(jnp.float32))
    slopes = (grad_ref[...].astype(jnp.float32) * sig).T.astype(jnp.bfloat16)
    out_ref[pl.ds(step * count, count), width:, :] = slopes.reshape(count, width, span)
    part = weight_refs[0].shape[0]
    term = dot(rows_ref[:, :part], weight_refs[0][...])
    for j in range(1, STREAMS):
        term = term + dot(rows_ref[:, j * part:(j + 1) * part], weight_refs[j][...])

    @pl.when(step == 0)
    def _():
        total_ref[...] = term

    @pl.when((step > 0) & (step < steps - 1))
    def _():
        total_ref[...] += term

    @pl.when(step == steps - 1)
    def _():
        total = total_ref[...] + term
        out_ref[:, :width, :] = total.T.astype(jnp.bfloat16).reshape(blocks, width, span)


def sends(layer_in, w_value, gate, grads, count, steps=4):
    span, depth = layer_in.shape
    channels = w_value.shape[1]
    width = channels // count
    block = pl.BlockSpec((span, channels // steps), lambda i: (0, i))
    streams = [pl.BlockSpec((depth // (steps * STREAMS), channels), functools.partial(lambda j, i: (STREAMS * i + j, 0), j))
               for j in range(STREAMS)]
    return call(
        send_kernel, "sends", 2 * span * depth * channels, 12_500_000, vmem=56, grid=(steps,),
        in_specs=[pl.BlockSpec((span, depth // steps), lambda i: (0, i))] + streams + [block, block],
        out_specs=whole((count, 2 * width, span)),
        out_shape=jax.ShapeDtypeStruct((count, 2 * width, span), jnp.bfloat16),
        scratch_shapes=[pltpu.VMEM((span, channels), jnp.float32)],
    )(layer_in, *[w_value] * STREAMS, gate, grads)


def quarter_kernel(place_ref, rows_ref, others_ref, same_ref, cross_ref, other_ref):
    z = place_ref[0] % 2
    for y in range(4):
        to = slice(y * LANES, (y + 1) * LANES)
        own = pl.ds(pl.multiple_of((2 * y + z) * LANES, LANES), LANES)
        same_ref[:, to] = rows_ref[:, own]
        other_ref[:, to] = others_ref[:, own]
        cross_ref[:, to] = rows_ref[:, pl.ds(pl.multiple_of((2 * y + 1 - z) * LANES, LANES), LANES)]


def quarters_of(place, layer_in):
    span, depth = layer_in.shape
    quarter = jax.ShapeDtypeStruct((span, depth // 4), jnp.bfloat16)
    return call(
        quarter_kernel, "quarters", 0, 5_000_000,
        grid_spec=pltpu.PrefetchScalarGridSpec(
            num_scalar_prefetch=1, grid=(2,),
            in_specs=[pl.BlockSpec((span, depth // 4), lambda i, place: (0, 2 * (place[1] % 2) + i)),
                      pl.BlockSpec((span, depth // 4), lambda i, place: (0, 2 - 2 * (place[1] % 2) + i))],
            out_specs=[pl.BlockSpec((span, 4 * LANES), lambda i, place: (0, i))] * 3),
        out_shape=[quarter] * 3,
    )(place, layer_in, layer_in)


def quad_place():
    seq_at = lax.axis_index("seq")
    return seq_at // 4 % 2 * 2 + seq_at % 2


def share_kernel(back_ref, *refs):
    parts, (out_ref, back_buf, rows_buf, out_buf, in_sem, out_sem) = refs[:8], refs[8:]
    span = rows_buf.shape[1]
    loads = [pltpu.make_async_copy(back_ref.at[:, pl.ds(0, 4 * span)], back_buf, in_sem.at[8])]
    loads += [pltpu.make_async_copy(part, rows_buf.at[n], in_sem.at[n]) for n, part in enumerate(parts)]
    for load in loads:
        load.start()
    loads[0].wait()
    stores = []
    for half in range(2):
        for load in loads[1 + 4 * half:5 + 4 * half]:
            load.wait()
        first = 8 * (half ^ (lax.axis_index("tp") % 2))
        for two in range(4):
            lanes = slice(two * 256, (two + 1) * 256)
            product = None
            for j in range(4):
                at = pl.multiple_of((quad_place() ^ j) * span, span)
                term = dot(back_buf[:, pl.ds(at, span)], rows_buf[4 * half + j, :, lanes])
                product = term if product is None else product + term
            product = product.astype(jnp.bfloat16)
            n = 4 * half + two
            out_buf[2 * n] = product[:, :LANES]
            out_buf[2 * n + 1] = product[:, LANES:]
            store = pltpu.make_async_copy(
                out_buf.at[pl.ds(2 * n, 2)], out_ref.at[pl.ds(first + 2 * two, 2)], out_sem.at[n])
            store.start()
            stores.append(store)
    for store in stores:
        store.wait()


def shares(back, mine, other):
    span, depth = mine[0].shape
    rows = back.shape[0]
    return call(
        share_kernel, "shares", 16 * rows * span * depth, 7_000_000, vmem=60,
        in_specs=[pl.BlockSpec(memory_space=pl.ANY)] * 9,
        out_specs=pl.BlockSpec(memory_space=pl.ANY),
        out_shape=jax.ShapeDtypeStruct((16, rows, LANES), jnp.bfloat16),
        scratch_shapes=[
            pltpu.VMEM((rows, 4 * span), jnp.bfloat16), pltpu.VMEM((8, span, depth), jnp.bfloat16),
            pltpu.VMEM((16, rows, LANES), jnp.bfloat16),
            pltpu.SemaphoreType.DMA((9,)), pltpu.SemaphoreType.DMA((8,))],
    )(back, *mine, *other)


def merge(pair, mine, mate):
    first, second = jnp.where(pair == 0, mine, mate), jnp.where(pair == 0, mate, mine)
    half = mine.shape[0] // 2
    return jnp.concatenate([first[half:], first[:half], second[:half], second[half:]], axis=0)


def weight_kernel(shares_ref, taps_ref, mate_ref, weight_ref, tap_sums_ref):
    for x in range(4):
        rows, lanes = slice(x * LANES, (x + 1) * LANES), slice(x * 2 * LANES, (x + 1) * 2 * LANES)
        totals = []
        for pair in range(2):
            terms = [shares_ref[j, rows, :].astype(jnp.float32) for j in range(16) if j % 4 // 2 == pair]
            totals.append(sum(terms[1:], terms[0]))
        weight_ref[:, lanes] = merge(0, *totals).T
        packed = merge(quad_place() // 2, taps_ref[rows, :].astype(jnp.float32), mate_ref[rows, :].astype(jnp.float32)).T
        tap_sums_ref[:, lanes] = (packed[16:24] + packed[8:16] + packed[0:8])[:TAPS]


def close_weight(parts, back, mate):
    count, rows, span = parts.shape
    channels = 2 * rows
    return call(
        weight_kernel, "close_weight", 2_000_000, 3_000_000, grid=(1,),
        in_specs=[whole(parts.shape),
                  pl.BlockSpec((rows, LANES), lambda i: (0, 12)), pl.BlockSpec((rows, LANES), lambda i: (0, 4))],
        out_specs=[whole((span, channels)), whole((TAPS, channels))],
        out_shape=[jax.ShapeDtypeStruct((span, channels), jnp.float32),
                   jax.ShapeDtypeStruct((TAPS, channels), jnp.float32)],
    )(parts, back, mate)


def input_kernel(
    back_ref, mate_ref, weight_ref, send_ref, keep_ref,
    mine_buf, mate_buf, own_buf, weight_buf, send_buf, keep_buf, own_sem, weight_sem, out_sem,
):
    span, rows = mine_buf.shape[1], weight_buf.shape[1]
    part = rows // STREAMS
    at = quad_place()
    own = [
        pltpu.make_async_copy(
            back_ref.at[:, pl.ds(pl.multiple_of(at * span, span), span)], mine_buf, own_sem.at[0]),
        pltpu.make_async_copy(mate_ref.at[:, pl.ds(0, span)], mate_buf, own_sem.at[1]),
    ]
    loads = []
    for n, flip in enumerate((1, 3, 0, 2)):
        base = (lax.axis_index("tp") ^ flip) * rows
        loads.append([
            pltpu.make_async_copy(
                weight_ref.at[pl.ds(pl.multiple_of(base + j * part, part), part)],
                weight_buf.at[n, pl.ds(j * part, part)], weight_sem.at[n, j]) for j in range(STREAMS)])
    for load in own + sum(loads, []):
        load.start()
    for load in own:
        load.wait()
    pair = at // 2
    for x in range(4):
        for odd, mine, other in ((0, 1 + pair, 2 - pair), (1, 3 * pair, 3 - 3 * pair)):
            rows_in = slice((2 * x + odd) * 64, (2 * x + odd + 1) * 64)
            own_buf[pl.ds(pl.multiple_of((4 * x + mine) * 64, 64), 64), :] = mine_buf[rows_in, :]
            own_buf[pl.ds(pl.multiple_of((4 * x + other) * 64, 64), 64), :] = mate_buf[rows_in, :]
    stores = []
    for n in range(4):
        for load in loads[n]:
            load.wait()
        term = dot(weight_buf[n], own_buf[...])
        buf, ref = (send_buf, send_ref) if n < 2 else (keep_buf, keep_ref)
        buf[n % 2] = term.astype(buf.dtype)
        store = pltpu.make_async_copy(buf.at[n % 2], ref.at[n % 2], out_sem.at[n])
        store.start()
        stores.append(store)
    for store in stores:
        store.wait()


def input_terms(back, mate, w_value):
    depth, channels = w_value.shape
    rows, span = depth // 4, 256
    anywhere = pl.BlockSpec(memory_space=pl.ANY)
    return call(
        input_kernel, "input_terms", 2 * span * depth * channels, 12_000_000, vmem=56,
        in_specs=[anywhere] * 3, out_specs=[anywhere] * 2,
        out_shape=[jax.ShapeDtypeStruct((2, rows, span), jnp.bfloat16),
                   jax.ShapeDtypeStruct((2, rows, span), jnp.float32)],
        scratch_shapes=[
            pltpu.VMEM((channels // 2, span), jnp.bfloat16), pltpu.VMEM((channels // 2, span), jnp.bfloat16),
            pltpu.VMEM((channels, span), jnp.bfloat16), pltpu.VMEM((4, rows, channels), jnp.bfloat16),
            pltpu.VMEM((2, rows, span), jnp.bfloat16), pltpu.VMEM((2, rows, span), jnp.float32),
            pltpu.SemaphoreType.DMA((2,)), pltpu.SemaphoreType.DMA((4, STREAMS)), pltpu.SemaphoreType.DMA((4,))],
    )(back, mate, w_value)


def close_kernel(keep_ref, core_ref, chip_ref, out_ref):
    total = keep_ref[0] + core_ref[0].astype(jnp.float32) + chip_ref[...].astype(jnp.float32)
    out_ref[...] = total.T.astype(jnp.bfloat16)


def close_input(keep, core, chip):
    rows, span = chip.shape
    first = pl.BlockSpec((1, 512, span), lambda i: (0, i, 0))
    return call(
        close_kernel, "close_input", 1_000_000, 3_000_000, grid=(rows // 512,),
        in_specs=[first, first, pl.BlockSpec((512, span), lambda i: (i, 0))],
        out_specs=pl.BlockSpec((span, 512), lambda i: (0, i)),
        out_shape=jax.ShapeDtypeStruct((span, rows), jnp.bfloat16))(keep, core, chip)


def gate_kernel(place_ref, mixed_ref, mate_ref, gate_ref, grad_ref, out_ref):
    mixed = merge(place_ref[0] // 2, mixed_ref[...].astype(jnp.float32), mate_ref[...].astype(jnp.float32)).T
    sig = jax.nn.sigmoid(gate_ref[...].astype(jnp.float32))
    out_ref[...] = (grad_ref[...].astype(jnp.float32) * mixed * sig * (1.0 - sig)).astype(jnp.bfloat16)


def gate_grad(place, back, mate, gate, grads):
    span, channels = gate.shape
    block = pl.BlockSpec((span, channels // 4), lambda i, place: (0, i))
    return call(
        gate_kernel, "gate_grad", 2_000_000, 2_500_000,
        grid_spec=pltpu.PrefetchScalarGridSpec(
            num_scalar_prefetch=1, grid=(4,),
            in_specs=[pl.BlockSpec((LANES, span), lambda i, place: (i, 4 + place[0] // 2)),
                      pl.BlockSpec((LANES, span), lambda i, place: (i, 1)), block, block],
            out_specs=block),
        out_shape=jax.ShapeDtypeStruct(gate.shape, jnp.bfloat16))(place, back, mate, gate, grads)


def local(layer_in, w_value, short_taps, long_filters, gate_proj, grad_out):
    seq_count = lax.axis_size("seq")
    seq_at, tp_at = lax.axis_index("seq"), lax.axis_index("tp")
    span, depth = layer_in.shape
    channels = w_value.shape[1]
    width = channels // seq_count
    quad_at = quad_place()
    place = jnp.stack([quad_at, tp_at]).astype(jnp.int32)
    cores, chips = [(0, 1), (1, 0), (2, 3), (3, 2)], [(0, 2), (2, 0), (1, 3), (3, 1)]

    def exchange(value, index_groups=None):
        return lax.all_to_all(
            value, "seq", split_axis=0, concat_axis=0, axis_index_groups=index_groups, tiled=True)

    def mates(value):
        return lax.ppermute(value, "seq", [(s, s ^ MATE) for s in range(seq_count)])

    outgoing = sends(layer_in, w_value, gate_proj, grad_out, seq_count)
    rows_in, outgoing = lax.optimization_barrier((layer_in, outgoing))
    arrived = exchange(outgoing)
    same, cross, other = quarters_of(place, rows_in)

    def across(value, flip):
        return lax.ppermute(
            value, ("seq", "tp"), [(4 * s + t, 4 * (s ^ flip) + (t ^ 2)) for s in range(seq_count) for t in range(4)])

    first = across(cross, 1)
    spectra = spectra_of(long_filters)
    same, cross, spectra = lax.optimization_barrier((same, cross, spectra))
    mine = [same, first, mates(same), across(cross, 1 ^ MATE)]

    own_taps = lax.dynamic_slice_in_dim(short_taps, seq_at * width, width, 1)
    back, lag = mixer(own_taps, arrived, spectra)
    back, mine = lax.optimization_barrier((back, mine))
    other = [other] + [lax.ppermute(part, "tp", cores) for part in mine[1:]]
    back = exchange(back, LEAGUES).reshape(channels // 2, back.shape[2])
    grad_filters = filter_grads(lag)
    back, grad_filters, other = lax.optimization_barrier((back, grad_filters, other))
    mate = mates(jnp.concatenate([
        lax.dynamic_slice_in_dim(back, (quad_at ^ 2) * span, span, 1),
        lax.dynamic_slice_in_dim(back, 4 * span + (1 - quad_at // 2) * span, span, 1),
        back[:, 6 * span:]], axis=1))
    parts = exchange(shares(back, mine, other), PLANES)

    send, keep = input_terms(back, mate, w_value)
    core = lax.ppermute(send, "tp", cores)
    send = (keep[1] + core[1].astype(jnp.float32)).astype(jnp.bfloat16)
    chip = lax.ppermute(send, "tp", chips)
    grad_input = close_input(keep, core, chip)
    grad_gate = gate_grad(place, back, mate, gate_proj, grad_out)
    parts, grad_input, grad_gate = lax.optimization_barrier((parts, grad_input, grad_gate))
    grad_weight, grad_taps = close_weight(parts, back, mate)
    return (grad_input, grad_weight, grad_taps, grad_filters, grad_gate)


def solution(mesh):
    in_specs = (
        P("seq", None),
        P(None, "tp"),
        P(None, "tp"),
        P(None, ("tp", "seq"), None),
        P("seq", "tp"),
        P("seq", "tp"),
    )
    out_specs = (
        P("seq", "tp"),
        P("seq", "tp"),
        P(None, "tp"),
        P(None, ("tp", "seq"), None),
        P("seq", "tp"),
    )
    return jax.shard_map(local, mesh=mesh, in_specs=in_specs, out_specs=out_specs, check_vma=False)
```

```python
import functools
import math

import jax
import jax.numpy as jnp
import ml_dtypes
import numpy as np
from jax import lax
from jax.experimental import pallas as pl
from jax.experimental.pallas import tpu as pltpu
from jax.sharding import PartitionSpec as P

LANES = 128
ROWS = 64
LENGTH = ROWS * LANES
TAPS = 7
REACH = TAPS // 2
BATCH = 4
GROUP, GROUPS = 2, 8


def halves(table):
    high = table.astype(ml_dtypes.bfloat16)
    low = (table - high.astype(np.float64)).astype(ml_dtypes.bfloat16)
    return high, low


@functools.lru_cache(maxsize=None)
def tables(blocks):
    half = np.arange(ROWS) + 0.5
    natural = np.arange(ROWS)
    split = (2 * np.arange(blocks)[None, :] + np.arange(2)[:, None]).reshape(-1)

    def first(order):
        turn = 2.0 * math.pi / LANES * np.outer(half, order)
        return halves(np.concatenate([np.cos(turn), -np.sin(turn)], axis=0))

    def last(order):
        turn = 2.0 * math.pi / LANES * np.outer(order, half)
        return halves(np.concatenate([np.cos(turn), -np.sin(turn)], axis=1) / LENGTH)

    split_high, split_low = first(split)
    nat_high, nat_low = first(natural)
    first_split = np.concatenate([split_high, split_low], axis=1)
    first_nat = np.concatenate([nat_high, nat_low, nat_high, nat_low], axis=1)
    inv_split_high, inv_split_low = last(split)
    inv_nat_high, inv_nat_low = last(natural)
    last_split = np.concatenate([inv_split_high, inv_split_high, inv_split_low], axis=1)
    last_nat = np.concatenate([inv_nat_high, inv_nat_high, inv_nat_low], axis=1)
    twist = 2.0 * math.pi / (2 * LENGTH) * np.outer(half, np.arange(LANES))
    twist = np.stack([np.cos(twist), -np.sin(twist)]).astype(np.float32)
    grid = 2.0 * math.pi / LANES * np.outer(np.arange(LANES), np.arange(LANES))
    cos, sin = np.cos(grid), np.sin(grid)

    def stacked(table):
        high, low = halves(table)
        return np.concatenate([high, high, low], axis=0)

    forward = np.block([[cos, -sin], [sin, cos]])
    mirror = np.block([[cos, sin], [sin, -cos]])
    inverse = np.block([[cos, sin], [-sin, cos]])
    pair = np.concatenate([stacked(forward), stacked(mirror)], axis=0)
    both = np.concatenate([stacked(inverse), stacked(np.block([[cos, sin], [sin, -cos]]))], axis=1)
    return {
        "first_split": first_split, "first_nat": first_nat, "twist": twist, "forward": stacked(forward), "pair": pair,
        "inverse": stacked(inverse), "both": both, "last_split": last_split, "last_nat": last_nat,
    }


def cut(value):
    high = value.astype(jnp.bfloat16)
    low = (value - high.astype(jnp.float32)).astype(jnp.bfloat16)
    return high, low


def store_parts(ref, row, col, real, imag):
    real_high, real_low = cut(real)
    imag_high, imag_low = cut(imag)
    parts = (real_high, imag_high, real_low, imag_low, real_high, imag_high)
    for at, part in enumerate(parts):
        ref[row:row + ROWS, col + at * LANES:col + (at + 1) * LANES] = part


def shifted(early, late, step):
    if step == 0:
        return early, late
    lane = lax.broadcasted_iota(jnp.int32, early.shape, 1)
    row = lax.broadcasted_iota(jnp.int32, early.shape, 0)
    count = early.shape[0]
    turned_early = pltpu.roll(early, (-step) % LANES, 1)
    turned_late = pltpu.roll(late, (-step) % LANES, 1)
    if step > 0:
        keep = lane < LANES - step
        beyond = jnp.where(row == count - 1, 0.0, pltpu.roll(turned_early, count - 1, 0))
        return jnp.where(keep, turned_early, turned_late), jnp.where(keep, turned_late, beyond)
    keep = lane >= -step
    before = jnp.where(row == 0, 0.0, pltpu.roll(turned_late, 1, 0))
    return jnp.where(keep, turned_early, before), jnp.where(keep, turned_late, turned_early)


def dot(left, right):
    return jnp.dot(left, right, preferred_element_type=jnp.float32)


Y_OF = ((1, 2), (0, 3))
QUADS = [[(x * 4 + Y_OF[odd][pair]) * 2 + z for pair in range(2) for z in range(2)] for x in range(4) for odd in range(2)]
LEAGUES = [[quad[2 * pair + z] for quad in QUADS for z in range(2)] for pair in range(2)]
PLANES = [[2 * j + z for j in range(16)] for z in range(2)]
MATE = 6


def twisted(array, col, twist_ref):
    real = array[:ROWS, col * LANES:(col + 1) * LANES]
    imag = array[ROWS:, col * LANES:(col + 1) * LANES]
    return real * twist_ref[0] - imag * twist_ref[1], real * twist_ref[1] + imag * twist_ref[0]


def untwisted(array, twist_ref):
    real, imag = array[:, :LANES], array[:, LANES:]
    return jnp.concatenate(
        [real * twist_ref[0] + imag * twist_ref[1], imag * twist_ref[0] - real * twist_ref[1]], axis=0)


def finish(table_ref, one, two):
    high, low = cut(jnp.concatenate([one, two], axis=1))
    return dot(table_ref[...], jnp.concatenate([high, low, high], axis=0))


def spectra_kernel(filters_ref, first_nat_ref, twist_ref, pair_ref, out_ref, kernel_buf):
    for q in range(BATCH):
        at = (pl.program_id(0) % (8 // BATCH)) * BATCH + q
        plus = filters_ref[0, 0, pl.ds(at, ROWS, stride=8), :]
        minus = filters_ref[1, 0, pl.ds(at, ROWS, stride=8), :]
        high, low = cut(jnp.concatenate([plus, minus], axis=1))
        section = dot(first_nat_ref[...], jnp.concatenate([high, high, low, low], axis=0))
        store_parts(kernel_buf, q * ROWS, 0, *twisted(section, 0, twist_ref))
        store_parts(kernel_buf, q * ROWS, 6 * LANES, *twisted(section, 1, twist_ref))
    out_ref[...] = dot(kernel_buf[...], pair_ref[...])


def lag_kernel(lag_ref, twist_ref, both_ref, last_nat_ref, out_ref):
    parts = lag_ref[...]
    unmixed = dot(jnp.concatenate([parts, parts[:, :2 * LANES]], axis=1), both_ref[...])
    for q in range(BATCH):
        at = (pl.program_id(0) % (8 // BATCH)) * BATCH + q
        rows = slice(q * ROWS, (q + 1) * ROWS)
        pair = finish(last_nat_ref, untwisted(unmixed[rows, :2 * LANES], twist_ref),
                      untwisted(unmixed[rows, 2 * LANES:], twist_ref))
        out_ref[0, 0, pl.ds(at, ROWS, stride=8), :] = pair[:, :LANES]
        out_ref[1, 0, pl.ds(at, ROWS, stride=8), :] = pair[:, LANES:]


def mixer_kernel(
    taps_ref, arrived_ref, spectra_ref, first_split_ref, twist_ref, forward_ref, inverse_ref, last_split_ref,
    back_ref, lag_ref,
    values_buf, slopes_buf, back_buf, mixed_buf, taps_buf, extra_buf, signal_buf, product_buf,
):
    blocks, width = arrived_ref.shape[0], arrived_ref.shape[1] // 2
    step = pl.program_id(0)

    @pl.when(step == 0)
    def _():
        for h in range(2):
            part = slice(h * LANES, (h + 1) * LANES)
            values_buf[h] = arrived_ref[:, :width, part].astype(jnp.float32).reshape(blocks * width, LANES)
            slopes_buf[h] = arrived_ref[:, width:, part].astype(jnp.float32).reshape(blocks * width, LANES)

    pooled = {}

    def start(g):
        for q in range(g * GROUP, (g + 1) * GROUP):
            c = step * GROUP * GROUPS + q
            early = values_buf[0, pl.ds(c, blocks, stride=width), :]
            late = values_buf[1, pl.ds(c, blocks, stride=width), :]
            sum_early, sum_late = None, None
            for k in range(TAPS):
                one, two = shifted(early, late, k - REACH)
                tap = taps_ref[k, c]
                sum_early = tap * one if k == 0 else sum_early + tap * one
                sum_late = tap * two if k == 0 else sum_late + tap * two
            short = jnp.concatenate([sum_early, sum_late], axis=0).astype(jnp.bfloat16)
            conv = short.astype(jnp.float32)
            slope = jnp.concatenate(
                [slopes_buf[h, pl.ds(c, blocks, stride=width), :] for h in range(2)], axis=0)
            sig = jax.nn.sigmoid(conv)
            pooled[q] = jnp.sum(conv * sig, keepdims=True) / LENGTH
            mean_grad = jnp.sum(slope, keepdims=True) / LENGTH
            extra_buf[q] = mean_grad * (sig * (1.0 + conv * (1.0 - sig)))
            both = jnp.concatenate([short, slope.astype(jnp.bfloat16)], axis=1)
            section = dot(first_split_ref[...], jnp.concatenate([both, both], axis=0))
            store_parts(signal_buf, 2 * q * ROWS, 0, *twisted(section, 0, twist_ref))
            store_parts(signal_buf, (2 * q + 1) * ROWS, 0, *twisted(section, 1, twist_ref))

    def multiply(g):
        base = 2 * g * GROUP * ROWS
        spec = dot(signal_buf[base:base + 2 * GROUP * ROWS], forward_ref[...])
        for q in range(GROUP):
            short, slope = spec[2 * q * ROWS:(2 * q + 1) * ROWS], spec[(2 * q + 1) * ROWS:(2 * q + 2) * ROWS]
            rows = slice((g * GROUP + q) * ROWS, (g * GROUP + q + 1) * ROWS)
            short_re, short_im = short[:, :LANES], short[:, LANES:]
            slope_re, slope_im = slope[:, :LANES], slope[:, LANES:]
            filt_re, filt_im = spectra_ref[rows, :LANES], spectra_ref[rows, LANES:]
            store_parts(product_buf, base + 2 * q * ROWS, 0,
                        short_re * filt_re - short_im * filt_im, short_re * filt_im + short_im * filt_re)
            store_parts(product_buf, base + (2 * q + 1) * ROWS, 0,
                        slope_re * filt_re + slope_im * filt_im, slope_im * filt_re - slope_re * filt_im)
            real_high, real_low = cut(slope_re * short_re + slope_im * short_im)
            imag_high, imag_low = cut(slope_im * short_re - slope_re * short_im)
            for at, part in enumerate((real_high, imag_high, real_low, imag_low)):
                lag_ref[rows, at * LANES:(at + 1) * LANES] = part

    def end(g):
        base = 2 * g * GROUP * ROWS
        unmixed = dot(product_buf[base:base + 2 * GROUP * ROWS], inverse_ref[...])
        for q in range(GROUP):
            c = step * GROUP * GROUPS + g * GROUP + q
            rows = 2 * q * ROWS
            long_pair = finish(last_split_ref, untwisted(unmixed[rows:rows + ROWS], twist_ref),
                               untwisted(unmixed[rows + ROWS:rows + 2 * ROWS], twist_ref))
            mixed = long_pair[:, :LANES] + pooled[g * GROUP + q]
            slope_back = long_pair[:, LANES:] + extra_buf[g * GROUP + q]
            slope_back = slope_back.astype(jnp.bfloat16).astype(jnp.float32)
            early = values_buf[0, pl.ds(c, blocks, stride=width), :]
            late = values_buf[1, pl.ds(c, blocks, stride=width), :]
            sum_early, sum_late = None, None
            for k in range(TAPS):
                one, two = shifted(slope_back[:blocks], slope_back[blocks:], REACH - k)
                tap = taps_ref[k, c]
                sum_early = tap * one if k == 0 else sum_early + tap * one
                sum_late = tap * two if k == 0 else sum_late + tap * two
                taps_buf[k, pl.ds(c, 1), :] = jnp.sum(one * early + two * late, axis=0, keepdims=True)
            for h, part in enumerate((sum_early, sum_late)):
                back_buf[h, pl.ds(c, blocks, stride=width), :] = part
                mixed_buf[h, pl.ds(c, blocks, stride=width), :] = mixed[h * blocks:(h + 1) * blocks]

    for turn in range(GROUPS + 2):
        if turn >= 2:
            end(turn - 2)
        if 1 <= turn <= GROUPS:
            multiply(turn - 1)
        if turn < GROUPS:
            start(turn)

    @pl.when(step == pl.num_programs(0) - 1)
    def _():
        for q, quad in enumerate(QUADS):
            for place, s in enumerate(quad):
                rows = slice(s * width, (s + 1) * width)
                for h in range(2):
                    part = back_buf[h, rows, :].astype(jnp.bfloat16)
                    lanes = slice((2 * place + h) * LANES, (2 * place + h + 1) * LANES)
                    back_ref[2 * q, :, lanes] = part
                    back_ref[2 * q + 1, :, lanes] = part
                    at = 8 + 2 * (place // 2) + h
                    back_ref[2 * q + place % 2, :, at * LANES:(at + 1) * LANES] = (
                        mixed_buf[h, rows, :].astype(jnp.bfloat16))
        lane = lax.broadcasted_iota(jnp.int32, (width, LANES), 1)
        packed = jnp.zeros((width, LANES), jnp.float32)
        for k in range(TAPS):
            rest = jnp.sum(taps_buf[k], axis=1, keepdims=True)
            for p in range(3):
                piece = rest.astype(jnp.bfloat16).astype(jnp.float32)
                packed = jnp.where(lane == 8 * p + k, piece, packed)
                rest = rest - piece
        for d in range(blocks // 2):
            back_ref[d, :, 12 * LANES:] = packed.astype(jnp.bfloat16)


def whole(shape):
    return pl.BlockSpec(shape, lambda *_: (0,) * len(shape))


def call(kernel, name, flops, nbytes, vmem=16, **kwargs):
    return pl.pallas_call(
        kernel, name=name,
        compiler_params=pltpu.CompilerParams(vmem_limit_bytes=vmem * 1024 * 1024),
        cost_estimate=pl.CostEstimate(flops=flops, bytes_accessed=nbytes, transcendentals=0), **kwargs)


def tables_of(names, blocks=LENGTH // 256):
    chosen = [jnp.asarray(tables(blocks)[name]) for name in names]
    return chosen, [whole(table.shape) for table in chosen]


PER_TILE = pl.BlockSpec((2, 1, ROWS * 8, LANES), lambda i: (0, i // (8 // BATCH), 0, 0))


def spectra_of(filters):
    width = filters.shape[1]
    tiles = width // 8
    view = filters.reshape(2, tiles, 8, ROWS, LANES).transpose(0, 1, 3, 2, 4).reshape(2, tiles, ROWS * 8, LANES)
    consts, specs = tables_of(("first_nat", "twist", "pair"))
    return call(
        spectra_kernel, "spectra", 3_000_000_000, 5_000_000, vmem=56,
        grid=(width // BATCH,), in_specs=[PER_TILE] + specs,
        out_specs=pl.BlockSpec((BATCH * ROWS, 2 * LANES), lambda i: (i, 0)),
        out_shape=jax.ShapeDtypeStruct((width * ROWS, 2 * LANES), jnp.float32),
        scratch_shapes=[pltpu.VMEM((BATCH * ROWS, 12 * LANES), jnp.bfloat16)],
    )(view, *consts)


def filter_grads(lag):
    width = lag.shape[0] // ROWS
    tiles = width // 8
    consts, specs = tables_of(("twist", "both", "last_nat"))
    out = call(
        lag_kernel, "filter_grads", 3_000_000_000, 5_000_000,
        grid=(width // BATCH,),
        in_specs=[pl.BlockSpec((BATCH * ROWS, 4 * LANES), lambda i: (i, 0))] + specs,
        out_specs=PER_TILE,
        out_shape=jax.ShapeDtypeStruct((2, tiles, ROWS * 8, LANES), jnp.float32),
    )(lag, *consts)
    return out.reshape(2, tiles, ROWS, 8, LANES).transpose(0, 1, 3, 2, 4).reshape(2, width, LENGTH)


def mixer(own_taps, arrived, spectra):
    blocks, width, span = arrived.shape[0], arrived.shape[1] // 2, arrived.shape[2]
    consts, specs = tables_of(("first_split", "twist", "forward", "inverse", "last_split"))
    back_shape = (blocks // 2, width, 6 * span + LANES)
    rows, batch = (2, blocks * width, LANES), GROUP * GROUPS
    return call(
        mixer_kernel, "mixer", 100_000_000, 1_000_000, vmem=56,
        grid=(width // batch,),
        in_specs=[pl.BlockSpec(memory_space=pltpu.SMEM), whole(arrived.shape),
                  pl.BlockSpec((batch * ROWS, 2 * LANES), lambda i: (i, 0))] + specs,
        out_specs=[whole(back_shape), pl.BlockSpec((batch * ROWS, 4 * LANES), lambda i: (i, 0))],
        out_shape=[
            jax.ShapeDtypeStruct(back_shape, jnp.bfloat16),
            jax.ShapeDtypeStruct((width * ROWS, 4 * LANES), jnp.bfloat16),
        ],
        scratch_shapes=[
            pltpu.VMEM(rows, jnp.float32),
            pltpu.VMEM(rows, jnp.float32),
            pltpu.VMEM(rows, jnp.float32),
            pltpu.VMEM(rows, jnp.float32),
            pltpu.VMEM((TAPS, width, LANES), jnp.float32),
            pltpu.VMEM((batch, ROWS, LANES), jnp.float32),
            pltpu.VMEM((2 * batch * ROWS, 6 * LANES), jnp.bfloat16),
            pltpu.VMEM((2 * batch * ROWS, 6 * LANES), jnp.bfloat16),
        ],
    )(own_taps, arrived, spectra, *consts)


STREAMS = 4


def send_kernel(rows_ref, *refs):
    weight_refs, (gate_ref, grad_ref, out_ref, total_ref) = refs[:STREAMS], refs[STREAMS:]
    blocks, width, span = out_ref.shape[0], out_ref.shape[1] // 2, out_ref.shape[2]
    step, steps = pl.program_id(0), pl.num_programs(0)
    count = blocks * gate_ref.shape[1] // total_ref.shape[1]
    sig = jax.nn.sigmoid(gate_ref[...].astype(jnp.float32))
    slopes = (grad_ref[...].astype(jnp.float32) * sig).T.astype(jnp.bfloat16)
    out_ref[pl.ds(step * count, count), width:, :] = slopes.reshape(count, width, span)
    part = weight_refs[0].shape[0]
    term = dot(rows_ref[:, :part], weight_refs[0][...])
    for j in range(1, STREAMS):
        term = term + dot(rows_ref[:, j * part:(j + 1) * part], weight_refs[j][...])

    @pl.when(step == 0)
    def _():
        total_ref[...] = term

    @pl.when((step > 0) & (step < steps - 1))
    def _():
        total_ref[...] += term

    @pl.when(step == steps - 1)
    def _():
        total = total_ref[...] + term
        out_ref[:, :width, :] = total.T.astype(jnp.bfloat16).reshape(blocks, width, span)


def sends(layer_in, w_value, gate, grads, count, steps=4):
    span, depth = layer_in.shape
    channels = w_value.shape[1]
    width = channels // count
    block = pl.BlockSpec((span, channels // steps), lambda i: (0, i))
    streams = [pl.BlockSpec((depth // (steps * STREAMS), channels), functools.partial(lambda j, i: (STREAMS * i + j, 0), j))
               for j in range(STREAMS)]
    return call(
        send_kernel, "sends", 2 * span * depth * channels, 12_500_000, vmem=56, grid=(steps,),
        in_specs=[pl.BlockSpec((span, depth // steps), lambda i: (0, i))] + streams + [block, block],
        out_specs=whole((count, 2 * width, span)),
        out_shape=jax.ShapeDtypeStruct((count, 2 * width, span), jnp.bfloat16),
        scratch_shapes=[pltpu.VMEM((span, channels), jnp.float32)],
    )(layer_in, *[w_value] * STREAMS, gate, grads)


def quarter_kernel(place_ref, rows_ref, others_ref, same_ref, cross_ref, other_ref):
    z = place_ref[0] % 2
    for y in range(4):
        to = slice(y * LANES, (y + 1) * LANES)
        own = pl.ds(pl.multiple_of((2 * y + z) * LANES, LANES), LANES)
        same_ref[:, to] = rows_ref[:, own]
        other_ref[:, to] = others_ref[:, own]
        cross_ref[:, to] = rows_ref[:, pl.ds(pl.multiple_of((2 * y + 1 - z) * LANES, LANES), LANES)]


def quarters_of(place, layer_in):
    span, depth = layer_in.shape
    quarter = jax.ShapeDtypeStruct((span, depth // 4), jnp.bfloat16)
    return call(
        quarter_kernel, "quarters", 0, 5_000_000,
        grid_spec=pltpu.PrefetchScalarGridSpec(
            num_scalar_prefetch=1, grid=(2,),
            in_specs=[pl.BlockSpec((span, depth // 4), lambda i, place: (0, 2 * (place[1] % 2) + i)),
                      pl.BlockSpec((span, depth // 4), lambda i, place: (0, 2 - 2 * (place[1] % 2) + i))],
            out_specs=[pl.BlockSpec((span, 4 * LANES), lambda i, place: (0, i))] * 3),
        out_shape=[quarter] * 3,
    )(place, layer_in, layer_in)


def quad_place():
    seq_at = lax.axis_index("seq")
    return seq_at // 4 % 2 * 2 + seq_at % 2


def share_kernel(back_ref, *refs):
    parts, (out_ref, back_buf, rows_buf, out_buf, in_sem, out_sem) = refs[:8], refs[8:]
    span = rows_buf.shape[1]
    loads = [pltpu.make_async_copy(back_ref.at[:, pl.ds(0, 4 * span)], back_buf, in_sem.at[8])]
    loads += [pltpu.make_async_copy(part, rows_buf.at[n], in_sem.at[n]) for n, part in enumerate(parts)]
    for load in loads:
        load.start()
    loads[0].wait()
    stores = []
    for half in range(2):
        for load in loads[1 + 4 * half:5 + 4 * half]:
            load.wait()
        first = 8 * (half ^ (lax.axis_index("tp") % 2))
        for two in range(4):
            lanes = slice(two * 256, (two + 1) * 256)
            product = None
            for j in range(4):
                at = pl.multiple_of((quad_place() ^ j) * span, span)
                term = dot(back_buf[:, pl.ds(at, span)], rows_buf[4 * half + j, :, lanes])
                product = term if product is None else product + term
            product = product.astype(jnp.bfloat16)
            n = 4 * half + two
            out_buf[2 * n] = product[:, :LANES]
            out_buf[2 * n + 1] = product[:, LANES:]
            store = pltpu.make_async_copy(
                out_buf.at[pl.ds(2 * n, 2)], out_ref.at[pl.ds(first + 2 * two, 2)], out_sem.at[n])
            store.start()
            stores.append(store)
    for store in stores:
        store.wait()


def shares(back, mine, other):
    span, depth = mine[0].shape
    rows = back.shape[0]
    return call(
        share_kernel, "shares", 16 * rows * span * depth, 7_000_000, vmem=60,
        in_specs=[pl.BlockSpec(memory_space=pl.ANY)] * 9,
        out_specs=pl.BlockSpec(memory_space=pl.ANY),
        out_shape=jax.ShapeDtypeStruct((16, rows, LANES), jnp.bfloat16),
        scratch_shapes=[
            pltpu.VMEM((rows, 4 * span), jnp.bfloat16), pltpu.VMEM((8, span, depth), jnp.bfloat16),
            pltpu.VMEM((16, rows, LANES), jnp.bfloat16),
            pltpu.SemaphoreType.DMA((9,)), pltpu.SemaphoreType.DMA((8,))],
    )(back, *mine, *other)


def merge(pair, mine, mate):
    first, second = jnp.where(pair == 0, mine, mate), jnp.where(pair == 0, mate, mine)
    half = mine.shape[0] // 2
    return jnp.concatenate([first[half:], first[:half], second[:half], second[half:]], axis=0)


def weight_kernel(shares_ref, taps_ref, mate_ref, weight_ref, tap_sums_ref):
    for x in range(4):
        rows, lanes = slice(x * LANES, (x + 1) * LANES), slice(x * 2 * LANES, (x + 1) * 2 * LANES)
        totals = []
        for pair in range(2):
            terms = [shares_ref[j, rows, :].astype(jnp.float32) for j in range(16) if j % 4 // 2 == pair]
            totals.append(sum(terms[1:], terms[0]))
        weight_ref[:, lanes] = merge(0, *totals).T
        packed = merge(quad_place() // 2, taps_ref[rows, :].astype(jnp.float32), mate_ref[rows, :].astype(jnp.float32)).T
        tap_sums_ref[:, lanes] = (packed[16:24] + packed[8:16] + packed[0:8])[:TAPS]


def close_weight(parts, back, mate):
    count, rows, span = parts.shape
    channels = 2 * rows
    return call(
        weight_kernel, "close_weight", 2_000_000, 3_000_000, grid=(1,),
        in_specs=[whole(parts.shape),
                  pl.BlockSpec((rows, LANES), lambda i: (0, 12)), pl.BlockSpec((rows, LANES), lambda i: (0, 4))],
        out_specs=[whole((span, channels)), whole((TAPS, channels))],
        out_shape=[jax.ShapeDtypeStruct((span, channels), jnp.float32),
                   jax.ShapeDtypeStruct((TAPS, channels), jnp.float32)],
    )(parts, back, mate)


def input_kernel(place_ref, back_ref, mate_ref, weight_ref, send_ref, keep_ref, own_buf):
    @pl.when(pl.program_id(0) == 0)
    def _():
        pair = place_ref[0] // 2
        for x in range(4):
            for odd, mine, other in ((0, 1 + pair, 2 - pair), (1, 3 * pair, 3 - 3 * pair)):
                rows = slice((2 * x + odd) * 64, (2 * x + odd + 1) * 64)
                own_buf[pl.ds(pl.multiple_of((4 * x + mine) * 64, 64), 64), :] = back_ref[rows, :]
                own_buf[pl.ds(pl.multiple_of((4 * x + other) * 64, 64), 64), :] = mate_ref[rows, :]

    term = dot(weight_ref[...], own_buf[...])

    @pl.when(pl.program_id(0) < 2)
    def _():
        send_ref[0] = term.astype(jnp.bfloat16)

    @pl.when(pl.program_id(0) >= 2)
    def _():
        keep_ref[0] = term


def input_terms(place, back, mate, w_value):
    depth, channels = w_value.shape
    rows, span = depth // 4, 256
    return call(
        input_kernel, "input_terms", 2 * span * depth * channels, 12_000_000, vmem=24,
        grid_spec=pltpu.PrefetchScalarGridSpec(
            num_scalar_prefetch=1, grid=(4,),
            in_specs=[pl.BlockSpec((channels // 2, span), lambda i, place: (0, place[0])),
                      pl.BlockSpec((channels // 2, span), lambda i, place: (0, 0)),
                      pl.BlockSpec((rows, channels), lambda i, place: (place[1] ^ ((2 * i + 1 - i // 2) % 4), 0))],
            out_specs=[pl.BlockSpec((1, rows, span), lambda i, place: (jnp.minimum(i, 1), 0, 0)),
                       pl.BlockSpec((1, rows, span), lambda i, place: (jnp.maximum(i - 2, 0), 0, 0))],
            scratch_shapes=[pltpu.VMEM((channels, span), jnp.bfloat16)]),
        out_shape=[jax.ShapeDtypeStruct((2, rows, span), jnp.bfloat16),
                   jax.ShapeDtypeStruct((2, rows, span), jnp.float32)],
    )(place, back, mate, w_value)


def close_kernel(keep_ref, core_ref, chip_ref, out_ref):
    total = keep_ref[0] + core_ref[0].astype(jnp.float32) + chip_ref[...].astype(jnp.float32)
    out_ref[...] = total.T.astype(jnp.bfloat16)


def close_input(keep, core, chip):
    rows, span = chip.shape
    first = pl.BlockSpec((1, 512, span), lambda i: (0, i, 0))
    return call(
        close_kernel, "close_input", 1_000_000, 3_000_000, grid=(rows // 512,),
        in_specs=[first, first, pl.BlockSpec((512, span), lambda i: (i, 0))],
        out_specs=pl.BlockSpec((span, 512), lambda i: (0, i)),
        out_shape=jax.ShapeDtypeStruct((span, rows), jnp.bfloat16))(keep, core, chip)


def gate_kernel(place_ref, mixed_ref, mate_ref, gate_ref, grad_ref, out_ref):
    mixed = merge(place_ref[0] // 2, mixed_ref[...].astype(jnp.float32), mate_ref[...].astype(jnp.float32)).T
    sig = jax.nn.sigmoid(gate_ref[...].astype(jnp.float32))
    out_ref[...] = (grad_ref[...].astype(jnp.float32) * mixed * sig * (1.0 - sig)).astype(jnp.bfloat16)


def gate_grad(place, back, mate, gate, grads):
    span, channels = gate.shape
    block = pl.BlockSpec((span, channels // 4), lambda i, place: (0, i))
    return call(
        gate_kernel, "gate_grad", 2_000_000, 2_500_000,
        grid_spec=pltpu.PrefetchScalarGridSpec(
            num_scalar_prefetch=1, grid=(4,),
            in_specs=[pl.BlockSpec((LANES, span), lambda i, place: (i, 4 + place[0] // 2)),
                      pl.BlockSpec((LANES, span), lambda i, place: (i, 1)), block, block],
            out_specs=block),
        out_shape=jax.ShapeDtypeStruct(gate.shape, jnp.bfloat16))(place, back, mate, gate, grads)


def local(layer_in, w_value, short_taps, long_filters, gate_proj, grad_out):
    seq_count = lax.axis_size("seq")
    seq_at, tp_at = lax.axis_index("seq"), lax.axis_index("tp")
    span, depth = layer_in.shape
    channels = w_value.shape[1]
    width = channels // seq_count
    quad_at = quad_place()
    place = jnp.stack([quad_at, tp_at]).astype(jnp.int32)
    cores, chips = [(0, 1), (1, 0), (2, 3), (3, 2)], [(0, 2), (2, 0), (1, 3), (3, 1)]

    def exchange(value, index_groups=None):
        return lax.all_to_all(
            value, "seq", split_axis=0, concat_axis=0, axis_index_groups=index_groups, tiled=True)

    def mates(value):
        return lax.ppermute(value, "seq", [(s, s ^ MATE) for s in range(seq_count)])

    outgoing = sends(layer_in, w_value, gate_proj, grad_out, seq_count)
    rows_in, outgoing = lax.optimization_barrier((layer_in, outgoing))
    arrived = exchange(outgoing)
    same, cross, other = quarters_of(place, rows_in)

    def across(value, flip):
        return lax.ppermute(
            value, ("seq", "tp"), [(4 * s + t, 4 * (s ^ flip) + (t ^ 2)) for s in range(seq_count) for t in range(4)])

    first = across(cross, 1)
    spectra = spectra_of(long_filters)
    same, cross, spectra = lax.optimization_barrier((same, cross, spectra))
    mine = [same, first, mates(same), across(cross, 1 ^ MATE)]

    own_taps = lax.dynamic_slice_in_dim(short_taps, seq_at * width, width, 1)
    back, lag = mixer(own_taps, arrived, spectra)
    back, mine = lax.optimization_barrier((back, mine))
    other = [other] + [lax.ppermute(part, "tp", cores) for part in mine[1:]]
    back = exchange(back, LEAGUES).reshape(channels // 2, back.shape[2])
    grad_filters = filter_grads(lag)
    back, grad_filters, other = lax.optimization_barrier((back, grad_filters, other))
    mate = mates(jnp.concatenate([
        lax.dynamic_slice_in_dim(back, (quad_at ^ 2) * span, span, 1),
        lax.dynamic_slice_in_dim(back, 4 * span + (1 - quad_at // 2) * span, span, 1),
        back[:, 6 * span:]], axis=1))
    outgoing, mate = lax.optimization_barrier((shares(back, mine, other), mate))
    parts = exchange(outgoing, PLANES)

    send, keep = input_terms(place, back, mate, w_value)
    core = lax.ppermute(send, "tp", cores)
    send = (keep[1] + core[1].astype(jnp.float32)).astype(jnp.bfloat16)
    chip = lax.ppermute(send, "tp", chips)
    grad_input = close_input(keep, core, chip)
    grad_gate = gate_grad(place, back, mate, gate_proj, grad_out)
    parts, grad_input, grad_gate = lax.optimization_barrier((parts, grad_input, grad_gate))
    grad_weight, grad_taps = close_weight(parts, back, mate)
    return (grad_input, grad_weight, grad_taps, grad_filters, grad_gate)


def solution(mesh):
    in_specs = (
        P("seq", None),
        P(None, "tp"),
        P(None, "tp"),
        P(None, ("tp", "seq"), None),
        P("seq", "tp"),
        P("seq", "tp"),
    )
    out_specs = (
        P("seq", "tp"),
        P("seq", "tp"),
        P(None, "tp"),
        P(None, ("tp", "seq"), None),
        P("seq", "tp"),
    )
    return jax.shard_map(local, mesh=mesh, in_specs=in_specs, out_specs=out_specs, check_vma=False)
```

```python
import functools
import math

import jax
import jax.numpy as jnp
import ml_dtypes
import numpy as np
from jax import lax
from jax.experimental import pallas as pl
from jax.experimental.pallas import tpu as pltpu
from jax.sharding import PartitionSpec as P

LANES = 128
ROWS = 64
LENGTH = ROWS * LANES
TAPS = 7
REACH = TAPS // 2
BATCH = 4
GROUP, GROUPS = 2, 8


def halves(table):
    high = table.astype(ml_dtypes.bfloat16)
    low = (table - high.astype(np.float64)).astype(ml_dtypes.bfloat16)
    return high, low


@functools.lru_cache(maxsize=None)
def tables(blocks):
    half = np.arange(ROWS) + 0.5
    natural = np.arange(ROWS)
    split = (2 * np.arange(blocks)[None, :] + np.arange(2)[:, None]).reshape(-1)

    def first(order):
        turn = 2.0 * math.pi / LANES * np.outer(half, order)
        return halves(np.concatenate([np.cos(turn), -np.sin(turn)], axis=0))

    def last(order):
        turn = 2.0 * math.pi / LANES * np.outer(order, half)
        return halves(np.concatenate([np.cos(turn), -np.sin(turn)], axis=1) / LENGTH)

    split_high, split_low = first(split)
    nat_high, nat_low = first(natural)
    first_split = np.concatenate([split_high, split_low], axis=1)
    first_nat = np.concatenate([nat_high, nat_low, nat_high, nat_low], axis=1)
    inv_split_high, inv_split_low = last(split)
    inv_nat_high, inv_nat_low = last(natural)
    last_split = np.concatenate([inv_split_high, inv_split_high, inv_split_low], axis=1)
    last_nat = np.concatenate([inv_nat_high, inv_nat_high, inv_nat_low], axis=1)
    twist = 2.0 * math.pi / (2 * LENGTH) * np.outer(half, np.arange(LANES))
    twist = np.stack([np.cos(twist), -np.sin(twist)]).astype(np.float32)
    grid = 2.0 * math.pi / LANES * np.outer(np.arange(LANES), np.arange(LANES))
    cos, sin = np.cos(grid), np.sin(grid)

    def stacked(table):
        high, low = halves(table)
        return np.concatenate([high, high, low], axis=0)

    forward = np.block([[cos, -sin], [sin, cos]])
    mirror = np.block([[cos, sin], [sin, -cos]])
    inverse = np.block([[cos, sin], [-sin, cos]])
    pair = np.concatenate([stacked(forward), stacked(mirror)], axis=0)
    both = np.concatenate([stacked(inverse), stacked(np.block([[cos, sin], [sin, -cos]]))], axis=1)
    return {
        "first_split": first_split, "first_nat": first_nat, "twist": twist, "forward": stacked(forward), "pair": pair,
        "inverse": stacked(inverse), "both": both, "last_split": last_split, "last_nat": last_nat,
    }


def cut(value):
    high = value.astype(jnp.bfloat16)
    low = (value - high.astype(jnp.float32)).astype(jnp.bfloat16)
    return high, low


def store_parts(ref, row, col, real, imag):
    real_high, real_low = cut(real)
    imag_high, imag_low = cut(imag)
    parts = (real_high, imag_high, real_low, imag_low, real_high, imag_high)
    for at, part in enumerate(parts):
        ref[row:row + ROWS, col + at * LANES:col + (at + 1) * LANES] = part


def shifted(early, late, step):
    if step == 0:
        return early, late
    lane = lax.broadcasted_iota(jnp.int32, early.shape, 1)
    row = lax.broadcasted_iota(jnp.int32, early.shape, 0)
    count = early.shape[0]
    turned_early = pltpu.roll(early, (-step) % LANES, 1)
    turned_late = pltpu.roll(late, (-step) % LANES, 1)
    if step > 0:
        keep = lane < LANES - step
        beyond = jnp.where(row == count - 1, 0.0, pltpu.roll(turned_early, count - 1, 0))
        return jnp.where(keep, turned_early, turned_late), jnp.where(keep, turned_late, beyond)
    keep = lane >= -step
    before = jnp.where(row == 0, 0.0, pltpu.roll(turned_late, 1, 0))
    return jnp.where(keep, turned_early, before), jnp.where(keep, turned_late, turned_early)


def dot(left, right):
    return jnp.dot(left, right, preferred_element_type=jnp.float32)


Y_OF = ((1, 2), (0, 3))
QUADS = [[(x * 4 + Y_OF[odd][pair]) * 2 + z for pair in range(2) for z in range(2)] for x in range(4) for odd in range(2)]
LEAGUES = [[quad[2 * pair + z] for quad in QUADS for z in range(2)] for pair in range(2)]
PLANES = [[2 * j + z for j in range(16)] for z in range(2)]
MATE = 6


def twisted(array, col, twist_ref):
    real = array[:ROWS, col * LANES:(col + 1) * LANES]
    imag = array[ROWS:, col * LANES:(col + 1) * LANES]
    return real * twist_ref[0] - imag * twist_ref[1], real * twist_ref[1] + imag * twist_ref[0]


def untwisted(array, twist_ref):
    real, imag = array[:, :LANES], array[:, LANES:]
    return jnp.concatenate(
        [real * twist_ref[0] + imag * twist_ref[1], imag * twist_ref[0] - real * twist_ref[1]], axis=0)


def finish(table_ref, one, two):
    high, low = cut(jnp.concatenate([one, two], axis=1))
    return dot(table_ref[...], jnp.concatenate([high, low, high], axis=0))


def spectra_kernel(filters_ref, first_nat_ref, twist_ref, pair_ref, out_ref, kernel_buf):
    for q in range(BATCH):
        at = (pl.program_id(0) % (8 // BATCH)) * BATCH + q
        plus = filters_ref[0, 0, pl.ds(at, ROWS, stride=8), :]
        minus = filters_ref[1, 0, pl.ds(at, ROWS, stride=8), :]
        high, low = cut(jnp.concatenate([plus, minus], axis=1))
        section = dot(first_nat_ref[...], jnp.concatenate([high, high, low, low], axis=0))
        store_parts(kernel_buf, q * ROWS, 0, *twisted(section, 0, twist_ref))
        store_parts(kernel_buf, q * ROWS, 6 * LANES, *twisted(section, 1, twist_ref))
    out_ref[...] = dot(kernel_buf[...], pair_ref[...])


def lag_kernel(lag_ref, twist_ref, both_ref, last_nat_ref, out_ref):
    parts = lag_ref[...]
    unmixed = dot(jnp.concatenate([parts, parts[:, :2 * LANES]], axis=1), both_ref[...])
    for q in range(BATCH):
        at = (pl.program_id(0) % (8 // BATCH)) * BATCH + q
        rows = slice(q * ROWS, (q + 1) * ROWS)
        pair = finish(last_nat_ref, untwisted(unmixed[rows, :2 * LANES], twist_ref),
                      untwisted(unmixed[rows, 2 * LANES:], twist_ref))
        out_ref[0, 0, pl.ds(at, ROWS, stride=8), :] = pair[:, :LANES]
        out_ref[1, 0, pl.ds(at, ROWS, stride=8), :] = pair[:, LANES:]


def mixer_kernel(
    taps_ref, arrived_ref, spectra_ref, first_split_ref, twist_ref, forward_ref, inverse_ref, last_split_ref,
    back_ref, lag_ref, taps_out_ref,
    values_buf, slopes_buf, back_buf, mixed_buf, taps_buf, extra_buf, signal_buf, product_buf,
):
    blocks, width = arrived_ref.shape[0], arrived_ref.shape[1] // 2
    step = pl.program_id(0)

    @pl.when(step == 0)
    def _():
        for h in range(2):
            part = slice(h * LANES, (h + 1) * LANES)
            values_buf[h] = arrived_ref[:, :width, part].astype(jnp.float32).reshape(blocks * width, LANES)
            slopes_buf[h] = arrived_ref[:, width:, part].astype(jnp.float32).reshape(blocks * width, LANES)

    pooled = {}

    def start(g):
        for q in range(g * GROUP, (g + 1) * GROUP):
            c = step * GROUP * GROUPS + q
            early = values_buf[0, pl.ds(c, blocks, stride=width), :]
            late = values_buf[1, pl.ds(c, blocks, stride=width), :]
            sum_early, sum_late = None, None
            for k in range(TAPS):
                one, two = shifted(early, late, k - REACH)
                tap = taps_ref[k, c]
                sum_early = tap * one if k == 0 else sum_early + tap * one
                sum_late = tap * two if k == 0 else sum_late + tap * two
            short = jnp.concatenate([sum_early, sum_late], axis=0).astype(jnp.bfloat16)
            conv = short.astype(jnp.float32)
            slope = jnp.concatenate(
                [slopes_buf[h, pl.ds(c, blocks, stride=width), :] for h in range(2)], axis=0)
            sig = jax.nn.sigmoid(conv)
            pooled[q] = jnp.sum(conv * sig, keepdims=True) / LENGTH
            mean_grad = jnp.sum(slope, keepdims=True) / LENGTH
            extra_buf[q] = mean_grad * (sig * (1.0 + conv * (1.0 - sig)))
            both = jnp.concatenate([short, slope.astype(jnp.bfloat16)], axis=1)
            section = dot(first_split_ref[...], jnp.concatenate([both, both], axis=0))
            store_parts(signal_buf, 2 * q * ROWS, 0, *twisted(section, 0, twist_ref))
            store_parts(signal_buf, (2 * q + 1) * ROWS, 0, *twisted(section, 1, twist_ref))

    def multiply(g):
        base = 2 * g * GROUP * ROWS
        spec = dot(signal_buf[base:base + 2 * GROUP * ROWS], forward_ref[...])
        for q in range(GROUP):
            short, slope = spec[2 * q * ROWS:(2 * q + 1) * ROWS], spec[(2 * q + 1) * ROWS:(2 * q + 2) * ROWS]
            rows = slice((g * GROUP + q) * ROWS, (g * GROUP + q + 1) * ROWS)
            short_re, short_im = short[:, :LANES], short[:, LANES:]
            slope_re, slope_im = slope[:, :LANES], slope[:, LANES:]
            filt_re, filt_im = spectra_ref[rows, :LANES], spectra_ref[rows, LANES:]
            store_parts(product_buf, base + 2 * q * ROWS, 0,
                        short_re * filt_re - short_im * filt_im, short_re * filt_im + short_im * filt_re)
            store_parts(product_buf, base + (2 * q + 1) * ROWS, 0,
                        slope_re * filt_re + slope_im * filt_im, slope_im * filt_re - slope_re * filt_im)
            real_high, real_low = cut(slope_re * short_re + slope_im * short_im)
            imag_high, imag_low = cut(slope_im * short_re - slope_re * short_im)
            for at, part in enumerate((real_high, imag_high, real_low, imag_low)):
                lag_ref[rows, at * LANES:(at + 1) * LANES] = part

    def end(g):
        base = 2 * g * GROUP * ROWS
        unmixed = dot(product_buf[base:base + 2 * GROUP * ROWS], inverse_ref[...])
        for q in range(GROUP):
            c = step * GROUP * GROUPS + g * GROUP + q
            rows = 2 * q * ROWS
            long_pair = finish(last_split_ref, untwisted(unmixed[rows:rows + ROWS], twist_ref),
                               untwisted(unmixed[rows + ROWS:rows + 2 * ROWS], twist_ref))
            mixed = long_pair[:, :LANES] + pooled[g * GROUP + q]
            slope_back = long_pair[:, LANES:] + extra_buf[g * GROUP + q]
            slope_back = slope_back.astype(jnp.bfloat16).astype(jnp.float32)
            early = values_buf[0, pl.ds(c, blocks, stride=width), :]
            late = values_buf[1, pl.ds(c, blocks, stride=width), :]
            sum_early, sum_late = None, None
            for k in range(TAPS):
                one, two = shifted(slope_back[:blocks], slope_back[blocks:], REACH - k)
                tap = taps_ref[k, c]
                sum_early = tap * one if k == 0 else sum_early + tap * one
                sum_late = tap * two if k == 0 else sum_late + tap * two
                taps_buf[k, pl.ds(c, 1), :] = jnp.sum(one * early + two * late, axis=0, keepdims=True)
            for h, part in enumerate((sum_early, sum_late)):
                back_buf[h, pl.ds(c, blocks, stride=width), :] = part
                mixed_buf[h, pl.ds(c, blocks, stride=width), :] = mixed[h * blocks:(h + 1) * blocks]

    for turn in range(GROUPS + 2):
        if turn >= 2:
            end(turn - 2)
        if 1 <= turn <= GROUPS:
            multiply(turn - 1)
        if turn < GROUPS:
            start(turn)

    @pl.when(step == pl.num_programs(0) - 1)
    def _():
        for q, quad in enumerate(QUADS):
            for place, s in enumerate(quad):
                rows = slice(s * width, (s + 1) * width)
                for h in range(2):
                    part = back_buf[h, rows, :].astype(jnp.bfloat16)
                    lanes = slice((2 * place + h) * LANES, (2 * place + h + 1) * LANES)
                    back_ref[2 * q, :, lanes] = part
                    back_ref[2 * q + 1, :, lanes] = part
                    at = 8 + 2 * (place // 2) + h
                    back_ref[2 * q + place % 2, :, at * LANES:(at + 1) * LANES] = (
                        mixed_buf[h, rows, :].astype(jnp.bfloat16))
        lane = lax.broadcasted_iota(jnp.int32, (width, LANES), 1)
        packed = jnp.zeros((width, LANES), jnp.float32)
        for k in range(TAPS):
            rest = jnp.sum(taps_buf[k], axis=1, keepdims=True)
            for p in range(3):
                piece = rest.astype(jnp.bfloat16).astype(jnp.float32)
                packed = jnp.where(lane == 8 * p + k, piece, packed)
                rest = rest - piece
        packed = jnp.concatenate([packed, jnp.zeros((LANES - width, LANES), jnp.float32)], axis=0).T
        rows = packed[:8] + pltpu.roll(packed[8:16], width, 1) + pltpu.roll(packed[16:24], 2 * width, 1)
        taps_out_ref[...] = jnp.concatenate([rows, jnp.zeros_like(rows)], axis=0).astype(jnp.bfloat16)


def whole(shape):
    return pl.BlockSpec(shape, lambda *_: (0,) * len(shape))


def call(kernel, name, flops, nbytes, vmem=16, **kwargs):
    return pl.pallas_call(
        kernel, name=name,
        compiler_params=pltpu.CompilerParams(vmem_limit_bytes=vmem * 1024 * 1024),
        cost_estimate=pl.CostEstimate(flops=flops, bytes_accessed=nbytes, transcendentals=0), **kwargs)


def tables_of(names, blocks=LENGTH // 256):
    chosen = [jnp.asarray(tables(blocks)[name]) for name in names]
    return chosen, [whole(table.shape) for table in chosen]


PER_TILE = pl.BlockSpec((2, 1, ROWS * 8, LANES), lambda i: (0, i // (8 // BATCH), 0, 0))


def spectra_of(filters):
    width = filters.shape[1]
    tiles = width // 8
    view = filters.reshape(2, tiles, 8, ROWS, LANES).transpose(0, 1, 3, 2, 4).reshape(2, tiles, ROWS * 8, LANES)
    consts, specs = tables_of(("first_nat", "twist", "pair"))
    return call(
        spectra_kernel, "spectra", 3_000_000_000, 5_000_000, vmem=56,
        grid=(width // BATCH,), in_specs=[PER_TILE] + specs,
        out_specs=pl.BlockSpec((BATCH * ROWS, 2 * LANES), lambda i: (i, 0)),
        out_shape=jax.ShapeDtypeStruct((width * ROWS, 2 * LANES), jnp.float32),
        scratch_shapes=[pltpu.VMEM((BATCH * ROWS, 12 * LANES), jnp.bfloat16)],
    )(view, *consts)


def filter_grads(lag):
    width = lag.shape[0] // ROWS
    tiles = width // 8
    consts, specs = tables_of(("twist", "both", "last_nat"))
    out = call(
        lag_kernel, "filter_grads", 3_000_000_000, 5_000_000,
        grid=(width // BATCH,),
        in_specs=[pl.BlockSpec((BATCH * ROWS, 4 * LANES), lambda i: (i, 0))] + specs,
        out_specs=PER_TILE,
        out_shape=jax.ShapeDtypeStruct((2, tiles, ROWS * 8, LANES), jnp.float32),
    )(lag, *consts)
    return out.reshape(2, tiles, ROWS, 8, LANES).transpose(0, 1, 3, 2, 4).reshape(2, width, LENGTH)


def mixer(own_taps, arrived, spectra):
    blocks, width, span = arrived.shape[0], arrived.shape[1] // 2, arrived.shape[2]
    consts, specs = tables_of(("first_split", "twist", "forward", "inverse", "last_split"))
    back_shape = (blocks // 2, width, 6 * span)
    rows, batch = (2, blocks * width, LANES), GROUP * GROUPS
    return call(
        mixer_kernel, "mixer", 100_000_000, 1_000_000, vmem=56,
        grid=(width // batch,),
        in_specs=[pl.BlockSpec(memory_space=pltpu.SMEM), whole(arrived.shape),
                  pl.BlockSpec((batch * ROWS, 2 * LANES), lambda i: (i, 0))] + specs,
        out_specs=[whole(back_shape), pl.BlockSpec((batch * ROWS, 4 * LANES), lambda i: (i, 0)), whole((16, LANES))],
        out_shape=[
            jax.ShapeDtypeStruct(back_shape, jnp.bfloat16),
            jax.ShapeDtypeStruct((width * ROWS, 4 * LANES), jnp.bfloat16),
            jax.ShapeDtypeStruct((16, LANES), jnp.bfloat16),
        ],
        scratch_shapes=[
            pltpu.VMEM(rows, jnp.float32),
            pltpu.VMEM(rows, jnp.float32),
            pltpu.VMEM(rows, jnp.float32),
            pltpu.VMEM(rows, jnp.float32),
            pltpu.VMEM((TAPS, width, LANES), jnp.float32),
            pltpu.VMEM((batch, ROWS, LANES), jnp.float32),
            pltpu.VMEM((2 * batch * ROWS, 6 * LANES), jnp.bfloat16),
            pltpu.VMEM((2 * batch * ROWS, 6 * LANES), jnp.bfloat16),
        ],
    )(own_taps, arrived, spectra, *consts)


STREAMS = 8


def send_kernel(rows_ref, *refs):
    weight_refs, (gate_ref, grad_ref, out_ref, total_ref) = refs[:STREAMS], refs[STREAMS:]
    blocks, width, span = out_ref.shape[0], out_ref.shape[1] // 2, out_ref.shape[2]
    step, steps = pl.program_id(0), pl.num_programs(0)
    count = blocks * gate_ref.shape[1] // total_ref.shape[1]
    sig = jax.nn.sigmoid(gate_ref[...].astype(jnp.float32))
    slopes = (grad_ref[...].astype(jnp.float32) * sig).T.astype(jnp.bfloat16)
    out_ref[pl.ds(step * count, count), width:, :] = slopes.reshape(count, width, span)
    part = weight_refs[0].shape[0]
    sides = []
    for side in range(2):
        refs = weight_refs[side::2]
        term = dot(rows_ref[:, :part], refs[0][...])
        for j in range(1, len(refs)):
            term = term + dot(rows_ref[:, j * part:(j + 1) * part], refs[j][...])
        sides.append(term)
    term = jnp.concatenate(sides, axis=1)

    @pl.when(step == 0)
    def _():
        total_ref[...] = term

    @pl.when((step > 0) & (step < steps - 1))
    def _():
        total_ref[...] += term

    @pl.when(step == steps - 1)
    def _():
        total = total_ref[...] + term
        out_ref[:, :width, :] = total.T.astype(jnp.bfloat16).reshape(blocks, width, span)


def sends(layer_in, w_value, gate, grads, count, steps=4):
    span, depth = layer_in.shape
    channels = w_value.shape[1]
    width = channels // count
    block = pl.BlockSpec((span, channels // steps), lambda i: (0, i))
    streams = [pl.BlockSpec((2 * depth // (steps * STREAMS), channels // 2),
                            functools.partial(lambda j, i: (STREAMS // 2 * i + j // 2, j % 2), j))
               for j in range(STREAMS)]
    return call(
        send_kernel, "sends", 2 * span * depth * channels, 12_500_000, vmem=56, grid=(steps,),
        in_specs=[pl.BlockSpec((span, depth // steps), lambda i: (0, i))] + streams + [block, block],
        out_specs=whole((count, 2 * width, span)),
        out_shape=jax.ShapeDtypeStruct((count, 2 * width, span), jnp.bfloat16),
        scratch_shapes=[pltpu.VMEM((span, channels), jnp.float32)],
    )(layer_in, *[w_value] * STREAMS, gate, grads)


def quarter_kernel(place_ref, rows_ref, others_ref, same_ref, cross_ref, other_ref):
    z = place_ref[0] % 2
    for y in range(4):
        to = slice(y * LANES, (y + 1) * LANES)
        own = pl.ds(pl.multiple_of((2 * y + z) * LANES, LANES), LANES)
        same_ref[:, to] = rows_ref[:, own]
        other_ref[:, to] = others_ref[:, own]
        cross_ref[:, to] = rows_ref[:, pl.ds(pl.multiple_of((2 * y + 1 - z) * LANES, LANES), LANES)]


def quarters_of(place, layer_in):
    span, depth = layer_in.shape
    quarter = jax.ShapeDtypeStruct((span, depth // 4), jnp.bfloat16)
    return call(
        quarter_kernel, "quarters", 0, 5_000_000,
        grid_spec=pltpu.PrefetchScalarGridSpec(
            num_scalar_prefetch=1, grid=(2,),
            in_specs=[pl.BlockSpec((span, depth // 4), lambda i, place: (0, 2 * (place[1] % 2) + i)),
                      pl.BlockSpec((span, depth // 4), lambda i, place: (0, 2 - 2 * (place[1] % 2) + i))],
            out_specs=[pl.BlockSpec((span, 4 * LANES), lambda i, place: (0, i))] * 3),
        out_shape=[quarter] * 3,
    )(place, layer_in, layer_in)


def quad_place():
    seq_at = lax.axis_index("seq")
    return seq_at // 4 % 2 * 2 + seq_at % 2


def share_kernel(back_ref, *refs):
    parts, (taps_ref, out_ref, back_buf, rows_buf, out_buf, in_sem, out_sem) = refs[:8], refs[8:]
    span, rows = rows_buf.shape[1], back_buf.shape[0]
    loads = [pltpu.make_async_copy(back_ref.at[:, pl.ds(0, 4 * span)], back_buf, in_sem.at[8])]
    loads += [pltpu.make_async_copy(part, rows_buf.at[n], in_sem.at[n]) for n, part in enumerate(parts)]
    for load in loads:
        load.start()
    loads[0].wait()
    stores = []
    for half in range(2):
        for load in loads[1 + 4 * half:5 + 4 * half]:
            load.wait()
        first = 8 * (half ^ (lax.axis_index("tp") % 2))
        for two in range(4):
            lanes = slice(two * 256, (two + 1) * 256)
            product = None
            for j in range(4):
                at = pl.multiple_of((quad_place() ^ j) * span, span)
                term = dot(back_buf[:, pl.ds(at, span)], rows_buf[4 * half + j, :, lanes])
                product = term if product is None else product + term
            product = product.astype(jnp.bfloat16)
            n = 4 * half + two
            for m in range(2):
                out_buf[2 * n + m, :rows] = product[:, m * LANES:(m + 1) * LANES]
                out_buf[2 * n + m, rows:] = taps_ref[...]
            store = pltpu.make_async_copy(
                out_buf.at[pl.ds(2 * n, 2)], out_ref.at[pl.ds(first + 2 * two, 2)], out_sem.at[n])
            store.start()
            stores.append(store)
    for store in stores:
        store.wait()


def shares(back, mine, other, taps):
    span, depth = mine[0].shape
    rows = back.shape[0]
    return call(
        share_kernel, "shares", 16 * rows * span * depth, 7_000_000, vmem=60,
        in_specs=[pl.BlockSpec(memory_space=pl.ANY)] * 9 + [pl.BlockSpec(memory_space=pltpu.VMEM)],
        out_specs=pl.BlockSpec(memory_space=pl.ANY),
        out_shape=jax.ShapeDtypeStruct((16, rows + 16, LANES), jnp.bfloat16),
        scratch_shapes=[
            pltpu.VMEM((rows, 4 * span), jnp.bfloat16), pltpu.VMEM((8, span, depth), jnp.bfloat16),
            pltpu.VMEM((16, rows + 16, LANES), jnp.bfloat16),
            pltpu.SemaphoreType.DMA((9,)), pltpu.SemaphoreType.DMA((8,))],
    )(back, *mine, *other, taps)


def merge(pair, mine, mate):
    first, second = jnp.where(pair == 0, mine, mate), jnp.where(pair == 0, mate, mine)
    half = mine.shape[0] // 2
    return jnp.concatenate([first[half:], first[:half], second[:half], second[half:]], axis=0)


def weight_kernel(*refs):
    share_refs, (taps_ref, weight_ref, tap_sums_ref) = refs[:4], refs[4:]
    for x, ref in enumerate(share_refs):
        totals = []
        for pair in range(2):
            terms = [ref[j].astype(jnp.float32) for j in range(16) if j % 4 // 2 == pair]
            totals.append(sum(terms[1:], terms[0]))
        weight_ref[:, x * 2 * LANES:(x + 1) * 2 * LANES] = merge(0, *totals).T
    z = lax.axis_index("seq") % 2
    lane = lax.broadcasted_iota(jnp.int32, (8, LANES), 1)
    for x in range(8):
        row = jnp.zeros((8, LANES), jnp.float32)
        for n in range(4):
            packed = taps_ref[2 * x + n // 2].astype(jnp.float32)
            packed = jnp.where(z == n % 2, packed[:8], packed[8:])
            packed = packed + pltpu.roll(packed, LANES - 32, 1) + pltpu.roll(packed, LANES - 64, 1)
            row = jnp.where(lane // 32 == n, packed if n == 0 else pltpu.roll(packed, 32 * n, 1), row)
        tap_sums_ref[:, x * LANES:(x + 1) * LANES] = row[:TAPS]


def close_weight(parts):
    count, rows, span = parts.shape
    rows -= 16
    channels = 2 * rows
    return call(
        weight_kernel, "close_weight", 2_000_000, 3_000_000, grid=(1,),
        in_specs=[pl.BlockSpec((count, LANES, span), functools.partial(lambda x, i: (0, x, 0), x)) for x in range(4)]
        + [pl.BlockSpec((count, 16, span), lambda i: (0, rows // 16, 0))],
        out_specs=[whole((span, channels)), whole((TAPS, channels))],
        out_shape=[jax.ShapeDtypeStruct((span, channels), jnp.float32),
                   jax.ShapeDtypeStruct((TAPS, channels), jnp.float32)],
    )(*[parts] * 5)


def input_kernel(place_ref, back_ref, mate_ref, weight_ref, send_ref, keep_ref, own_buf):
    @pl.when(pl.program_id(0) == 0)
    def _():
        pair = place_ref[0] // 2
        for x in range(4):
            for odd, mine, other in ((0, 1 + pair, 2 - pair), (1, 3 * pair, 3 - 3 * pair)):
                rows = slice((2 * x + odd) * 64, (2 * x + odd + 1) * 64)
                own_buf[pl.ds(pl.multiple_of((4 * x + mine) * 64, 64), 64), :] = back_ref[rows, :]
                own_buf[pl.ds(pl.multiple_of((4 * x + other) * 64, 64), 64), :] = mate_ref[rows, :]

    term = dot(weight_ref[...], own_buf[...])

    @pl.when(pl.program_id(0) < 2)
    def _():
        send_ref[0] = term.astype(jnp.bfloat16)

    @pl.when(pl.program_id(0) >= 2)
    def _():
        keep_ref[0] = term


def input_terms(place, back, mate, w_value):
    depth, channels = w_value.shape
    rows, span = depth // 4, 256
    return call(
        input_kernel, "input_terms", 2 * span * depth * channels, 12_000_000, vmem=24,
        grid_spec=pltpu.PrefetchScalarGridSpec(
            num_scalar_prefetch=1, grid=(4,),
            in_specs=[pl.BlockSpec((channels // 2, span), lambda i, place: (0, place[0])),
                      pl.BlockSpec((channels // 2, span), lambda i, place: (0, 0)),
                      pl.BlockSpec((rows, channels), lambda i, place: (place[1] ^ ((2 * i + 1 - i // 2) % 4), 0))],
            out_specs=[pl.BlockSpec((1, rows, span), lambda i, place: (jnp.minimum(i, 1), 0, 0)),
                       pl.BlockSpec((1, rows, span), lambda i, place: (jnp.maximum(i - 2, 0), 0, 0))],
            scratch_shapes=[pltpu.VMEM((channels, span), jnp.bfloat16)]),
        out_shape=[jax.ShapeDtypeStruct((2, rows, span), jnp.bfloat16),
                   jax.ShapeDtypeStruct((2, rows, span), jnp.float32)],
    )(place, back, mate, w_value)


def close_kernel(keep_ref, core_ref, chip_ref, out_ref):
    total = keep_ref[0] + core_ref[0].astype(jnp.float32) + chip_ref[...].astype(jnp.float32)
    out_ref[...] = total.T.astype(jnp.bfloat16)


def close_input(keep, core, chip):
    rows, span = chip.shape
    first = pl.BlockSpec((1, 512, span), lambda i: (0, i, 0))
    return call(
        close_kernel, "close_input", 1_000_000, 3_000_000, grid=(rows // 512,),
        in_specs=[first, first, pl.BlockSpec((512, span), lambda i: (i, 0))],
        out_specs=pl.BlockSpec((span, 512), lambda i: (0, i)),
        out_shape=jax.ShapeDtypeStruct((span, rows), jnp.bfloat16))(keep, core, chip)


def gate_kernel(place_ref, mixed_ref, mate_ref, gate_ref, grad_ref, out_ref):
    mixed = merge(place_ref[0] // 2, mixed_ref[...].astype(jnp.float32), mate_ref[...].astype(jnp.float32)).T
    sig = jax.nn.sigmoid(gate_ref[...].astype(jnp.float32))
    out_ref[...] = (grad_ref[...].astype(jnp.float32) * mixed * sig * (1.0 - sig)).astype(jnp.bfloat16)


def gate_grad(place, back, mate, gate, grads):
    span, channels = gate.shape
    block = pl.BlockSpec((span, channels // 4), lambda i, place: (0, i))
    return call(
        gate_kernel, "gate_grad", 2_000_000, 2_500_000,
        grid_spec=pltpu.PrefetchScalarGridSpec(
            num_scalar_prefetch=1, grid=(4,),
            in_specs=[pl.BlockSpec((LANES, span), lambda i, place: (i, 4 + place[0] // 2)),
                      pl.BlockSpec((LANES, span), lambda i, place: (i, 1)), block, block],
            out_specs=block),
        out_shape=jax.ShapeDtypeStruct(gate.shape, jnp.bfloat16))(place, back, mate, gate, grads)


def local(layer_in, w_value, short_taps, long_filters, gate_proj, grad_out):
    seq_count = lax.axis_size("seq")
    seq_at, tp_at = lax.axis_index("seq"), lax.axis_index("tp")
    span, depth = layer_in.shape
    channels = w_value.shape[1]
    width = channels // seq_count
    quad_at = quad_place()
    place = jnp.stack([quad_at, tp_at]).astype(jnp.int32)
    cores, chips = [(0, 1), (1, 0), (2, 3), (3, 2)], [(0, 2), (2, 0), (1, 3), (3, 1)]

    def exchange(value, index_groups=None):
        return lax.all_to_all(
            value, "seq", split_axis=0, concat_axis=0, axis_index_groups=index_groups, tiled=True)

    def mates(value):
        return lax.ppermute(value, "seq", [(s, s ^ MATE) for s in range(seq_count)])

    outgoing = sends(layer_in, w_value, gate_proj, grad_out, seq_count)
    rows_in, outgoing = lax.optimization_barrier((layer_in, outgoing))
    arrived = exchange(outgoing)
    same, cross, other = quarters_of(place, rows_in)

    def across(value, flip):
        return lax.ppermute(
            value, ("seq", "tp"), [(4 * s + t, 4 * (s ^ flip) + (t ^ 2)) for s in range(seq_count) for t in range(4)])

    first = across(cross, 1)
    spectra = spectra_of(long_filters)
    same, cross, spectra = lax.optimization_barrier((same, cross, spectra))
    mine = [same, first, mates(same), across(cross, 1 ^ MATE)]

    own_taps = lax.dynamic_slice_in_dim(short_taps, seq_at * width, width, 1)
    back, lag, taps = mixer(own_taps, arrived, spectra)
    back, mine = lax.optimization_barrier((back, mine))
    other = [other] + [lax.ppermute(part, "tp", cores) for part in mine[1:]]
    back = exchange(back, LEAGUES).reshape(channels // 2, back.shape[2])
    grad_filters = filter_grads(lag)
    partner = lax.ppermute(taps, "seq", [(s, s ^ 1) for s in range(seq_count)])
    taps = jnp.concatenate([taps[:8], partner[:8]], axis=0)
    back, grad_filters, other, taps = lax.optimization_barrier((back, grad_filters, other, taps))
    mate = mates(jnp.concatenate([
        lax.dynamic_slice_in_dim(back, (quad_at ^ 2) * span, span, 1),
        lax.dynamic_slice_in_dim(back, 4 * span + (1 - quad_at // 2) * span, span, 1)], axis=1))
    outgoing, mate = lax.optimization_barrier((shares(back, mine, other, taps), mate))
    parts = exchange(outgoing, PLANES)

    send, keep = input_terms(place, back, mate, w_value)
    core = lax.ppermute(send, "tp", cores)
    send = (keep[1] + core[1].astype(jnp.float32)).astype(jnp.bfloat16)
    chip = lax.ppermute(send, "tp", chips)
    grad_input = close_input(keep, core, chip)
    grad_gate = gate_grad(place, back, mate, gate_proj, grad_out)
    parts, grad_input, grad_gate = lax.optimization_barrier((parts, grad_input, grad_gate))
    grad_weight, grad_taps = close_weight(parts)
    return (grad_input, grad_weight, grad_taps, grad_filters, grad_gate)


def solution(mesh):
    in_specs = (
        P("seq", None),
        P(None, "tp"),
        P(None, "tp"),
        P(None, ("tp", "seq"), None),
        P("seq", "tp"),
        P("seq", "tp"),
    )
    out_specs = (
        P("seq", "tp"),
        P("seq", "tp"),
        P(None, "tp"),
        P(None, ("tp", "seq"), None),
        P("seq", "tp"),
    )
    return jax.shard_map(local, mesh=mesh, in_specs=in_specs, out_specs=out_specs, check_vma=False)
```

```python
import functools
import math

import jax
import jax.numpy as jnp
import ml_dtypes
import numpy as np
from jax import lax
from jax.experimental import pallas as pl
from jax.experimental.pallas import tpu as pltpu
from jax.sharding import PartitionSpec as P

LANES = 128
ROWS = 64
LENGTH = ROWS * LANES
TAPS = 7
REACH = TAPS // 2
BATCH = 4
GROUP, GROUPS = 2, 8


def halves(table):
    high = table.astype(ml_dtypes.bfloat16)
    low = (table - high.astype(np.float64)).astype(ml_dtypes.bfloat16)
    return high, low


@functools.lru_cache(maxsize=None)
def tables(blocks):
    half = np.arange(ROWS) + 0.5
    natural = np.arange(ROWS)
    split = (2 * np.arange(blocks)[None, :] + np.arange(2)[:, None]).reshape(-1)

    def first(order):
        turn = 2.0 * math.pi / LANES * np.outer(half, order)
        return halves(np.concatenate([np.cos(turn), -np.sin(turn)], axis=0))

    def last(order):
        turn = 2.0 * math.pi / LANES * np.outer(order, half)
        return halves(np.concatenate([np.cos(turn), -np.sin(turn)], axis=1) / LENGTH)

    split_high, split_low = first(split)
    nat_high, nat_low = first(natural)
    first_split = np.concatenate([split_high, split_low], axis=1)
    first_nat = np.concatenate([nat_high, nat_low, nat_high, nat_low], axis=1)
    inv_split_high, inv_split_low = last(split)
    inv_nat_high, inv_nat_low = last(natural)
    last_split = np.concatenate([inv_split_high, inv_split_high, inv_split_low], axis=1)
    last_nat = np.concatenate([inv_nat_high, inv_nat_high, inv_nat_low], axis=1)
    twist = 2.0 * math.pi / (2 * LENGTH) * np.outer(half, np.arange(LANES))
    twist = np.stack([np.cos(twist), -np.sin(twist)]).astype(np.float32)
    grid = 2.0 * math.pi / LANES * np.outer(np.arange(LANES), np.arange(LANES))
    cos, sin = np.cos(grid), np.sin(grid)

    def stacked(table):
        high, low = halves(table)
        return np.concatenate([high, high, low], axis=0)

    forward = np.block([[cos, -sin], [sin, cos]])
    mirror = np.block([[cos, sin], [sin, -cos]])
    inverse = np.block([[cos, sin], [-sin, cos]])
    pair = np.concatenate([stacked(forward), stacked(mirror)], axis=0)
    both = np.concatenate([stacked(inverse), stacked(np.block([[cos, sin], [sin, -cos]]))], axis=1)
    return {
        "first_split": first_split, "first_nat": first_nat, "twist": twist, "forward": stacked(forward), "pair": pair,
        "inverse": stacked(inverse), "both": both, "last_split": last_split, "last_nat": last_nat,
    }


def cut(value):
    high = value.astype(jnp.bfloat16)
    low = (value - high.astype(jnp.float32)).astype(jnp.bfloat16)
    return high, low


def store_parts(ref, row, col, real, imag):
    real_high, real_low = cut(real)
    imag_high, imag_low = cut(imag)
    parts = (real_high, imag_high, real_low, imag_low, real_high, imag_high)
    for at, part in enumerate(parts):
        ref[row:row + ROWS, col + at * LANES:col + (at + 1) * LANES] = part


def shifted(early, late, step):
    if step == 0:
        return early, late
    lane = lax.broadcasted_iota(jnp.int32, early.shape, 1)
    row = lax.broadcasted_iota(jnp.int32, early.shape, 0)
    count = early.shape[0]
    turned_early = pltpu.roll(early, (-step) % LANES, 1)
    turned_late = pltpu.roll(late, (-step) % LANES, 1)
    if step > 0:
        keep = lane < LANES - step
        beyond = jnp.where(row == count - 1, 0.0, pltpu.roll(turned_early, count - 1, 0))
        return jnp.where(keep, turned_early, turned_late), jnp.where(keep, turned_late, beyond)
    keep = lane >= -step
    before = jnp.where(row == 0, 0.0, pltpu.roll(turned_late, 1, 0))
    return jnp.where(keep, turned_early, before), jnp.where(keep, turned_late, turned_early)


def dot(left, right):
    return jnp.dot(left, right, preferred_element_type=jnp.float32)


Y_OF = ((1, 2), (0, 3))
QUADS = [[(x * 4 + Y_OF[odd][pair]) * 2 + z for pair in range(2) for z in range(2)] for x in range(4) for odd in range(2)]
LEAGUES = [[quad[2 * pair + z] for quad in QUADS for z in range(2)] for pair in range(2)]
PLANES = [[2 * j + z for j in range(16)] for z in range(2)]
MATE = 6


def twisted(array, col, twist_ref):
    real = array[:ROWS, col * LANES:(col + 1) * LANES]
    imag = array[ROWS:, col * LANES:(col + 1) * LANES]
    return real * twist_ref[0] - imag * twist_ref[1], real * twist_ref[1] + imag * twist_ref[0]


def untwisted(array, twist_ref):
    real, imag = array[:, :LANES], array[:, LANES:]
    return jnp.concatenate(
        [real * twist_ref[0] + imag * twist_ref[1], imag * twist_ref[0] - real * twist_ref[1]], axis=0)


def finish(table_ref, one, two):
    high, low = cut(jnp.concatenate([one, two], axis=1))
    return dot(table_ref[...], jnp.concatenate([high, low, high], axis=0))


def spectra_kernel(filters_ref, first_nat_ref, twist_ref, pair_ref, out_ref, kernel_buf):
    for q in range(BATCH):
        at = (pl.program_id(0) % (8 // BATCH)) * BATCH + q
        plus = filters_ref[0, 0, pl.ds(at, ROWS, stride=8), :]
        minus = filters_ref[1, 0, pl.ds(at, ROWS, stride=8), :]
        high, low = cut(jnp.concatenate([plus, minus], axis=1))
        section = dot(first_nat_ref[...], jnp.concatenate([high, high, low, low], axis=0))
        store_parts(kernel_buf, q * ROWS, 0, *twisted(section, 0, twist_ref))
        store_parts(kernel_buf, q * ROWS, 6 * LANES, *twisted(section, 1, twist_ref))
    out_ref[...] = dot(kernel_buf[...], pair_ref[...])


def lag_kernel(lag_one_ref, lag_two_ref, twist_ref, both_ref, last_nat_ref, out_ref):
    parts = jnp.where(pl.program_id(0) < pl.num_programs(0) // 2, lag_one_ref[...], lag_two_ref[...])
    unmixed = dot(jnp.concatenate([parts, parts[:, :2 * LANES]], axis=1), both_ref[...])
    for q in range(BATCH):
        at = (pl.program_id(0) % (8 // BATCH)) * BATCH + q
        rows = slice(q * ROWS, (q + 1) * ROWS)
        pair = finish(last_nat_ref, untwisted(unmixed[rows, :2 * LANES], twist_ref),
                      untwisted(unmixed[rows, 2 * LANES:], twist_ref))
        out_ref[0, 0, pl.ds(at, ROWS, stride=8), :] = pair[:, :LANES]
        out_ref[1, 0, pl.ds(at, ROWS, stride=8), :] = pair[:, LANES:]


def mixer_kernel(
    first, taps_ref, arrived_ref, spectra_ref, first_split_ref, twist_ref, forward_ref, inverse_ref, last_split_ref,
    back_ref, lag_ref, taps_out_ref,
    values_buf, slopes_buf, back_buf, mixed_buf, taps_buf, extra_buf, signal_buf, product_buf,
):
    blocks, total, width = arrived_ref.shape[0], arrived_ref.shape[1] // 2, back_ref.shape[1]
    step = pl.program_id(0)

    @pl.when(step == 0)
    def _():
        for h in range(2):
            part = slice(h * LANES, (h + 1) * LANES)
            for buf, at in ((values_buf, first), (slopes_buf, total + first)):
                buf[h] = arrived_ref[:, at:at + width, part].astype(jnp.float32).reshape(blocks * width, LANES)

    pooled = {}

    def start(g):
        for q in range(g * GROUP, (g + 1) * GROUP):
            c = step * GROUP * GROUPS + q
            early = values_buf[0, pl.ds(c, blocks, stride=width), :]
            late = values_buf[1, pl.ds(c, blocks, stride=width), :]
            sum_early, sum_late = None, None
            for k in range(TAPS):
                one, two = shifted(early, late, k - REACH)
                tap = taps_ref[k, first + c]
                sum_early = tap * one if k == 0 else sum_early + tap * one
                sum_late = tap * two if k == 0 else sum_late + tap * two
            short = jnp.concatenate([sum_early, sum_late], axis=0).astype(jnp.bfloat16)
            conv = short.astype(jnp.float32)
            slope = jnp.concatenate(
                [slopes_buf[h, pl.ds(c, blocks, stride=width), :] for h in range(2)], axis=0)
            sig = jax.nn.sigmoid(conv)
            pooled[q] = jnp.sum(conv * sig, keepdims=True) / LENGTH
            mean_grad = jnp.sum(slope, keepdims=True) / LENGTH
            extra_buf[q] = mean_grad * (sig * (1.0 + conv * (1.0 - sig)))
            both = jnp.concatenate([short, slope.astype(jnp.bfloat16)], axis=1)
            section = dot(first_split_ref[...], jnp.concatenate([both, both], axis=0))
            store_parts(signal_buf, 2 * q * ROWS, 0, *twisted(section, 0, twist_ref))
            store_parts(signal_buf, (2 * q + 1) * ROWS, 0, *twisted(section, 1, twist_ref))

    def multiply(g):
        base = 2 * g * GROUP * ROWS
        spec = dot(signal_buf[base:base + 2 * GROUP * ROWS], forward_ref[...])
        for q in range(GROUP):
            short, slope = spec[2 * q * ROWS:(2 * q + 1) * ROWS], spec[(2 * q + 1) * ROWS:(2 * q + 2) * ROWS]
            rows = slice((g * GROUP + q) * ROWS, (g * GROUP + q + 1) * ROWS)
            short_re, short_im = short[:, :LANES], short[:, LANES:]
            slope_re, slope_im = slope[:, :LANES], slope[:, LANES:]
            filt_re, filt_im = spectra_ref[rows, :LANES], spectra_ref[rows, LANES:]
            store_parts(product_buf, base + 2 * q * ROWS, 0,
                        short_re * filt_re - short_im * filt_im, short_re * filt_im + short_im * filt_re)
            store_parts(product_buf, base + (2 * q + 1) * ROWS, 0,
                        slope_re * filt_re + slope_im * filt_im, slope_im * filt_re - slope_re * filt_im)
            real_high, real_low = cut(slope_re * short_re + slope_im * short_im)
            imag_high, imag_low = cut(slope_im * short_re - slope_re * short_im)
            for at, part in enumerate((real_high, imag_high, real_low, imag_low)):
                lag_ref[rows, at * LANES:(at + 1) * LANES] = part

    def end(g):
        base = 2 * g * GROUP * ROWS
        unmixed = dot(product_buf[base:base + 2 * GROUP * ROWS], inverse_ref[...])
        for q in range(GROUP):
            c = step * GROUP * GROUPS + g * GROUP + q
            rows = 2 * q * ROWS
            long_pair = finish(last_split_ref, untwisted(unmixed[rows:rows + ROWS], twist_ref),
                               untwisted(unmixed[rows + ROWS:rows + 2 * ROWS], twist_ref))
            mixed = long_pair[:, :LANES] + pooled[g * GROUP + q]
            slope_back = long_pair[:, LANES:] + extra_buf[g * GROUP + q]
            slope_back = slope_back.astype(jnp.bfloat16).astype(jnp.float32)
            early = values_buf[0, pl.ds(c, blocks, stride=width), :]
            late = values_buf[1, pl.ds(c, blocks, stride=width), :]
            sum_early, sum_late = None, None
            for k in range(TAPS):
                one, two = shifted(slope_back[:blocks], slope_back[blocks:], REACH - k)
                tap = taps_ref[k, first + c]
                sum_early = tap * one if k == 0 else sum_early + tap * one
                sum_late = tap * two if k == 0 else sum_late + tap * two
                taps_buf[k, pl.ds(c, 1), :] = jnp.sum(one * early + two * late, axis=0, keepdims=True)
            for h, part in enumerate((sum_early, sum_late)):
                back_buf[h, pl.ds(c, blocks, stride=width), :] = part
                mixed_buf[h, pl.ds(c, blocks, stride=width), :] = mixed[h * blocks:(h + 1) * blocks]

    for turn in range(GROUPS + 2):
        if turn >= 2:
            end(turn - 2)
        if 1 <= turn <= GROUPS:
            multiply(turn - 1)
        if turn < GROUPS:
            start(turn)

    @pl.when(step == pl.num_programs(0) - 1)
    def _():
        for q, quad in enumerate(QUADS):
            for place, s in enumerate(quad):
                rows = slice(s * width, (s + 1) * width)
                for h in range(2):
                    part = back_buf[h, rows, :].astype(jnp.bfloat16)
                    lanes = slice((2 * place + h) * LANES, (2 * place + h + 1) * LANES)
                    back_ref[2 * q, :, lanes] = part
                    back_ref[2 * q + 1, :, lanes] = part
                    at = 8 + 2 * (place // 2) + h
                    back_ref[2 * q + place % 2, :, at * LANES:(at + 1) * LANES] = (
                        mixed_buf[h, rows, :].astype(jnp.bfloat16))
        lane = lax.broadcasted_iota(jnp.int32, (width, LANES), 1)
        packed = jnp.zeros((width, LANES), jnp.float32)
        for k in range(TAPS):
            rest = jnp.sum(taps_buf[k], axis=1, keepdims=True)
            for p in range(3):
                piece = rest.astype(jnp.bfloat16).astype(jnp.float32)
                packed = jnp.where(lane == 8 * p + k, piece, packed)
                rest = rest - piece
        packed = jnp.concatenate([packed, jnp.zeros((LANES - width, LANES), jnp.float32)], axis=0).T
        rows = pltpu.roll(packed[8:16], total + first, 1) + pltpu.roll(packed[16:24], 2 * total + first, 1)
        rows = rows + (pltpu.roll(packed[:8], first, 1) if first else packed[:8])
        taps_out_ref[...] = jnp.concatenate([rows, jnp.zeros_like(rows)], axis=0).astype(jnp.bfloat16)


def whole(shape):
    return pl.BlockSpec(shape, lambda *_: (0,) * len(shape))


def call(kernel, name, flops, nbytes, vmem=16, **kwargs):
    return pl.pallas_call(
        kernel, name=name,
        compiler_params=pltpu.CompilerParams(vmem_limit_bytes=vmem * 1024 * 1024),
        cost_estimate=pl.CostEstimate(flops=flops, bytes_accessed=nbytes, transcendentals=0), **kwargs)


def tables_of(names, blocks=LENGTH // 256):
    chosen = [jnp.asarray(tables(blocks)[name]) for name in names]
    return chosen, [whole(table.shape) for table in chosen]


PER_TILE = pl.BlockSpec((2, 1, ROWS * 8, LANES), lambda i: (0, i // (8 // BATCH), 0, 0))


def spectra_of(filters):
    width = filters.shape[1]
    tiles = width // 8
    view = filters.reshape(2, tiles, 8, ROWS, LANES).transpose(0, 1, 3, 2, 4).reshape(2, tiles, ROWS * 8, LANES)
    consts, specs = tables_of(("first_nat", "twist", "pair"))
    return call(
        spectra_kernel, "spectra", 3_000_000_000, 5_000_000, vmem=56,
        grid=(width // BATCH,), in_specs=[PER_TILE] + specs,
        out_specs=pl.BlockSpec((BATCH * ROWS, 2 * LANES), lambda i: (i, 0)),
        out_shape=jax.ShapeDtypeStruct((width * ROWS, 2 * LANES), jnp.float32),
        scratch_shapes=[pltpu.VMEM((BATCH * ROWS, 12 * LANES), jnp.bfloat16)],
    )(view, *consts)


def filter_grads(lag_one, lag_two):
    width = 2 * lag_one.shape[0] // ROWS
    tiles, steps = width // 8, width // BATCH // 2
    consts, specs = tables_of(("twist", "both", "last_nat"))
    out = call(
        lag_kernel, "filter_grads", 3_000_000_000, 5_000_000,
        grid=(width // BATCH,),
        in_specs=[pl.BlockSpec((BATCH * ROWS, 4 * LANES), lambda i: (jnp.minimum(i, steps - 1), 0)),
                  pl.BlockSpec((BATCH * ROWS, 4 * LANES), lambda i: (jnp.maximum(i - steps, 0), 0))] + specs,
        out_specs=PER_TILE,
        out_shape=jax.ShapeDtypeStruct((2, tiles, ROWS * 8, LANES), jnp.float32),
    )(lag_one, lag_two, *consts)
    return out.reshape(2, tiles, ROWS, 8, LANES).transpose(0, 1, 3, 2, 4).reshape(2, width, LENGTH)


def mixer(own_taps, arrived, spectra, half):
    blocks, width, span = arrived.shape[0], arrived.shape[1] // 4, arrived.shape[2]
    consts, specs = tables_of(("first_split", "twist", "forward", "inverse", "last_split"))
    back_shape = (blocks // 2, width, 6 * span)
    rows, batch = (2, blocks * width, LANES), GROUP * GROUPS
    return call(
        functools.partial(mixer_kernel, half * width), "mixer", 9_000_000_000, 4_000_000, vmem=56,
        grid=(width // batch,),
        in_specs=[pl.BlockSpec(memory_space=pltpu.SMEM), whole(arrived.shape),
                  pl.BlockSpec((batch * ROWS, 2 * LANES), lambda i: (half * (width // batch) + i, 0))] + specs,
        out_specs=[whole(back_shape), pl.BlockSpec((batch * ROWS, 4 * LANES), lambda i: (i, 0)), whole((16, LANES))],
        out_shape=[
            jax.ShapeDtypeStruct(back_shape, jnp.bfloat16),
            jax.ShapeDtypeStruct((width * ROWS, 4 * LANES), jnp.bfloat16),
            jax.ShapeDtypeStruct((16, LANES), jnp.bfloat16),
        ],
        scratch_shapes=[
            pltpu.VMEM(rows, jnp.float32),
            pltpu.VMEM(rows, jnp.float32),
            pltpu.VMEM(rows, jnp.float32),
            pltpu.VMEM(rows, jnp.float32),
            pltpu.VMEM((TAPS, width, LANES), jnp.float32),
            pltpu.VMEM((batch, ROWS, LANES), jnp.float32),
            pltpu.VMEM((2 * batch * ROWS, 6 * LANES), jnp.bfloat16),
            pltpu.VMEM((2 * batch * ROWS, 6 * LANES), jnp.bfloat16),
        ],
    )(own_taps, arrived, spectra, *consts)


STREAMS = 8


def send_kernel(rows_ref, *refs):
    weight_refs, (gate_ref, grad_ref, out_ref, total_ref) = refs[:STREAMS], refs[STREAMS:]
    blocks, width, span = out_ref.shape[0], out_ref.shape[1] // 2, out_ref.shape[2]
    step, steps = pl.program_id(0), pl.num_programs(0)
    count = blocks * gate_ref.shape[1] // total_ref.shape[1]
    sig = jax.nn.sigmoid(gate_ref[...].astype(jnp.float32))
    slopes = (grad_ref[...].astype(jnp.float32) * sig).T.astype(jnp.bfloat16)
    out_ref[pl.ds(step * count, count), width:, :] = slopes.reshape(count, width, span)
    part = weight_refs[0].shape[0]
    sides = []
    for side in range(2):
        refs = weight_refs[side::2]
        term = dot(rows_ref[:, :part], refs[0][...])
        for j in range(1, len(refs)):
            term = term + dot(rows_ref[:, j * part:(j + 1) * part], refs[j][...])
        sides.append(term)
    term = jnp.concatenate(sides, axis=1)

    @pl.when(step == 0)
    def _():
        total_ref[...] = term

    @pl.when((step > 0) & (step < steps - 1))
    def _():
        total_ref[...] += term

    @pl.when(step == steps - 1)
    def _():
        total = total_ref[...] + term
        out_ref[:, :width, :] = total.T.astype(jnp.bfloat16).reshape(blocks, width, span)


def sends(layer_in, w_value, gate, grads, count, steps=4):
    span, depth = layer_in.shape
    channels = w_value.shape[1]
    width = channels // count
    block = pl.BlockSpec((span, channels // steps), lambda i: (0, i))
    streams = [pl.BlockSpec((2 * depth // (steps * STREAMS), channels // 2),
                            functools.partial(lambda j, i: (STREAMS // 2 * i + j // 2, j % 2), j))
               for j in range(STREAMS)]
    return call(
        send_kernel, "sends", 2 * span * depth * channels, 12_500_000, vmem=56, grid=(steps,),
        in_specs=[pl.BlockSpec((span, depth // steps), lambda i: (0, i))] + streams + [block, block],
        out_specs=whole((count, 2 * width, span)),
        out_shape=jax.ShapeDtypeStruct((count, 2 * width, span), jnp.bfloat16),
        scratch_shapes=[pltpu.VMEM((span, channels), jnp.float32)],
    )(layer_in, *[w_value] * STREAMS, gate, grads)


def quarter_kernel(place_ref, rows_ref, others_ref, same_ref, cross_ref, other_ref):
    z = place_ref[0] % 2
    for y in range(4):
        to = slice(y * LANES, (y + 1) * LANES)
        own = pl.ds(pl.multiple_of((2 * y + z) * LANES, LANES), LANES)
        same_ref[:, to] = rows_ref[:, own]
        other_ref[:, to] = others_ref[:, own]
        cross_ref[:, to] = rows_ref[:, pl.ds(pl.multiple_of((2 * y + 1 - z) * LANES, LANES), LANES)]


def quarters_of(place, layer_in):
    span, depth = layer_in.shape
    quarter = jax.ShapeDtypeStruct((span, depth // 4), jnp.bfloat16)
    return call(
        quarter_kernel, "quarters", 0, 5_000_000,
        grid_spec=pltpu.PrefetchScalarGridSpec(
            num_scalar_prefetch=1, grid=(2,),
            in_specs=[pl.BlockSpec((span, depth // 4), lambda i, place: (0, 2 * (place[1] % 2) + i)),
                      pl.BlockSpec((span, depth // 4), lambda i, place: (0, 2 - 2 * (place[1] % 2) + i))],
            out_specs=[pl.BlockSpec((span, 4 * LANES), lambda i, place: (0, i))] * 3),
        out_shape=[quarter] * 3,
    )(place, layer_in, layer_in)


def quad_place():
    seq_at = lax.axis_index("seq")
    return seq_at // 4 % 2 * 2 + seq_at % 2


def share_kernel(half, back_ref, *refs):
    parts, refs = refs[:8], refs[8:]
    if half:
        taps_ref, _, out_ref, back_buf, rows_buf, out_buf, in_sem, out_sem = refs
    else:
        out_ref, back_buf, rows_buf, out_buf, in_sem, out_sem = refs
    span, rows, sent = rows_buf.shape[1], back_buf.shape[0], out_buf.shape[1]
    loads = [pltpu.make_async_copy(back_ref.at[:, pl.ds(0, 4 * span)], back_buf, in_sem.at[8])]
    loads += [pltpu.make_async_copy(part, rows_buf.at[n], in_sem.at[n]) for n, part in enumerate(parts)]
    for load in loads:
        load.start()
    loads[0].wait()
    stores = []
    for side in range(2):
        for load in loads[1 + 4 * side:5 + 4 * side]:
            load.wait()
        first = 8 * (side ^ (lax.axis_index("tp") % 2))
        for two in range(4):
            lanes = slice(two * 256, (two + 1) * 256)
            product = None
            for j in range(4):
                at = pl.multiple_of((quad_place() ^ j) * span, span)
                term = dot(back_buf[:, pl.ds(at, span)], rows_buf[4 * side + j, :, lanes])
                product = term if product is None else product + term
            product = product.astype(jnp.bfloat16)
            n = 4 * side + two
            for m in range(2):
                out_buf[2 * n + m, :rows] = product[:, m * LANES:(m + 1) * LANES]
                if half:
                    out_buf[2 * n + m, rows:] = taps_ref[...]
            store = pltpu.make_async_copy(
                out_buf.at[pl.ds(2 * n, 2)],
                out_ref.at[pl.ds(first + 2 * two, 2), pl.ds(half * rows, sent)], out_sem.at[n])
            store.start()
            stores.append(store)
    for store in stores:
        store.wait()


def shares(back, mine, other, taps=None, before=None):
    span, depth = mine[0].shape
    rows = back.shape[0]
    half = 0 if before is None else 1
    operands = [back, *mine, *other] + ([taps, before] if half else [])
    anywhere = pl.BlockSpec(memory_space=pl.ANY)
    return call(
        functools.partial(share_kernel, half), "shares", 16 * rows * span * depth, 7_000_000, vmem=60,
        in_specs=[anywhere] * 9 + ([pl.BlockSpec(memory_space=pltpu.VMEM), anywhere] if half else []),
        out_specs=anywhere,
        out_shape=jax.ShapeDtypeStruct((16, 2 * rows + 16, LANES), jnp.bfloat16),
        input_output_aliases={10: 0} if half else {},
        scratch_shapes=[
            pltpu.VMEM((rows, 4 * span), jnp.bfloat16), pltpu.VMEM((8, span, depth), jnp.bfloat16),
            pltpu.VMEM((16, rows + 16 * half, LANES), jnp.bfloat16),
            pltpu.SemaphoreType.DMA((9,)), pltpu.SemaphoreType.DMA((8,))],
    )(*operands)


def merge(pair, mine, mate):
    leagues = [[jnp.where(pair == 0, one, two) for one, two in zip(mine, mate)],
               [jnp.where(pair == 0, two, one) for one, two in zip(mine, mate)]]
    size = mine[0].shape[0] // 4
    pieces = []
    for y in range(4):
        league, odd = y // 2, Y_OF[0][y // 2] != y
        for z in range(2):
            at = (2 * odd + z) * size
            pieces += [leagues[league][half][at:at + size] for half in range(2)]
    return jnp.concatenate(pieces, axis=0)


def weight_kernel(*refs):
    share_refs, (taps_ref, weight_ref, tap_sums_ref) = refs[:8], refs[8:]
    for x in range(4):
        totals = [[], []]
        for pair in range(2):
            for half in range(2):
                ref = share_refs[4 * half + x]
                terms = [ref[j].astype(jnp.float32) for j in range(16) if j % 4 // 2 == pair]
                totals[pair].append(sum(terms[1:], terms[0]))
        weight_ref[:, x * 2 * LANES:(x + 1) * 2 * LANES] = merge(0, *totals).T
    z = lax.axis_index("seq") % 2
    lane = lax.broadcasted_iota(jnp.int32, (8, LANES), 1)
    for x in range(8):
        row = jnp.zeros((8, LANES), jnp.float32)
        for n in range(4):
            packed = taps_ref[2 * x + n // 2].astype(jnp.float32)
            packed = jnp.where(z == n % 2, packed[:8], packed[8:])
            packed = packed + pltpu.roll(packed, LANES - 32, 1) + pltpu.roll(packed, LANES - 64, 1)
            row = jnp.where(lane // 32 == n, packed if n == 0 else pltpu.roll(packed, 32 * n, 1), row)
        tap_sums_ref[:, x * LANES:(x + 1) * LANES] = row[:TAPS]


def close_weight(parts):
    count, rows, span = parts.shape
    rows -= 16
    channels = 2 * rows
    return call(
        weight_kernel, "close_weight", 2_000_000, 3_000_000, grid=(1,),
        in_specs=[pl.BlockSpec((count, 64, span), functools.partial(lambda n, i: (0, n, 0), n)) for n in range(8)]
        + [pl.BlockSpec((count, 16, span), lambda i: (0, rows // 16, 0))],
        out_specs=[whole((span, channels)), whole((TAPS, channels))],
        out_shape=[jax.ShapeDtypeStruct((span, channels), jnp.float32),
                   jax.ShapeDtypeStruct((TAPS, channels), jnp.float32)],
    )(*[parts] * 9)


def input_kernel(place_ref, *refs):
    back_refs, mate_refs, (weight_ref, send_ref, keep_ref, own_buf) = refs[:2], refs[2:4], refs[4:]

    @pl.when(pl.program_id(0) == 0)
    def _():
        pair = place_ref[0] // 2
        for half in range(2):
            for x in range(4):
                for odd, mine, other in ((0, 1 + pair, 2 - pair), (1, 3 * pair, 3 - 3 * pair)):
                    for z in range(2):
                        at = ((2 * x + odd) * 2 + z) * 16
                        for ref, y in ((back_refs[half], mine), (mate_refs[half], other)):
                            to = pl.multiple_of(((4 * x + y) * 2 + z) * 32 + half * 16, 16)
                            own_buf[pl.ds(to, 16), :] = ref[at:at + 16, :]

    term = dot(weight_ref[...], own_buf[...])

    @pl.when(pl.program_id(0) < 2)
    def _():
        send_ref[0] = term.astype(jnp.bfloat16)

    @pl.when(pl.program_id(0) >= 2)
    def _():
        keep_ref[0] = term


def input_terms(place, backs, mates, w_value):
    depth, channels = w_value.shape
    rows, span = depth // 4, 256
    return call(
        input_kernel, "input_terms", 2 * span * depth * channels, 12_000_000, vmem=24,
        grid_spec=pltpu.PrefetchScalarGridSpec(
            num_scalar_prefetch=1, grid=(4,),
            in_specs=[pl.BlockSpec((channels // 4, span), lambda i, place: (0, place[0]))] * 2
            + [pl.BlockSpec((channels // 4, span), lambda i, place: (0, 0))] * 2
            + [pl.BlockSpec((rows, channels), lambda i, place: (place[1] ^ ((2 * i + 1 - i // 2) % 4), 0))],
            out_specs=[pl.BlockSpec((1, rows, span), lambda i, place: (jnp.minimum(i, 1), 0, 0)),
                       pl.BlockSpec((1, rows, span), lambda i, place: (jnp.maximum(i - 2, 0), 0, 0))],
            scratch_shapes=[pltpu.VMEM((channels, span), jnp.bfloat16)]),
        out_shape=[jax.ShapeDtypeStruct((2, rows, span), jnp.bfloat16),
                   jax.ShapeDtypeStruct((2, rows, span), jnp.float32)],
    )(place, *backs, *mates, w_value)


def close_kernel(keep_ref, core_ref, chip_ref, out_ref):
    total = keep_ref[0] + core_ref[0].astype(jnp.float32) + chip_ref[...].astype(jnp.float32)
    out_ref[...] = total.T.astype(jnp.bfloat16)


def close_input(keep, core, chip):
    rows, span = chip.shape
    first = pl.BlockSpec((1, 512, span), lambda i: (0, i, 0))
    return call(
        close_kernel, "close_input", 1_000_000, 3_000_000, grid=(rows // 512,),
        in_specs=[first, first, pl.BlockSpec((512, span), lambda i: (i, 0))],
        out_specs=pl.BlockSpec((span, 512), lambda i: (0, i)),
        out_shape=jax.ShapeDtypeStruct((span, rows), jnp.bfloat16))(keep, core, chip)


def gate_kernel(place_ref, one_ref, two_ref, mate_one_ref, mate_two_ref, gate_ref, grad_ref, out_ref):
    mine = [ref[...].astype(jnp.float32) for ref in (one_ref, two_ref)]
    mate = [ref[...].astype(jnp.float32) for ref in (mate_one_ref, mate_two_ref)]
    mixed = merge(place_ref[0] // 2, mine, mate).T
    sig = jax.nn.sigmoid(gate_ref[...].astype(jnp.float32))
    out_ref[...] = (grad_ref[...].astype(jnp.float32) * mixed * sig * (1.0 - sig)).astype(jnp.bfloat16)


def gate_grad(place, backs, mates, gate, grads):
    span, channels = gate.shape
    block = pl.BlockSpec((span, channels // 4), lambda i, place: (0, i))
    return call(
        gate_kernel, "gate_grad", 2_000_000, 2_500_000,
        grid_spec=pltpu.PrefetchScalarGridSpec(
            num_scalar_prefetch=1, grid=(4,),
            in_specs=[pl.BlockSpec((64, span), lambda i, place: (i, 4 + place[0] // 2))] * 2
            + [pl.BlockSpec((64, span), lambda i, place: (i, 1))] * 2 + [block, block],
            out_specs=block),
        out_shape=jax.ShapeDtypeStruct(gate.shape, jnp.bfloat16))(place, *backs, *mates, gate, grads)


def local(layer_in, w_value, short_taps, long_filters, gate_proj, grad_out):
    seq_count = lax.axis_size("seq")
    seq_at, tp_at = lax.axis_index("seq"), lax.axis_index("tp")
    span, depth = layer_in.shape
    channels = w_value.shape[1]
    width = channels // seq_count
    quad_at = quad_place()
    place = jnp.stack([quad_at, tp_at]).astype(jnp.int32)
    cores, chips = [(0, 1), (1, 0), (2, 3), (3, 2)], [(0, 2), (2, 0), (1, 3), (3, 1)]

    def exchange(value, index_groups=None):
        return lax.all_to_all(
            value, "seq", split_axis=0, concat_axis=0, axis_index_groups=index_groups, tiled=True)

    def mates(value):
        return lax.ppermute(value, "seq", [(s, s ^ MATE) for s in range(seq_count)])

    outgoing = sends(layer_in, w_value, gate_proj, grad_out, seq_count)
    rows_in, outgoing = lax.optimization_barrier((layer_in, outgoing))
    arrived = exchange(outgoing)
    same, cross, other = quarters_of(place, rows_in)

    def across(value, flip):
        return lax.ppermute(
            value, ("seq", "tp"), [(4 * s + t, 4 * (s ^ flip) + (t ^ 2)) for s in range(seq_count) for t in range(4)])

    first = across(cross, 1)
    spectra = spectra_of(long_filters)
    same, cross, spectra = lax.optimization_barrier((same, cross, spectra))
    mine = [same, first, mates(same), across(cross, 1 ^ MATE)]

    own_taps = lax.dynamic_slice_in_dim(short_taps, seq_at * width, width, 1)
    def league(value):
        return exchange(value, LEAGUES).reshape(channels // 4, value.shape[2])

    def for_mate(back):
        return mates(jnp.concatenate([
            lax.dynamic_slice_in_dim(back, (quad_at ^ 2) * span, span, 1),
            lax.dynamic_slice_in_dim(back, 4 * span + (1 - quad_at // 2) * span, span, 1)], axis=1))

    back_one, lag_one, taps_one = mixer(own_taps, arrived, spectra, 0)
    arrived, back_one = lax.optimization_barrier((arrived, back_one))
    back_two, lag_two, taps_two = mixer(own_taps, arrived, spectra, 1)
    back_one = league(back_one)
    back_one, back_two, mine = lax.optimization_barrier((back_one, back_two, mine))
    other = [other] + [lax.ppermute(part, "tp", cores) for part in mine[1:]]
    back_two = league(back_two)
    mate_one = for_mate(back_one)
    grad_filters = filter_grads(lag_one, lag_two)
    taps = taps_one + taps_two
    partner = lax.ppermute(taps, "seq", [(s, s ^ 1) for s in range(seq_count)])
    taps = jnp.concatenate([taps[:8], partner[:8]], axis=0)
    outgoing = shares(back_one, mine, other)
    back_two, outgoing, mate_one, grad_filters, taps = lax.optimization_barrier(
        (back_two, outgoing, mate_one, grad_filters, taps))
    mate_two = for_mate(back_two)
    outgoing, mate_two = lax.optimization_barrier((shares(back_two, mine, other, taps, outgoing), mate_two))
    parts = exchange(outgoing, PLANES)
    backs, their = [back_one, back_two], [mate_one, mate_two]

    send, keep = input_terms(place, backs, their, w_value)
    core = lax.ppermute(send, "tp", cores)
    send = (keep[1] + core[1].astype(jnp.float32)).astype(jnp.bfloat16)
    chip = lax.ppermute(send, "tp", chips)
    grad_input = close_input(keep, core, chip)
    grad_gate = gate_grad(place, backs, their, gate_proj, grad_out)
    parts, grad_input, grad_gate = lax.optimization_barrier((parts, grad_input, grad_gate))
    grad_weight, grad_taps = close_weight(parts)
    return (grad_input, grad_weight, grad_taps, grad_filters, grad_gate)


def solution(mesh):
    in_specs = (
        P("seq", None),
        P(None, "tp"),
        P(None, "tp"),
        P(None, ("tp", "seq"), None),
        P("seq", "tp"),
        P("seq", "tp"),
    )
    out_specs = (
        P("seq", "tp"),
        P("seq", "tp"),
        P(None, "tp"),
        P(None, ("tp", "seq"), None),
        P("seq", "tp"),
    )
    return jax.shard_map(local, mesh=mesh, in_specs=in_specs, out_specs=out_specs, check_vma=False)
```

```python
import functools
import math

import jax
import jax.numpy as jnp
import ml_dtypes
import numpy as np
from jax import lax
from jax.experimental import pallas as pl
from jax.experimental.pallas import tpu as pltpu
from jax.sharding import PartitionSpec as P

LANES = 128
ROWS = 64
LENGTH = ROWS * LANES
TAPS = 7
REACH = TAPS // 2
BATCH = 4
GROUP, GROUPS = 2, 8


def halves(table):
    high = table.astype(ml_dtypes.bfloat16)
    low = (table - high.astype(np.float64)).astype(ml_dtypes.bfloat16)
    return high, low


@functools.lru_cache(maxsize=None)
def tables(blocks):
    half = np.arange(ROWS) + 0.5
    natural = np.arange(ROWS)
    split = (2 * np.arange(blocks)[None, :] + np.arange(2)[:, None]).reshape(-1)

    def first(order):
        turn = 2.0 * math.pi / LANES * np.outer(half, order)
        return halves(np.concatenate([np.cos(turn), -np.sin(turn)], axis=0))

    def last(order):
        turn = 2.0 * math.pi / LANES * np.outer(order, half)
        return halves(np.concatenate([np.cos(turn), -np.sin(turn)], axis=1) / LENGTH)

    split_high, split_low = first(split)
    nat_high, nat_low = first(natural)
    first_split = np.concatenate([split_high, split_low], axis=1)
    first_nat = np.concatenate([nat_high, nat_low, nat_high, nat_low], axis=1)
    inv_split_high, inv_split_low = last(split)
    inv_nat_high, inv_nat_low = last(natural)
    last_split = np.concatenate([inv_split_high, inv_split_high, inv_split_low], axis=1)
    last_nat = np.concatenate([inv_nat_high, inv_nat_high, inv_nat_low], axis=1)
    twist = 2.0 * math.pi / (2 * LENGTH) * np.outer(half, np.arange(LANES))
    twist = np.stack([np.cos(twist), -np.sin(twist)]).astype(np.float32)
    grid = 2.0 * math.pi / LANES * np.outer(np.arange(LANES), np.arange(LANES))
    cos, sin = np.cos(grid), np.sin(grid)

    def stacked(table):
        high, low = halves(table)
        return np.concatenate([high, high, low], axis=0)

    forward = np.block([[cos, -sin], [sin, cos]])
    mirror = np.block([[cos, sin], [sin, -cos]])
    inverse = np.block([[cos, sin], [-sin, cos]])
    pair = np.concatenate([stacked(forward), stacked(mirror)], axis=0)
    both = np.concatenate([stacked(inverse), stacked(np.block([[cos, sin], [sin, -cos]]))], axis=1)
    return {
        "first_split": first_split, "first_nat": first_nat, "twist": twist, "forward": stacked(forward), "pair": pair,
        "inverse": stacked(inverse), "both": both, "last_split": last_split, "last_nat": last_nat,
    }


def cut(value):
    high = value.astype(jnp.bfloat16)
    low = (value - high.astype(jnp.float32)).astype(jnp.bfloat16)
    return high, low


def store_parts(ref, row, col, real, imag):
    real_high, real_low = cut(real)
    imag_high, imag_low = cut(imag)
    parts = (real_high, imag_high, real_low, imag_low, real_high, imag_high)
    for at, part in enumerate(parts):
        ref[row:row + ROWS, col + at * LANES:col + (at + 1) * LANES] = part


def shifted(early, late, step):
    if step == 0:
        return early, late
    lane = lax.broadcasted_iota(jnp.int32, early.shape, 1)
    row = lax.broadcasted_iota(jnp.int32, early.shape, 0)
    count = early.shape[0]
    turned_early = pltpu.roll(early, (-step) % LANES, 1)
    turned_late = pltpu.roll(late, (-step) % LANES, 1)
    if step > 0:
        keep = lane < LANES - step
        beyond = jnp.where(row == count - 1, 0.0, pltpu.roll(turned_early, count - 1, 0))
        return jnp.where(keep, turned_early, turned_late), jnp.where(keep, turned_late, beyond)
    keep = lane >= -step
    before = jnp.where(row == 0, 0.0, pltpu.roll(turned_late, 1, 0))
    return jnp.where(keep, turned_early, before), jnp.where(keep, turned_late, turned_early)


def dot(left, right):
    return jnp.dot(left, right, preferred_element_type=jnp.float32)


Y_OF = ((1, 2), (0, 3))
QUADS = [[(x * 4 + Y_OF[odd][pair]) * 2 + z for pair in range(2) for z in range(2)] for x in range(4) for odd in range(2)]
LEAGUES = [[quad[2 * pair + z] for quad in QUADS for z in range(2)] for pair in range(2)]
PLANES = [[2 * j + z for j in range(16)] for z in range(2)]
MATE = 6


def twisted(array, col, twist_ref):
    real = array[:ROWS, col * LANES:(col + 1) * LANES]
    imag = array[ROWS:, col * LANES:(col + 1) * LANES]
    return real * twist_ref[0] - imag * twist_ref[1], real * twist_ref[1] + imag * twist_ref[0]


def untwisted(array, twist_ref):
    real, imag = array[:, :LANES], array[:, LANES:]
    return jnp.concatenate(
        [real * twist_ref[0] + imag * twist_ref[1], imag * twist_ref[0] - real * twist_ref[1]], axis=0)


def finish(table_ref, one, two):
    high, low = cut(jnp.concatenate([one, two], axis=1))
    return dot(table_ref[...], jnp.concatenate([high, low, high], axis=0))


def spectra_kernel(filters_ref, first_nat_ref, twist_ref, pair_ref, out_ref, kernel_buf):
    for q in range(BATCH):
        at = (pl.program_id(0) % (8 // BATCH)) * BATCH + q
        plus = filters_ref[0, 0, pl.ds(at, ROWS, stride=8), :]
        minus = filters_ref[1, 0, pl.ds(at, ROWS, stride=8), :]
        high, low = cut(jnp.concatenate([plus, minus], axis=1))
        section = dot(first_nat_ref[...], jnp.concatenate([high, high, low, low], axis=0))
        store_parts(kernel_buf, q * ROWS, 0, *twisted(section, 0, twist_ref))
        store_parts(kernel_buf, q * ROWS, 6 * LANES, *twisted(section, 1, twist_ref))
    out_ref[...] = dot(kernel_buf[...], pair_ref[...])


def lag_kernel(lag_one_ref, lag_two_ref, twist_ref, both_ref, last_nat_ref, out_ref):
    parts = jnp.where(pl.program_id(0) < pl.num_programs(0) // 2, lag_one_ref[...], lag_two_ref[...])
    unmixed = dot(jnp.concatenate([parts, parts[:, :2 * LANES]], axis=1), both_ref[...])
    for q in range(BATCH):
        at = (pl.program_id(0) % (8 // BATCH)) * BATCH + q
        rows = slice(q * ROWS, (q + 1) * ROWS)
        pair = finish(last_nat_ref, untwisted(unmixed[rows, :2 * LANES], twist_ref),
                      untwisted(unmixed[rows, 2 * LANES:], twist_ref))
        out_ref[0, 0, pl.ds(at, ROWS, stride=8), :] = pair[:, :LANES]
        out_ref[1, 0, pl.ds(at, ROWS, stride=8), :] = pair[:, LANES:]


def mixer_kernel(
    first, taps_ref, arrived_ref, spectra_ref, first_split_ref, twist_ref, forward_ref, inverse_ref, last_split_ref,
    back_ref, lag_ref, taps_out_ref,
    values_buf, slopes_buf, back_buf, mixed_buf, taps_buf, extra_buf, signal_buf, product_buf,
):
    blocks, total, width = arrived_ref.shape[0], arrived_ref.shape[1] // 2, back_ref.shape[1]
    step = pl.program_id(0)

    @pl.when(step == 0)
    def _():
        for h in range(2):
            part = slice(h * LANES, (h + 1) * LANES)
            for buf, at in ((values_buf, first), (slopes_buf, total + first)):
                buf[h] = arrived_ref[:, at:at + width, part].astype(jnp.float32).reshape(blocks * width, LANES)

    pooled = {}

    def start(g):
        for q in range(g * GROUP, (g + 1) * GROUP):
            c = step * GROUP * GROUPS + q
            early = values_buf[0, pl.ds(c, blocks, stride=width), :]
            late = values_buf[1, pl.ds(c, blocks, stride=width), :]
            sum_early, sum_late = None, None
            for k in range(TAPS):
                one, two = shifted(early, late, k - REACH)
                tap = taps_ref[k, first + c]
                sum_early = tap * one if k == 0 else sum_early + tap * one
                sum_late = tap * two if k == 0 else sum_late + tap * two
            short = jnp.concatenate([sum_early, sum_late], axis=0).astype(jnp.bfloat16)
            conv = short.astype(jnp.float32)
            slope = jnp.concatenate(
                [slopes_buf[h, pl.ds(c, blocks, stride=width), :] for h in range(2)], axis=0)
            sig = jax.nn.sigmoid(conv)
            pooled[q] = jnp.sum(conv * sig, keepdims=True) / LENGTH
            mean_grad = jnp.sum(slope, keepdims=True) / LENGTH
            extra_buf[q] = mean_grad * (sig * (1.0 + conv * (1.0 - sig)))
            both = jnp.concatenate([short, slope.astype(jnp.bfloat16)], axis=1)
            section = dot(first_split_ref[...], jnp.concatenate([both, both], axis=0))
            store_parts(signal_buf, 2 * q * ROWS, 0, *twisted(section, 0, twist_ref))
            store_parts(signal_buf, (2 * q + 1) * ROWS, 0, *twisted(section, 1, twist_ref))

    def multiply(g):
        base = 2 * g * GROUP * ROWS
        spec = dot(signal_buf[base:base + 2 * GROUP * ROWS], forward_ref[...])
        for q in range(GROUP):
            short, slope = spec[2 * q * ROWS:(2 * q + 1) * ROWS], spec[(2 * q + 1) * ROWS:(2 * q + 2) * ROWS]
            rows = slice((g * GROUP + q) * ROWS, (g * GROUP + q + 1) * ROWS)
            short_re, short_im = short[:, :LANES], short[:, LANES:]
            slope_re, slope_im = slope[:, :LANES], slope[:, LANES:]
            filt_re, filt_im = spectra_ref[rows, :LANES], spectra_ref[rows, LANES:]
            store_parts(product_buf, base + 2 * q * ROWS, 0,
                        short_re * filt_re - short_im * filt_im, short_re * filt_im + short_im * filt_re)
            store_parts(product_buf, base + (2 * q + 1) * ROWS, 0,
                        slope_re * filt_re + slope_im * filt_im, slope_im * filt_re - slope_re * filt_im)
            real_high, real_low = cut(slope_re * short_re + slope_im * short_im)
            imag_high, imag_low = cut(slope_im * short_re - slope_re * short_im)
            for at, part in enumerate((real_high, imag_high, real_low, imag_low)):
                lag_ref[rows, at * LANES:(at + 1) * LANES] = part

    def end(g):
        base = 2 * g * GROUP * ROWS
        unmixed = dot(product_buf[base:base + 2 * GROUP * ROWS], inverse_ref[...])
        for q in range(GROUP):
            c = step * GROUP * GROUPS + g * GROUP + q
            rows = 2 * q * ROWS
            long_pair = finish(last_split_ref, untwisted(unmixed[rows:rows + ROWS], twist_ref),
                               untwisted(unmixed[rows + ROWS:rows + 2 * ROWS], twist_ref))
            mixed = long_pair[:, :LANES] + pooled[g * GROUP + q]
            slope_back = long_pair[:, LANES:] + extra_buf[g * GROUP + q]
            slope_back = slope_back.astype(jnp.bfloat16).astype(jnp.float32)
            early = values_buf[0, pl.ds(c, blocks, stride=width), :]
            late = values_buf[1, pl.ds(c, blocks, stride=width), :]
            sum_early, sum_late = None, None
            for k in range(TAPS):
                one, two = shifted(slope_back[:blocks], slope_back[blocks:], REACH - k)
                tap = taps_ref[k, first + c]
                sum_early = tap * one if k == 0 else sum_early + tap * one
                sum_late = tap * two if k == 0 else sum_late + tap * two
                taps_buf[k, pl.ds(c, 1), :] = jnp.sum(one * early + two * late, axis=0, keepdims=True)
            for h, part in enumerate((sum_early, sum_late)):
                back_buf[h, pl.ds(c, blocks, stride=width), :] = part
                mixed_buf[h, pl.ds(c, blocks, stride=width), :] = mixed[h * blocks:(h + 1) * blocks]

    for turn in range(GROUPS + 2):
        if turn >= 2:
            end(turn - 2)
        if 1 <= turn <= GROUPS:
            multiply(turn - 1)
        if turn < GROUPS:
            start(turn)

    @pl.when(step == pl.num_programs(0) - 1)
    def _():
        for q, quad in enumerate(QUADS):
            for place, s in enumerate(quad):
                rows = slice(s * width, (s + 1) * width)
                for h in range(2):
                    part = back_buf[h, rows, :].astype(jnp.bfloat16)
                    lanes = slice((2 * place + h) * LANES, (2 * place + h + 1) * LANES)
                    back_ref[2 * q, :, lanes] = part
                    back_ref[2 * q + 1, :, lanes] = part
                    at = 8 + 2 * (place // 2) + h
                    back_ref[2 * q + place % 2, :, at * LANES:(at + 1) * LANES] = (
                        mixed_buf[h, rows, :].astype(jnp.bfloat16))
        lane = lax.broadcasted_iota(jnp.int32, (width, LANES), 1)
        packed = jnp.zeros((width, LANES), jnp.float32)
        for k in range(TAPS):
            rest = jnp.sum(taps_buf[k], axis=1, keepdims=True)
            for p in range(3):
                piece = rest.astype(jnp.bfloat16).astype(jnp.float32)
                packed = jnp.where(lane == 8 * p + k, piece, packed)
                rest = rest - piece
        packed = jnp.concatenate([packed, jnp.zeros((LANES - width, LANES), jnp.float32)], axis=0).T
        rows = pltpu.roll(packed[8:16], total + first, 1) + pltpu.roll(packed[16:24], 2 * total + first, 1)
        rows = rows + (pltpu.roll(packed[:8], first, 1) if first else packed[:8])
        taps_out_ref[...] = jnp.concatenate([rows, jnp.zeros_like(rows)], axis=0).astype(jnp.bfloat16)


def whole(shape):
    return pl.BlockSpec(shape, lambda *_: (0,) * len(shape))


def call(kernel, name, flops, nbytes, vmem=16, **kwargs):
    return pl.pallas_call(
        kernel, name=name,
        compiler_params=pltpu.CompilerParams(vmem_limit_bytes=vmem * 1024 * 1024),
        cost_estimate=pl.CostEstimate(flops=flops, bytes_accessed=nbytes, transcendentals=0), **kwargs)


def tables_of(names, blocks=LENGTH // 256):
    chosen = [jnp.asarray(tables(blocks)[name]) for name in names]
    return chosen, [whole(table.shape) for table in chosen]


PER_TILE = pl.BlockSpec((2, 1, ROWS * 8, LANES), lambda i: (0, i // (8 // BATCH), 0, 0))


def spectra_of(filters):
    width = filters.shape[1]
    tiles = width // 8
    view = filters.reshape(2, tiles, 8, ROWS, LANES).transpose(0, 1, 3, 2, 4).reshape(2, tiles, ROWS * 8, LANES)
    consts, specs = tables_of(("first_nat", "twist", "pair"))
    return call(
        spectra_kernel, "spectra", 3_000_000_000, 5_000_000, vmem=56,
        grid=(width // BATCH,), in_specs=[PER_TILE] + specs,
        out_specs=pl.BlockSpec((BATCH * ROWS, 2 * LANES), lambda i: (i, 0)),
        out_shape=jax.ShapeDtypeStruct((width * ROWS, 2 * LANES), jnp.float32),
        scratch_shapes=[pltpu.VMEM((BATCH * ROWS, 12 * LANES), jnp.bfloat16)],
    )(view, *consts)


def filter_grads(lag_one, lag_two):
    width = 2 * lag_one.shape[0] // ROWS
    tiles, steps = width // 8, width // BATCH // 2
    consts, specs = tables_of(("twist", "both", "last_nat"))
    out = call(
        lag_kernel, "filter_grads", 3_000_000_000, 5_000_000,
        grid=(width // BATCH,),
        in_specs=[pl.BlockSpec((BATCH * ROWS, 4 * LANES), lambda i: (jnp.minimum(i, steps - 1), 0)),
                  pl.BlockSpec((BATCH * ROWS, 4 * LANES), lambda i: (jnp.maximum(i - steps, 0), 0))] + specs,
        out_specs=PER_TILE,
        out_shape=jax.ShapeDtypeStruct((2, tiles, ROWS * 8, LANES), jnp.float32),
    )(lag_one, lag_two, *consts)
    return out.reshape(2, tiles, ROWS, 8, LANES).transpose(0, 1, 3, 2, 4).reshape(2, width, LENGTH)


def mixer(own_taps, arrived, spectra, half):
    blocks, width, span = arrived.shape[0], arrived.shape[1] // 4, arrived.shape[2]
    consts, specs = tables_of(("first_split", "twist", "forward", "inverse", "last_split"))
    back_shape = (blocks // 2, width, 6 * span)
    rows, batch = (2, blocks * width, LANES), GROUP * GROUPS
    return call(
        functools.partial(mixer_kernel, half * width), "mixer", 9_000_000_000, 4_000_000, vmem=56,
        grid=(width // batch,),
        in_specs=[pl.BlockSpec(memory_space=pltpu.SMEM), whole(arrived.shape),
                  pl.BlockSpec((batch * ROWS, 2 * LANES), lambda i: (half * (width // batch) + i, 0))] + specs,
        out_specs=[whole(back_shape), pl.BlockSpec((batch * ROWS, 4 * LANES), lambda i: (i, 0)), whole((16, LANES))],
        out_shape=[
            jax.ShapeDtypeStruct(back_shape, jnp.bfloat16),
            jax.ShapeDtypeStruct((width * ROWS, 4 * LANES), jnp.bfloat16),
            jax.ShapeDtypeStruct((16, LANES), jnp.bfloat16),
        ],
        scratch_shapes=[
            pltpu.VMEM(rows, jnp.float32),
            pltpu.VMEM(rows, jnp.float32),
            pltpu.VMEM(rows, jnp.float32),
            pltpu.VMEM(rows, jnp.float32),
            pltpu.VMEM((TAPS, width, LANES), jnp.float32),
            pltpu.VMEM((batch, ROWS, LANES), jnp.float32),
            pltpu.VMEM((2 * batch * ROWS, 6 * LANES), jnp.bfloat16),
            pltpu.VMEM((2 * batch * ROWS, 6 * LANES), jnp.bfloat16),
        ],
    )(own_taps, arrived, spectra, *consts)


STREAMS = 8


def send_kernel(rows_ref, *refs):
    weight_refs, (gate_ref, grad_ref, out_ref, total_ref) = refs[:STREAMS], refs[STREAMS:]
    blocks, width, span = out_ref.shape[0], out_ref.shape[1] // 2, out_ref.shape[2]
    step, steps = pl.program_id(0), pl.num_programs(0)
    count = blocks * gate_ref.shape[1] // total_ref.shape[1]
    sig = jax.nn.sigmoid(gate_ref[...].astype(jnp.float32))
    slopes = (grad_ref[...].astype(jnp.float32) * sig).T.astype(jnp.bfloat16)
    out_ref[pl.ds(step * count, count), width:, :] = slopes.reshape(count, width, span)
    part = weight_refs[0].shape[0]
    sides = []
    for side in range(2):
        refs = weight_refs[side::2]
        term = dot(rows_ref[:, :part], refs[0][...])
        for j in range(1, len(refs)):
            term = term + dot(rows_ref[:, j * part:(j + 1) * part], refs[j][...])
        sides.append(term)
    term = jnp.concatenate(sides, axis=1)

    @pl.when(step == 0)
    def _():
        total_ref[...] = term

    @pl.when((step > 0) & (step < steps - 1))
    def _():
        total_ref[...] += term

    @pl.when(step == steps - 1)
    def _():
        total = total_ref[...] + term
        out_ref[:, :width, :] = total.T.astype(jnp.bfloat16).reshape(blocks, width, span)


def sends(layer_in, w_value, gate, grads, count, steps=4):
    span, depth = layer_in.shape
    channels = w_value.shape[1]
    width = channels // count
    block = pl.BlockSpec((span, channels // steps), lambda i: (0, i))
    streams = [pl.BlockSpec((2 * depth // (steps * STREAMS), channels // 2),
                            functools.partial(lambda j, i: (STREAMS // 2 * i + j // 2, j % 2), j))
               for j in range(STREAMS)]
    return call(
        send_kernel, "sends", 2 * span * depth * channels, 12_500_000, vmem=56, grid=(steps,),
        in_specs=[pl.BlockSpec((span, depth // steps), lambda i: (0, i))] + streams + [block, block],
        out_specs=whole((count, 2 * width, span)),
        out_shape=jax.ShapeDtypeStruct((count, 2 * width, span), jnp.bfloat16),
        scratch_shapes=[pltpu.VMEM((span, channels), jnp.float32)],
    )(layer_in, *[w_value] * STREAMS, gate, grads)


def quarter_kernel(place_ref, rows_ref, others_ref, same_ref, cross_ref, other_ref):
    z = place_ref[0] % 2
    for y in range(4):
        to = slice(y * LANES, (y + 1) * LANES)
        own = pl.ds(pl.multiple_of((2 * y + z) * LANES, LANES), LANES)
        same_ref[:, to] = rows_ref[:, own]
        other_ref[:, to] = others_ref[:, own]
        cross_ref[:, to] = rows_ref[:, pl.ds(pl.multiple_of((2 * y + 1 - z) * LANES, LANES), LANES)]


def quarters_of(place, layer_in):
    span, depth = layer_in.shape
    quarter = jax.ShapeDtypeStruct((span, depth // 4), jnp.bfloat16)
    return call(
        quarter_kernel, "quarters", 0, 5_000_000,
        grid_spec=pltpu.PrefetchScalarGridSpec(
            num_scalar_prefetch=1, grid=(2,),
            in_specs=[pl.BlockSpec((span, depth // 4), lambda i, place: (0, 2 * (place[1] % 2) + i)),
                      pl.BlockSpec((span, depth // 4), lambda i, place: (0, 2 - 2 * (place[1] % 2) + i))],
            out_specs=[pl.BlockSpec((span, 4 * LANES), lambda i, place: (0, i))] * 3),
        out_shape=[quarter] * 3,
    )(place, layer_in, layer_in)


def quad_place():
    seq_at = lax.axis_index("seq")
    return seq_at // 4 % 2 * 2 + seq_at % 2


def share_kernel(half, back_ref, *refs):
    parts, refs = refs[:8], refs[8:]
    if half:
        taps_ref, _, out_ref, back_buf, rows_buf, out_buf, in_sem, out_sem = refs
    else:
        out_ref, back_buf, rows_buf, out_buf, in_sem, out_sem = refs
    span, rows, sent = rows_buf.shape[1], back_buf.shape[0], out_buf.shape[1]
    loads = [pltpu.make_async_copy(back_ref.at[:, pl.ds(0, 4 * span)], back_buf, in_sem.at[8])]
    loads += [pltpu.make_async_copy(part, rows_buf.at[n], in_sem.at[n]) for n, part in enumerate(parts)]
    for load in loads:
        load.start()
    loads[0].wait()
    stores = []
    for side in range(2):
        for load in loads[1 + 4 * side:5 + 4 * side]:
            load.wait()
        first = 8 * (side ^ (lax.axis_index("tp") % 2))
        for two in range(4):
            lanes = slice(two * 256, (two + 1) * 256)
            product = None
            for j in range(4):
                at = pl.multiple_of((quad_place() ^ j) * span, span)
                term = dot(back_buf[:, pl.ds(at, span)], rows_buf[4 * side + j, :, lanes])
                product = term if product is None else product + term
            product = product.astype(jnp.bfloat16)
            n = 4 * side + two
            for m in range(2):
                out_buf[2 * n + m, :rows] = product[:, m * LANES:(m + 1) * LANES]
                if half:
                    out_buf[2 * n + m, rows:] = taps_ref[...]
            store = pltpu.make_async_copy(
                out_buf.at[pl.ds(2 * n, 2)],
                out_ref.at[pl.ds(first + 2 * two, 2), pl.ds(half * rows, sent)], out_sem.at[n])
            store.start()
            stores.append(store)
    for store in stores:
        store.wait()


def shares(back, mine, other, taps=None, before=None):
    span, depth = mine[0].shape
    rows = back.shape[0]
    half = 0 if before is None else 1
    operands = [back, *mine, *other] + ([taps, before] if half else [])
    anywhere = pl.BlockSpec(memory_space=pl.ANY)
    return call(
        functools.partial(share_kernel, half), "shares", 16 * rows * span * depth, 7_000_000, vmem=60,
        in_specs=[anywhere] * 9 + ([pl.BlockSpec(memory_space=pltpu.VMEM), anywhere] if half else []),
        out_specs=anywhere,
        out_shape=jax.ShapeDtypeStruct((16, 2 * rows + 16, LANES), jnp.bfloat16),
        input_output_aliases={10: 0} if half else {},
        scratch_shapes=[
            pltpu.VMEM((rows, 4 * span), jnp.bfloat16), pltpu.VMEM((8, span, depth), jnp.bfloat16),
            pltpu.VMEM((16, rows + 16 * half, LANES), jnp.bfloat16),
            pltpu.SemaphoreType.DMA((9,)), pltpu.SemaphoreType.DMA((8,))],
    )(*operands)


def merge(pair, mine, mate):
    leagues = [[jnp.where(pair == 0, one, two) for one, two in zip(mine, mate)],
               [jnp.where(pair == 0, two, one) for one, two in zip(mine, mate)]]
    size = mine[0].shape[0] // 4
    pieces = []
    for y in range(4):
        league, odd = y // 2, Y_OF[0][y // 2] != y
        for z in range(2):
            at = (2 * odd + z) * size
            pieces += [leagues[league][half][at:at + size] for half in range(2)]
    return jnp.concatenate(pieces, axis=0)


def weight_kernel(*refs):
    share_refs, (taps_ref, weight_ref, tap_sums_ref) = refs[:8], refs[8:]
    for x in range(4):
        totals = [[], []]
        for pair in range(2):
            for half in range(2):
                ref = share_refs[4 * half + x]
                terms = [ref[j].astype(jnp.float32) for j in range(16) if j % 4 // 2 == pair]
                totals[pair].append(sum(terms[1:], terms[0]))
        weight_ref[:, x * 2 * LANES:(x + 1) * 2 * LANES] = merge(0, *totals).T
    z = lax.axis_index("seq") % 2
    lane = lax.broadcasted_iota(jnp.int32, (8, LANES), 1)
    for x in range(8):
        row = jnp.zeros((8, LANES), jnp.float32)
        for n in range(4):
            packed = taps_ref[2 * x + n // 2].astype(jnp.float32)
            packed = jnp.where(z == n % 2, packed[:8], packed[8:])
            packed = packed + pltpu.roll(packed, LANES - 32, 1) + pltpu.roll(packed, LANES - 64, 1)
            row = jnp.where(lane // 32 == n, packed if n == 0 else pltpu.roll(packed, 32 * n, 1), row)
        tap_sums_ref[:, x * LANES:(x + 1) * LANES] = row[:TAPS]


def close_weight(parts):
    count, rows, span = parts.shape
    rows -= 16
    channels = 2 * rows
    return call(
        weight_kernel, "close_weight", 2_000_000, 3_000_000, grid=(1,),
        in_specs=[pl.BlockSpec((count, 64, span), functools.partial(lambda n, i: (0, n, 0), n)) for n in range(8)]
        + [pl.BlockSpec((count, 16, span), lambda i: (0, rows // 16, 0))],
        out_specs=[whole((span, channels)), whole((TAPS, channels))],
        out_shape=[jax.ShapeDtypeStruct((span, channels), jnp.float32),
                   jax.ShapeDtypeStruct((TAPS, channels), jnp.float32)],
    )(*[parts] * 9)


def input_kernel(place_ref, *refs):
    back_refs, mate_refs, (weight_ref, send_ref, keep_ref, own_buf) = refs[:2], refs[2:4], refs[4:]

    @pl.when(pl.program_id(0) == 0)
    def _():
        pair = place_ref[0] // 2
        for half in range(2):
            for x in range(4):
                for odd, mine, other in ((0, 1 + pair, 2 - pair), (1, 3 * pair, 3 - 3 * pair)):
                    for z in range(2):
                        at = ((2 * x + odd) * 2 + z) * 16
                        for ref, y in ((back_refs[half], mine), (mate_refs[half], other)):
                            to = pl.multiple_of(((4 * x + y) * 2 + z) * 32 + half * 16, 16)
                            own_buf[pl.ds(to, 16), :] = ref[at:at + 16, :]

    term = dot(weight_ref[...], own_buf[...])

    @pl.when(pl.program_id(0) < 2)
    def _():
        send_ref[0] = term.astype(jnp.bfloat16)

    @pl.when(pl.program_id(0) >= 2)
    def _():
        keep_ref[0] = term


def input_terms(place, backs, mates, w_value):
    depth, channels = w_value.shape
    rows, span = depth // 4, 256
    return call(
        input_kernel, "input_terms", 2 * span * depth * channels, 12_000_000, vmem=24,
        grid_spec=pltpu.PrefetchScalarGridSpec(
            num_scalar_prefetch=1, grid=(4,),
            in_specs=[pl.BlockSpec((channels // 4, span), lambda i, place: (0, place[0]))] * 2
            + [pl.BlockSpec((channels // 4, span), lambda i, place: (0, 0))] * 2
            + [pl.BlockSpec((rows, channels), lambda i, place: (place[1] ^ ((2 * i + 1 - i // 2) % 4), 0))],
            out_specs=[pl.BlockSpec((1, rows, span), lambda i, place: (jnp.minimum(i, 1), 0, 0)),
                       pl.BlockSpec((1, rows, span), lambda i, place: (jnp.maximum(i - 2, 0), 0, 0))],
            scratch_shapes=[pltpu.VMEM((channels, span), jnp.bfloat16)]),
        out_shape=[jax.ShapeDtypeStruct((2, rows, span), jnp.bfloat16),
                   jax.ShapeDtypeStruct((2, rows, span), jnp.float32)],
    )(place, *backs, *mates, w_value)


def close_kernel(keep_ref, core_ref, chip_ref, out_ref):
    total = keep_ref[0] + core_ref[0].astype(jnp.float32) + chip_ref[...].astype(jnp.float32)
    out_ref[...] = total.T.astype(jnp.bfloat16)


def close_input(keep, core, chip):
    rows, span = chip.shape
    first = pl.BlockSpec((1, 512, span), lambda i: (0, i, 0))
    return call(
        close_kernel, "close_input", 1_000_000, 3_000_000, grid=(rows // 512,),
        in_specs=[first, first, pl.BlockSpec((512, span), lambda i: (i, 0))],
        out_specs=pl.BlockSpec((span, 512), lambda i: (0, i)),
        out_shape=jax.ShapeDtypeStruct((span, rows), jnp.bfloat16))(keep, core, chip)


def gate_kernel(place_ref, one_ref, two_ref, mate_one_ref, mate_two_ref, gate_ref, grad_ref, out_ref):
    mine = [ref[...].astype(jnp.float32) for ref in (one_ref, two_ref)]
    mate = [ref[...].astype(jnp.float32) for ref in (mate_one_ref, mate_two_ref)]
    mixed = merge(place_ref[0] // 2, mine, mate).T
    sig = jax.nn.sigmoid(gate_ref[...].astype(jnp.float32))
    out_ref[...] = (grad_ref[...].astype(jnp.float32) * mixed * sig * (1.0 - sig)).astype(jnp.bfloat16)


def gate_grad(place, backs, mates, gate, grads):
    span, channels = gate.shape
    block = pl.BlockSpec((span, channels // 4), lambda i, place: (0, i))
    return call(
        gate_kernel, "gate_grad", 2_000_000, 2_500_000,
        grid_spec=pltpu.PrefetchScalarGridSpec(
            num_scalar_prefetch=1, grid=(4,),
            in_specs=[pl.BlockSpec((64, span), lambda i, place: (i, 4 + place[0] // 2))] * 2
            + [pl.BlockSpec((64, span), lambda i, place: (i, 1))] * 2 + [block, block],
            out_specs=block),
        out_shape=jax.ShapeDtypeStruct(gate.shape, jnp.bfloat16))(place, *backs, *mates, gate, grads)


def local(layer_in, w_value, short_taps, long_filters, gate_proj, grad_out):
    seq_count = lax.axis_size("seq")
    seq_at, tp_at = lax.axis_index("seq"), lax.axis_index("tp")
    span, depth = layer_in.shape
    channels = w_value.shape[1]
    width = channels // seq_count
    quad_at = quad_place()
    place = jnp.stack([quad_at, tp_at]).astype(jnp.int32)
    cores, chips = [(0, 1), (1, 0), (2, 3), (3, 2)], [(0, 2), (2, 0), (1, 3), (3, 1)]

    def exchange(value, index_groups=None):
        return lax.all_to_all(
            value, "seq", split_axis=0, concat_axis=0, axis_index_groups=index_groups, tiled=True)

    def mates(value):
        return lax.ppermute(value, "seq", [(s, s ^ MATE) for s in range(seq_count)])

    outgoing = sends(layer_in, w_value, gate_proj, grad_out, seq_count)
    rows_in, outgoing = lax.optimization_barrier((layer_in, outgoing))
    arrived = exchange(outgoing)
    same, cross, other = quarters_of(place, rows_in)

    def across(value, flip):
        return lax.ppermute(
            value, ("seq", "tp"), [(4 * s + t, 4 * (s ^ flip) + (t ^ 2)) for s in range(seq_count) for t in range(4)])

    first = across(cross, 1)
    spectra = spectra_of(long_filters)
    same, cross, spectra = lax.optimization_barrier((same, cross, spectra))
    mine = [same, first, mates(same), across(cross, 1 ^ MATE)]

    own_taps = lax.dynamic_slice_in_dim(short_taps, seq_at * width, width, 1)
    def league(value):
        return exchange(value, LEAGUES).reshape(channels // 4, value.shape[2])

    def for_mate(back):
        return mates(jnp.concatenate([
            lax.dynamic_slice_in_dim(back, (quad_at ^ 2) * span, span, 1),
            lax.dynamic_slice_in_dim(back, 4 * span + (1 - quad_at // 2) * span, span, 1)], axis=1))

    back_one, lag_one, taps_one = mixer(own_taps, arrived, spectra, 0)
    arrived, back_one = lax.optimization_barrier((arrived, back_one))
    back_two, lag_two, taps_two = mixer(own_taps, arrived, spectra, 1)
    back_one = league(back_one)
    back_one, back_two, mine = lax.optimization_barrier((back_one, back_two, mine))
    other = [other] + [lax.ppermute(part, "tp", cores) for part in mine[1:]]
    back_two = league(back_two)
    mate_one = for_mate(back_one)
    taps = taps_one + taps_two
    partner = lax.ppermute(taps, "seq", [(s, s ^ 1) for s in range(seq_count)])
    taps = jnp.concatenate([taps[:8], partner[:8]], axis=0)
    outgoing = shares(back_one, mine, other)
    back_two, outgoing, mate_one, taps = lax.optimization_barrier((back_two, outgoing, mate_one, taps))
    mate_two = for_mate(back_two)
    outgoing, mate_two = lax.optimization_barrier((shares(back_two, mine, other, taps, outgoing), mate_two))
    parts = exchange(outgoing, PLANES)
    backs, their = [back_one, back_two], [mate_one, mate_two]

    send, keep = input_terms(place, backs, their, w_value)
    core = lax.ppermute(send, "tp", cores)
    send = (keep[1] + core[1].astype(jnp.float32)).astype(jnp.bfloat16)
    send, lag_one, lag_two = lax.optimization_barrier((send, lag_one, lag_two))
    chip = lax.ppermute(send, "tp", chips)
    grad_filters = filter_grads(lag_one, lag_two)
    grad_input = close_input(keep, core, chip)
    grad_gate = gate_grad(place, backs, their, gate_proj, grad_out)
    parts, grad_input, grad_gate = lax.optimization_barrier((parts, grad_input, grad_gate))
    grad_weight, grad_taps = close_weight(parts)
    return (grad_input, grad_weight, grad_taps, grad_filters, grad_gate)


def solution(mesh):
    in_specs = (
        P("seq", None),
        P(None, "tp"),
        P(None, "tp"),
        P(None, ("tp", "seq"), None),
        P("seq", "tp"),
        P("seq", "tp"),
    )
    out_specs = (
        P("seq", "tp"),
        P("seq", "tp"),
        P(None, "tp"),
        P(None, ("tp", "seq"), None),
        P("seq", "tp"),
    )
    return jax.shard_map(local, mesh=mesh, in_specs=in_specs, out_specs=out_specs, check_vma=False)
```

```python
import functools
import math

import jax
import jax.numpy as jnp
import ml_dtypes
import numpy as np
from jax import lax
from jax.experimental import pallas as pl
from jax.experimental.pallas import tpu as pltpu
from jax.sharding import PartitionSpec as P

LANES = 128
ROWS = 64
LENGTH = ROWS * LANES
TAPS = 7
REACH = TAPS // 2
BATCH = 4
GROUP, GROUPS = 2, 8


def halves(table):
    high = table.astype(ml_dtypes.bfloat16)
    low = (table - high.astype(np.float64)).astype(ml_dtypes.bfloat16)
    return high, low


@functools.lru_cache(maxsize=None)
def tables(blocks):
    half = np.arange(ROWS) + 0.5
    natural = np.arange(ROWS)
    split = (2 * np.arange(blocks)[None, :] + np.arange(2)[:, None]).reshape(-1)

    def first(order):
        turn = 2.0 * math.pi / LANES * np.outer(half, order)
        return halves(np.concatenate([np.cos(turn), -np.sin(turn)], axis=0))

    def last(order):
        turn = 2.0 * math.pi / LANES * np.outer(order, half)
        return halves(np.concatenate([np.cos(turn), -np.sin(turn)], axis=1) / LENGTH)

    split_high, split_low = first(split)
    nat_high, nat_low = first(natural)
    first_split = np.concatenate([split_high, split_low], axis=1)
    first_nat = np.concatenate([nat_high, nat_low, nat_high, nat_low], axis=1)
    inv_split_high, inv_split_low = last(split)
    inv_nat_high, inv_nat_low = last(natural)
    last_split = np.concatenate([inv_split_high, inv_split_high, inv_split_low], axis=1)
    last_nat = np.concatenate([inv_nat_high, inv_nat_high, inv_nat_low], axis=1)
    twist = 2.0 * math.pi / (2 * LENGTH) * np.outer(half, np.arange(LANES))
    twist = np.stack([np.cos(twist), -np.sin(twist)]).astype(np.float32)
    grid = 2.0 * math.pi / LANES * np.outer(np.arange(LANES), np.arange(LANES))
    cos, sin = np.cos(grid), np.sin(grid)

    def stacked(table):
        high, low = halves(table)
        return np.concatenate([high, high, low], axis=0)

    forward = np.block([[cos, -sin], [sin, cos]])
    mirror = np.block([[cos, sin], [sin, -cos]])
    inverse = np.block([[cos, sin], [-sin, cos]])
    pair = np.concatenate([stacked(forward), stacked(mirror)], axis=0)
    both = np.concatenate([stacked(inverse), stacked(np.block([[cos, sin], [sin, -cos]]))], axis=1)
    return {
        "first_split": first_split, "first_nat": first_nat, "twist": twist, "forward": stacked(forward), "pair": pair,
        "inverse": stacked(inverse), "both": both, "last_split": last_split, "last_nat": last_nat,
    }


def cut(value):
    high = value.astype(jnp.bfloat16)
    low = (value - high.astype(jnp.float32)).astype(jnp.bfloat16)
    return high, low


def store_parts(ref, row, col, real, imag):
    real_high, real_low = cut(real)
    imag_high, imag_low = cut(imag)
    parts = (real_high, imag_high, real_low, imag_low, real_high, imag_high)
    for at, part in enumerate(parts):
        ref[row:row + ROWS, col + at * LANES:col + (at + 1) * LANES] = part


def shifted(early, late, step):
    if step == 0:
        return early, late
    lane = lax.broadcasted_iota(jnp.int32, early.shape, 1)
    row = lax.broadcasted_iota(jnp.int32, early.shape, 0)
    count = early.shape[0]
    turned_early = pltpu.roll(early, (-step) % LANES, 1)
    turned_late = pltpu.roll(late, (-step) % LANES, 1)
    if step > 0:
        keep = lane < LANES - step
        beyond = jnp.where(row == count - 1, 0.0, pltpu.roll(turned_early, count - 1, 0))
        return jnp.where(keep, turned_early, turned_late), jnp.where(keep, turned_late, beyond)
    keep = lane >= -step
    before = jnp.where(row == 0, 0.0, pltpu.roll(turned_late, 1, 0))
    return jnp.where(keep, turned_early, before), jnp.where(keep, turned_late, turned_early)


def dot(left, right):
    return jnp.dot(left, right, preferred_element_type=jnp.float32)


Y_OF = ((1, 2), (0, 3))
QUADS = [[(x * 4 + Y_OF[odd][pair]) * 2 + z for pair in range(2) for z in range(2)] for x in range(4) for odd in range(2)]
LEAGUES = [[quad[2 * pair + z] for quad in QUADS for z in range(2)] for pair in range(2)]
PLANES = [[2 * j + z for j in range(16)] for z in range(2)]
MATE = 6


def twisted(array, col, twist_ref):
    real = array[:ROWS, col * LANES:(col + 1) * LANES]
    imag = array[ROWS:, col * LANES:(col + 1) * LANES]
    return real * twist_ref[0] - imag * twist_ref[1], real * twist_ref[1] + imag * twist_ref[0]


def untwisted(array, twist_ref):
    real, imag = array[:, :LANES], array[:, LANES:]
    return jnp.concatenate(
        [real * twist_ref[0] + imag * twist_ref[1], imag * twist_ref[0] - real * twist_ref[1]], axis=0)


def finish(table_ref, one, two):
    high, low = cut(jnp.concatenate([one, two], axis=1))
    return dot(table_ref[...], jnp.concatenate([high, low, high], axis=0))


def spectra_kernel(filters_ref, first_nat_ref, twist_ref, pair_ref, out_ref, kernel_buf):
    for q in range(BATCH):
        at = (pl.program_id(0) % (8 // BATCH)) * BATCH + q
        plus = filters_ref[0, 0, pl.ds(at, ROWS, stride=8), :]
        minus = filters_ref[1, 0, pl.ds(at, ROWS, stride=8), :]
        high, low = cut(jnp.concatenate([plus, minus], axis=1))
        section = dot(first_nat_ref[...], jnp.concatenate([high, high, low, low], axis=0))
        store_parts(kernel_buf, q * ROWS, 0, *twisted(section, 0, twist_ref))
        store_parts(kernel_buf, q * ROWS, 6 * LANES, *twisted(section, 1, twist_ref))
    out_ref[...] = dot(kernel_buf[...], pair_ref[...])


def lag_kernel(lag_one_ref, lag_two_ref, twist_ref, both_ref, last_nat_ref, out_ref):
    parts = jnp.where(pl.program_id(0) < pl.num_programs(0) // 2, lag_one_ref[...], lag_two_ref[...])
    unmixed = dot(jnp.concatenate([parts, parts[:, :2 * LANES]], axis=1), both_ref[...])
    for q in range(BATCH):
        at = (pl.program_id(0) % (8 // BATCH)) * BATCH + q
        rows = slice(q * ROWS, (q + 1) * ROWS)
        pair = finish(last_nat_ref, untwisted(unmixed[rows, :2 * LANES], twist_ref),
                      untwisted(unmixed[rows, 2 * LANES:], twist_ref))
        out_ref[0, 0, pl.ds(at, ROWS, stride=8), :] = pair[:, :LANES]
        out_ref[1, 0, pl.ds(at, ROWS, stride=8), :] = pair[:, LANES:]


def mixer_kernel(
    first, taps_ref, arrived_ref, spectra_ref, first_split_ref, twist_ref, forward_ref, inverse_ref, last_split_ref,
    back_ref, lag_ref, taps_out_ref,
    values_buf, slopes_buf, back_buf, mixed_buf, taps_buf, extra_buf, signal_buf, product_buf,
):
    blocks, total, width = arrived_ref.shape[0], arrived_ref.shape[1] // 2, back_ref.shape[1]
    step = pl.program_id(0)

    @pl.when(step == 0)
    def _():
        for h in range(2):
            part = slice(h * LANES, (h + 1) * LANES)
            for buf, at in ((values_buf, first), (slopes_buf, total + first)):
                buf[h] = arrived_ref[:, at:at + width, part].astype(jnp.float32).reshape(blocks * width, LANES)

    pooled = {}

    def start(g):
        for q in range(g * GROUP, (g + 1) * GROUP):
            c = step * GROUP * GROUPS + q
            early = values_buf[0, pl.ds(c, blocks, stride=width), :]
            late = values_buf[1, pl.ds(c, blocks, stride=width), :]
            sum_early, sum_late = None, None
            for k in range(TAPS):
                one, two = shifted(early, late, k - REACH)
                tap = taps_ref[k, first + c]
                sum_early = tap * one if k == 0 else sum_early + tap * one
                sum_late = tap * two if k == 0 else sum_late + tap * two
            short = jnp.concatenate([sum_early, sum_late], axis=0).astype(jnp.bfloat16)
            conv = short.astype(jnp.float32)
            slope = jnp.concatenate(
                [slopes_buf[h, pl.ds(c, blocks, stride=width), :] for h in range(2)], axis=0)
            sig = jax.nn.sigmoid(conv)
            pooled[q] = jnp.sum(conv * sig, keepdims=True) / LENGTH
            mean_grad = jnp.sum(slope, keepdims=True) / LENGTH
            extra_buf[q] = mean_grad * (sig * (1.0 + conv * (1.0 - sig)))
            both = jnp.concatenate([short, slope.astype(jnp.bfloat16)], axis=1)
            section = dot(first_split_ref[...], jnp.concatenate([both, both], axis=0))
            store_parts(signal_buf, 2 * q * ROWS, 0, *twisted(section, 0, twist_ref))
            store_parts(signal_buf, (2 * q + 1) * ROWS, 0, *twisted(section, 1, twist_ref))

    def multiply(g):
        base = 2 * g * GROUP * ROWS
        spec = dot(signal_buf[base:base + 2 * GROUP * ROWS], forward_ref[...])
        for q in range(GROUP):
            short, slope = spec[2 * q * ROWS:(2 * q + 1) * ROWS], spec[(2 * q + 1) * ROWS:(2 * q + 2) * ROWS]
            rows = slice((g * GROUP + q) * ROWS, (g * GROUP + q + 1) * ROWS)
            short_re, short_im = short[:, :LANES], short[:, LANES:]
            slope_re, slope_im = slope[:, :LANES], slope[:, LANES:]
            filt_re, filt_im = spectra_ref[rows, :LANES], spectra_ref[rows, LANES:]
            store_parts(product_buf, base + 2 * q * ROWS, 0,
                        short_re * filt_re - short_im * filt_im, short_re * filt_im + short_im * filt_re)
            store_parts(product_buf, base + (2 * q + 1) * ROWS, 0,
                        slope_re * filt_re + slope_im * filt_im, slope_im * filt_re - slope_re * filt_im)
            real_high, real_low = cut(slope_re * short_re + slope_im * short_im)
            imag_high, imag_low = cut(slope_im * short_re - slope_re * short_im)
            for at, part in enumerate((real_high, imag_high, real_low, imag_low)):
                lag_ref[rows, at * LANES:(at + 1) * LANES] = part

    def end(g):
        base = 2 * g * GROUP * ROWS
        unmixed = dot(product_buf[base:base + 2 * GROUP * ROWS], inverse_ref[...])
        for q in range(GROUP):
            c = step * GROUP * GROUPS + g * GROUP + q
            rows = 2 * q * ROWS
            long_pair = finish(last_split_ref, untwisted(unmixed[rows:rows + ROWS], twist_ref),
                               untwisted(unmixed[rows + ROWS:rows + 2 * ROWS], twist_ref))
            mixed = long_pair[:, :LANES] + pooled[g * GROUP + q]
            slope_back = long_pair[:, LANES:] + extra_buf[g * GROUP + q]
            slope_back = slope_back.astype(jnp.bfloat16).astype(jnp.float32)
            early = values_buf[0, pl.ds(c, blocks, stride=width), :]
            late = values_buf[1, pl.ds(c, blocks, stride=width), :]
            sum_early, sum_late = None, None
            for k in range(TAPS):
                one, two = shifted(slope_back[:blocks], slope_back[blocks:], REACH - k)
                tap = taps_ref[k, first + c]
                sum_early = tap * one if k == 0 else sum_early + tap * one
                sum_late = tap * two if k == 0 else sum_late + tap * two
                taps_buf[k, pl.ds(c, 1), :] = jnp.sum(one * early + two * late, axis=0, keepdims=True)
            for h, part in enumerate((sum_early, sum_late)):
                back_buf[h, pl.ds(c, blocks, stride=width), :] = part
                mixed_buf[h, pl.ds(c, blocks, stride=width), :] = mixed[h * blocks:(h + 1) * blocks]

    for turn in range(GROUPS + 2):
        if turn >= 2:
            end(turn - 2)
        if 1 <= turn <= GROUPS:
            multiply(turn - 1)
        if turn < GROUPS:
            start(turn)

    @pl.when(step == pl.num_programs(0) - 1)
    def _():
        for q, quad in enumerate(QUADS):
            for place, s in enumerate(quad):
                rows = slice(s * width, (s + 1) * width)
                for h in range(2):
                    part = back_buf[h, rows, :].astype(jnp.bfloat16)
                    lanes = slice((2 * place + h) * LANES, (2 * place + h + 1) * LANES)
                    back_ref[2 * q, :, lanes] = part
                    back_ref[2 * q + 1, :, lanes] = part
                    at = 8 + 2 * (place // 2) + h
                    back_ref[2 * q + place % 2, :, at * LANES:(at + 1) * LANES] = (
                        mixed_buf[h, rows, :].astype(jnp.bfloat16))
        lane = lax.broadcasted_iota(jnp.int32, (width, LANES), 1)
        packed = jnp.zeros((width, LANES), jnp.float32)
        for k in range(TAPS):
            rest = jnp.sum(taps_buf[k], axis=1, keepdims=True)
            for p in range(3):
                piece = rest.astype(jnp.bfloat16).astype(jnp.float32)
                packed = jnp.where(lane == 8 * p + k, piece, packed)
                rest = rest - piece
        packed = jnp.concatenate([packed, jnp.zeros((LANES - width, LANES), jnp.float32)], axis=0).T
        rows = pltpu.roll(packed[8:16], total + first, 1) + pltpu.roll(packed[16:24], 2 * total + first, 1)
        rows = rows + (pltpu.roll(packed[:8], first, 1) if first else packed[:8])
        taps_out_ref[...] = jnp.concatenate([rows, jnp.zeros_like(rows)], axis=0).astype(jnp.bfloat16)


def whole(shape):
    return pl.BlockSpec(shape, lambda *_: (0,) * len(shape))


def call(kernel, name, flops, nbytes, vmem=16, **kwargs):
    return pl.pallas_call(
        kernel, name=name,
        compiler_params=pltpu.CompilerParams(vmem_limit_bytes=vmem * 1024 * 1024),
        cost_estimate=pl.CostEstimate(flops=flops, bytes_accessed=nbytes, transcendentals=0), **kwargs)


def tables_of(names, blocks=LENGTH // 256):
    chosen = [jnp.asarray(tables(blocks)[name]) for name in names]
    return chosen, [whole(table.shape) for table in chosen]


PER_TILE = pl.BlockSpec((2, 1, ROWS * 8, LANES), lambda i: (0, i // (8 // BATCH), 0, 0))


def spectra_of(filters):
    width = filters.shape[1]
    tiles = width // 8
    view = filters.reshape(2, tiles, 8, ROWS, LANES).transpose(0, 1, 3, 2, 4).reshape(2, tiles, ROWS * 8, LANES)
    consts, specs = tables_of(("first_nat", "twist", "pair"))
    return call(
        spectra_kernel, "spectra", 3_000_000_000, 5_000_000, vmem=56,
        grid=(width // BATCH,), in_specs=[PER_TILE] + specs,
        out_specs=pl.BlockSpec((BATCH * ROWS, 2 * LANES), lambda i: (i, 0)),
        out_shape=jax.ShapeDtypeStruct((width * ROWS, 2 * LANES), jnp.float32),
        scratch_shapes=[pltpu.VMEM((BATCH * ROWS, 12 * LANES), jnp.bfloat16)],
    )(view, *consts)


def filter_grads(lag_one, lag_two):
    width = 2 * lag_one.shape[0] // ROWS
    tiles, steps = width // 8, width // BATCH // 2
    consts, specs = tables_of(("twist", "both", "last_nat"))
    out = call(
        lag_kernel, "filter_grads", 3_000_000_000, 5_000_000,
        grid=(width // BATCH,),
        in_specs=[pl.BlockSpec((BATCH * ROWS, 4 * LANES), lambda i: (jnp.minimum(i, steps - 1), 0)),
                  pl.BlockSpec((BATCH * ROWS, 4 * LANES), lambda i: (jnp.maximum(i - steps, 0), 0))] + specs,
        out_specs=PER_TILE,
        out_shape=jax.ShapeDtypeStruct((2, tiles, ROWS * 8, LANES), jnp.float32),
    )(lag_one, lag_two, *consts)
    return out.reshape(2, tiles, ROWS, 8, LANES).transpose(0, 1, 3, 2, 4).reshape(2, width, LENGTH)


def mixer(own_taps, arrived, spectra, half):
    blocks, width, span = arrived.shape[0], arrived.shape[1] // 4, arrived.shape[2]
    consts, specs = tables_of(("first_split", "twist", "forward", "inverse", "last_split"))
    back_shape = (blocks // 2, width, 6 * span)
    rows, batch = (2, blocks * width, LANES), GROUP * GROUPS
    return call(
        functools.partial(mixer_kernel, half * width), "mixer", 9_000_000_000, 4_000_000, vmem=56,
        grid=(width // batch,),
        in_specs=[pl.BlockSpec(memory_space=pltpu.SMEM), whole(arrived.shape),
                  pl.BlockSpec((batch * ROWS, 2 * LANES), lambda i: (half * (width // batch) + i, 0))] + specs,
        out_specs=[whole(back_shape), pl.BlockSpec((batch * ROWS, 4 * LANES), lambda i: (i, 0)), whole((16, LANES))],
        out_shape=[
            jax.ShapeDtypeStruct(back_shape, jnp.bfloat16),
            jax.ShapeDtypeStruct((width * ROWS, 4 * LANES), jnp.bfloat16),
            jax.ShapeDtypeStruct((16, LANES), jnp.bfloat16),
        ],
        scratch_shapes=[
            pltpu.VMEM(rows, jnp.float32),
            pltpu.VMEM(rows, jnp.float32),
            pltpu.VMEM(rows, jnp.float32),
            pltpu.VMEM(rows, jnp.float32),
            pltpu.VMEM((TAPS, width, LANES), jnp.float32),
            pltpu.VMEM((batch, ROWS, LANES), jnp.float32),
            pltpu.VMEM((2 * batch * ROWS, 6 * LANES), jnp.bfloat16),
            pltpu.VMEM((2 * batch * ROWS, 6 * LANES), jnp.bfloat16),
        ],
    )(own_taps, arrived, spectra, *consts)


STREAMS = 8


def send_kernel(rows_ref, *refs):
    weight_refs, (gate_ref, grad_ref, out_ref, total_ref) = refs[:STREAMS], refs[STREAMS:]
    blocks, width, span = out_ref.shape[0], out_ref.shape[1] // 2, out_ref.shape[2]
    step, steps = pl.program_id(0), pl.num_programs(0)
    count = blocks * gate_ref.shape[1] // total_ref.shape[1]
    sig = jax.nn.sigmoid(gate_ref[...].astype(jnp.float32))
    slopes = (grad_ref[...].astype(jnp.float32) * sig).T.astype(jnp.bfloat16)
    out_ref[pl.ds(step * count, count), width:, :] = slopes.reshape(count, width, span)
    part = weight_refs[0].shape[0]
    sides = []
    for side in range(2):
        refs = weight_refs[side::2]
        term = dot(rows_ref[:, :part], refs[0][...])
        for j in range(1, len(refs)):
            term = term + dot(rows_ref[:, j * part:(j + 1) * part], refs[j][...])
        sides.append(term)
    term = jnp.concatenate(sides, axis=1)

    @pl.when(step == 0)
    def _():
        total_ref[...] = term

    @pl.when((step > 0) & (step < steps - 1))
    def _():
        total_ref[...] += term

    @pl.when(step == steps - 1)
    def _():
        total = total_ref[...] + term
        out_ref[:, :width, :] = total.T.astype(jnp.bfloat16).reshape(blocks, width, span)


def sends(layer_in, w_value, gate, grads, count, steps=4):
    span, depth = layer_in.shape
    channels = w_value.shape[1]
    width = channels // count
    block = pl.BlockSpec((span, channels // steps), lambda i: (0, i))
    streams = [pl.BlockSpec((2 * depth // (steps * STREAMS), channels // 2),
                            functools.partial(lambda j, i: (STREAMS // 2 * i + j // 2, j % 2), j))
               for j in range(STREAMS)]
    return call(
        send_kernel, "sends", 2 * span * depth * channels, 12_500_000, vmem=56, grid=(steps,),
        in_specs=[pl.BlockSpec((span, depth // steps), lambda i: (0, i))] + streams + [block, block],
        out_specs=whole((count, 2 * width, span)),
        out_shape=jax.ShapeDtypeStruct((count, 2 * width, span), jnp.bfloat16),
        scratch_shapes=[pltpu.VMEM((span, channels), jnp.float32)],
    )(layer_in, *[w_value] * STREAMS, gate, grads)


def quarter_kernel(place_ref, rows_ref, others_ref, same_ref, cross_ref, other_ref):
    z = place_ref[0] % 2
    for y in range(4):
        to = slice(y * LANES, (y + 1) * LANES)
        own = pl.ds(pl.multiple_of((2 * y + z) * LANES, LANES), LANES)
        same_ref[:, to] = rows_ref[:, own]
        other_ref[:, to] = others_ref[:, own]
        cross_ref[:, to] = rows_ref[:, pl.ds(pl.multiple_of((2 * y + 1 - z) * LANES, LANES), LANES)]


def quarters_of(place, layer_in):
    span, depth = layer_in.shape
    quarter = jax.ShapeDtypeStruct((span, depth // 4), jnp.bfloat16)
    return call(
        quarter_kernel, "quarters", 0, 5_000_000,
        grid_spec=pltpu.PrefetchScalarGridSpec(
            num_scalar_prefetch=1, grid=(2,),
            in_specs=[pl.BlockSpec((span, depth // 4), lambda i, place: (0, 2 * (place[1] % 2) + i)),
                      pl.BlockSpec((span, depth // 4), lambda i, place: (0, 2 - 2 * (place[1] % 2) + i))],
            out_specs=[pl.BlockSpec((span, 4 * LANES), lambda i, place: (0, i))] * 3),
        out_shape=[quarter] * 3,
    )(place, layer_in, layer_in)


def quad_place():
    seq_at = lax.axis_index("seq")
    return seq_at // 4 % 2 * 2 + seq_at % 2


def share_kernel(half, back_ref, *refs):
    parts, refs = refs[:8], refs[8:]
    if half:
        taps_ref, _, out_ref, back_buf, rows_buf, out_buf, in_sem, out_sem = refs
    else:
        out_ref, back_buf, rows_buf, out_buf, in_sem, out_sem = refs
    span, rows, sent = rows_buf.shape[1], back_buf.shape[0], out_buf.shape[1]
    loads = [pltpu.make_async_copy(back_ref.at[:, pl.ds(0, 4 * span)], back_buf, in_sem.at[8])]
    loads += [pltpu.make_async_copy(part, rows_buf.at[n], in_sem.at[n]) for n, part in enumerate(parts)]
    for load in loads:
        load.start()
    loads[0].wait()
    stores = []
    for side in range(2):
        for load in loads[1 + 4 * side:5 + 4 * side]:
            load.wait()
        first = 8 * (side ^ (lax.axis_index("tp") % 2))
        for two in range(4):
            lanes = slice(two * 256, (two + 1) * 256)
            product = None
            for j in range(4):
                at = pl.multiple_of((quad_place() ^ j) * span, span)
                term = dot(back_buf[:, pl.ds(at, span)], rows_buf[4 * side + j, :, lanes])
                product = term if product is None else product + term
            product = product.astype(jnp.bfloat16)
            n = 4 * side + two
            for m in range(2):
                out_buf[2 * n + m, :rows] = product[:, m * LANES:(m + 1) * LANES]
                if half:
                    out_buf[2 * n + m, rows:] = taps_ref[...]
            store = pltpu.make_async_copy(
                out_buf.at[pl.ds(2 * n, 2)],
                out_ref.at[pl.ds(first + 2 * two, 2), pl.ds(half * rows, sent)], out_sem.at[n])
            store.start()
            stores.append(store)
    for store in stores:
        store.wait()


def shares(back, mine, other, taps=None, before=None):
    span, depth = mine[0].shape
    rows = back.shape[0]
    half = 0 if before is None else 1
    operands = [back, *mine, *other] + ([taps, before] if half else [])
    anywhere = pl.BlockSpec(memory_space=pl.ANY)
    return call(
        functools.partial(share_kernel, half), "shares", 16 * rows * span * depth, 7_000_000, vmem=60,
        in_specs=[anywhere] * 9 + ([pl.BlockSpec(memory_space=pltpu.VMEM), anywhere] if half else []),
        out_specs=anywhere,
        out_shape=jax.ShapeDtypeStruct((16, 2 * rows + 16, LANES), jnp.bfloat16),
        input_output_aliases={10: 0} if half else {},
        scratch_shapes=[
            pltpu.VMEM((rows, 4 * span), jnp.bfloat16), pltpu.VMEM((8, span, depth), jnp.bfloat16),
            pltpu.VMEM((16, rows + 16 * half, LANES), jnp.bfloat16),
            pltpu.SemaphoreType.DMA((9,)), pltpu.SemaphoreType.DMA((8,))],
    )(*operands)


def merge(pair, mine, mate):
    leagues = [[jnp.where(pair == 0, one, two) for one, two in zip(mine, mate)],
               [jnp.where(pair == 0, two, one) for one, two in zip(mine, mate)]]
    size = mine[0].shape[0] // 4
    pieces = []
    for y in range(4):
        league, odd = y // 2, Y_OF[0][y // 2] != y
        for z in range(2):
            at = (2 * odd + z) * size
            pieces += [leagues[league][half][at:at + size] for half in range(2)]
    return jnp.concatenate(pieces, axis=0)


def weight_kernel(*refs):
    share_refs, (taps_ref, weight_ref, tap_sums_ref) = refs[:8], refs[8:]
    for x in range(4):
        totals = [[], []]
        for pair in range(2):
            for half in range(2):
                ref = share_refs[4 * half + x]
                terms = [ref[j].astype(jnp.float32) for j in range(16) if j % 4 // 2 == pair]
                totals[pair].append(sum(terms[1:], terms[0]))
        weight_ref[:, x * 2 * LANES:(x + 1) * 2 * LANES] = merge(0, *totals).T
    z = lax.axis_index("seq") % 2
    lane = lax.broadcasted_iota(jnp.int32, (8, LANES), 1)
    for x in range(8):
        row = jnp.zeros((8, LANES), jnp.float32)
        for n in range(4):
            packed = taps_ref[2 * x + n // 2].astype(jnp.float32)
            packed = jnp.where(z == n % 2, packed[:8], packed[8:])
            packed = packed + pltpu.roll(packed, LANES - 32, 1) + pltpu.roll(packed, LANES - 64, 1)
            row = jnp.where(lane // 32 == n, packed if n == 0 else pltpu.roll(packed, 32 * n, 1), row)
        tap_sums_ref[:, x * LANES:(x + 1) * LANES] = row[:TAPS]


def close_weight(parts):
    count, rows, span = parts.shape
    rows -= 16
    channels = 2 * rows
    return call(
        weight_kernel, "close_weight", 2_000_000, 3_000_000, grid=(1,),
        in_specs=[pl.BlockSpec((count, 64, span), functools.partial(lambda n, i: (0, n, 0), n)) for n in range(8)]
        + [pl.BlockSpec((count, 16, span), lambda i: (0, rows // 16, 0))],
        out_specs=[whole((span, channels)), whole((TAPS, channels))],
        out_shape=[jax.ShapeDtypeStruct((span, channels), jnp.float32),
                   jax.ShapeDtypeStruct((TAPS, channels), jnp.float32)],
    )(*[parts] * 9)


def input_kernel(place_ref, *refs):
    back_refs, mate_refs, (weight_ref, send_ref, keep_ref, own_buf) = refs[:2], refs[2:4], refs[4:]

    @pl.when(pl.program_id(0) == 0)
    def _():
        pair = place_ref[0] // 2
        for half in range(2):
            for x in range(4):
                for odd, mine, other in ((0, 1 + pair, 2 - pair), (1, 3 * pair, 3 - 3 * pair)):
                    for z in range(2):
                        at = ((2 * x + odd) * 2 + z) * 16
                        for ref, y in ((back_refs[half], mine), (mate_refs[half], other)):
                            to = pl.multiple_of(((4 * x + y) * 2 + z) * 32 + half * 16, 16)
                            own_buf[pl.ds(to, 16), :] = ref[at:at + 16, :]

    term = dot(weight_ref[...], own_buf[...])

    @pl.when(pl.program_id(0) < 2)
    def _():
        send_ref[0] = term.astype(jnp.bfloat16)

    @pl.when(pl.program_id(0) >= 2)
    def _():
        keep_ref[0] = term


def input_terms(place, backs, mates, w_value):
    depth, channels = w_value.shape
    rows, span = depth // 4, 256
    return call(
        input_kernel, "input_terms", 2 * span * depth * channels, 12_000_000, vmem=24,
        grid_spec=pltpu.PrefetchScalarGridSpec(
            num_scalar_prefetch=1, grid=(4,),
            in_specs=[pl.BlockSpec((channels // 4, span), lambda i, place: (0, place[0]))] * 2
            + [pl.BlockSpec((channels // 4, span), lambda i, place: (0, 0))] * 2
            + [pl.BlockSpec((rows, channels), lambda i, place: (place[1] ^ ((2 * i + 1 - i // 2) % 4), 0))],
            out_specs=[pl.BlockSpec((1, rows, span), lambda i, place: (jnp.minimum(i, 1), 0, 0)),
                       pl.BlockSpec((1, rows, span), lambda i, place: (jnp.maximum(i - 2, 0), 0, 0))],
            scratch_shapes=[pltpu.VMEM((channels, span), jnp.bfloat16)]),
        out_shape=[jax.ShapeDtypeStruct((2, rows, span), jnp.bfloat16),
                   jax.ShapeDtypeStruct((2, rows, span), jnp.float32)],
    )(place, *backs, *mates, w_value)


def close_kernel(keep_ref, core_ref, chip_ref, out_ref):
    total = keep_ref[0] + core_ref[0].astype(jnp.float32) + chip_ref[...].astype(jnp.float32)
    out_ref[...] = total.T.astype(jnp.bfloat16)


def close_input(keep, core, chip):
    rows, span = chip.shape
    first = pl.BlockSpec((1, 512, span), lambda i: (0, i, 0))
    return call(
        close_kernel, "close_input", 1_000_000, 3_000_000, grid=(rows // 512,),
        in_specs=[first, first, pl.BlockSpec((512, span), lambda i: (i, 0))],
        out_specs=pl.BlockSpec((span, 512), lambda i: (0, i)),
        out_shape=jax.ShapeDtypeStruct((span, rows), jnp.bfloat16))(keep, core, chip)


def gate_kernel(place_ref, one_ref, two_ref, mate_one_ref, mate_two_ref, gate_ref, grad_ref, out_ref):
    mine = [ref[...].astype(jnp.float32) for ref in (one_ref, two_ref)]
    mate = [ref[...].astype(jnp.float32) for ref in (mate_one_ref, mate_two_ref)]
    mixed = merge(place_ref[0] // 2, mine, mate).T
    sig = jax.nn.sigmoid(gate_ref[...].astype(jnp.float32))
    out_ref[...] = (grad_ref[...].astype(jnp.float32) * mixed * sig * (1.0 - sig)).astype(jnp.bfloat16)


def gate_grad(place, backs, mates, gate, grads):
    span, channels = gate.shape
    block = pl.BlockSpec((span, channels // 4), lambda i, place: (0, i))
    return call(
        gate_kernel, "gate_grad", 2_000_000, 2_500_000,
        grid_spec=pltpu.PrefetchScalarGridSpec(
            num_scalar_prefetch=1, grid=(4,),
            in_specs=[pl.BlockSpec((64, span), lambda i, place: (i, 4 + place[0] // 2))] * 2
            + [pl.BlockSpec((64, span), lambda i, place: (i, 1))] * 2 + [block, block],
            out_specs=block),
        out_shape=jax.ShapeDtypeStruct(gate.shape, jnp.bfloat16))(place, *backs, *mates, gate, grads)


def local(layer_in, w_value, short_taps, long_filters, gate_proj, grad_out):
    seq_count = lax.axis_size("seq")
    seq_at, tp_at = lax.axis_index("seq"), lax.axis_index("tp")
    span, depth = layer_in.shape
    channels = w_value.shape[1]
    width = channels // seq_count
    quad_at = quad_place()
    place = jnp.stack([quad_at, tp_at]).astype(jnp.int32)
    cores, chips = [(0, 1), (1, 0), (2, 3), (3, 2)], [(0, 2), (2, 0), (1, 3), (3, 1)]

    def exchange(value, index_groups=None):
        return lax.all_to_all(
            value, "seq", split_axis=0, concat_axis=0, axis_index_groups=index_groups, tiled=True)

    def mates(value):
        return lax.ppermute(value, "seq", [(s, s ^ MATE) for s in range(seq_count)])

    outgoing = sends(layer_in, w_value, gate_proj, grad_out, seq_count)
    rows_in, outgoing = lax.optimization_barrier((layer_in, outgoing))
    arrived = exchange(outgoing)
    same, cross, other = quarters_of(place, rows_in)

    def across(value, flip):
        return lax.ppermute(
            value, ("seq", "tp"), [(4 * s + t, 4 * (s ^ flip) + (t ^ 2)) for s in range(seq_count) for t in range(4)])

    first = across(cross, 1)
    spectra = spectra_of(long_filters)
    same, cross, spectra = lax.optimization_barrier((same, cross, spectra))
    mine = [same, first, mates(same), across(cross, 1 ^ MATE)]

    own_taps = lax.dynamic_slice_in_dim(short_taps, seq_at * width, width, 1)
    def league(value):
        return exchange(value, LEAGUES).reshape(channels // 4, value.shape[2])

    def for_mate(back):
        return mates(jnp.concatenate([
            lax.dynamic_slice_in_dim(back, (quad_at ^ 2) * span, span, 1),
            lax.dynamic_slice_in_dim(back, 4 * span + (1 - quad_at // 2) * span, span, 1)], axis=1))

    back_one, lag_one, taps_one = mixer(own_taps, arrived, spectra, 0)
    arrived, back_one = lax.optimization_barrier((arrived, back_one))
    back_two, lag_two, taps_two = mixer(own_taps, arrived, spectra, 1)
    back_one = league(back_one)
    back_one, back_two, mine = lax.optimization_barrier((back_one, back_two, mine))
    other = [other] + [lax.ppermute(part, "tp", cores) for part in mine[1:]]
    back_two = league(back_two)
    mate_one = for_mate(back_one)
    taps = taps_one + taps_two
    partner = lax.ppermute(taps, "seq", [(s, s ^ 1) for s in range(seq_count)])
    taps = jnp.concatenate([taps[:8], partner[:8]], axis=0)
    outgoing = shares(back_one, mine, other)
    back_two, outgoing, mate_one = lax.optimization_barrier((back_two, outgoing, mate_one))
    mate_two = for_mate(back_two)
    outgoing, mate_two = lax.optimization_barrier((shares(back_two, mine, other, taps, outgoing), mate_two))
    parts = exchange(outgoing, PLANES)
    backs, their = [back_one, back_two], [mate_one, mate_two]

    send, keep = input_terms(place, backs, their, w_value)
    core = lax.ppermute(send, "tp", cores)
    send = (keep[1] + core[1].astype(jnp.float32)).astype(jnp.bfloat16)
    send, lag_one, lag_two = lax.optimization_barrier((send, lag_one, lag_two))
    chip = lax.ppermute(send, "tp", chips)
    grad_filters = filter_grads(lag_one, lag_two)
    grad_input = close_input(keep, core, chip)
    grad_gate = gate_grad(place, backs, their, gate_proj, grad_out)
    parts, grad_input, grad_gate = lax.optimization_barrier((parts, grad_input, grad_gate))
    grad_weight, grad_taps = close_weight(parts)
    return (grad_input, grad_weight, grad_taps, grad_filters, grad_gate)


def solution(mesh):
    in_specs = (
        P("seq", None),
        P(None, "tp"),
        P(None, "tp"),
        P(None, ("tp", "seq"), None),
        P("seq", "tp"),
        P("seq", "tp"),
    )
    out_specs = (
        P("seq", "tp"),
        P("seq", "tp"),
        P(None, "tp"),
        P(None, ("tp", "seq"), None),
        P("seq", "tp"),
    )
    return jax.shard_map(local, mesh=mesh, in_specs=in_specs, out_specs=out_specs, check_vma=False)
```

```python
import functools
import math

import jax
import jax.numpy as jnp
import ml_dtypes
import numpy as np
from jax import lax
from jax.experimental import pallas as pl
from jax.experimental.pallas import tpu as pltpu
from jax.sharding import PartitionSpec as P

LANES = 128
ROWS = 64
LENGTH = ROWS * LANES
TAPS = 7
REACH = TAPS // 2
BATCH = 4
GROUP, GROUPS = 2, 8


def halves(table):
    high = table.astype(ml_dtypes.bfloat16)
    low = (table - high.astype(np.float64)).astype(ml_dtypes.bfloat16)
    return high, low


@functools.lru_cache(maxsize=None)
def tables(blocks):
    half = np.arange(ROWS) + 0.5
    natural = np.arange(ROWS)
    split = (2 * np.arange(blocks)[None, :] + np.arange(2)[:, None]).reshape(-1)

    def first(order):
        turn = 2.0 * math.pi / LANES * np.outer(half, order)
        return halves(np.concatenate([np.cos(turn), -np.sin(turn)], axis=0))

    def last(order):
        turn = 2.0 * math.pi / LANES * np.outer(order, half)
        return halves(np.concatenate([np.cos(turn), -np.sin(turn)], axis=1) / LENGTH)

    split_high, split_low = first(split)
    nat_high, nat_low = first(natural)
    first_split = np.concatenate([split_high, split_low], axis=1)
    first_nat = np.concatenate([nat_high, nat_low, nat_high, nat_low], axis=1)
    inv_split_high, inv_split_low = last(split)
    inv_nat_high, inv_nat_low = last(natural)
    last_split = np.concatenate([inv_split_high, inv_split_high, inv_split_low], axis=1)
    last_nat = np.concatenate([inv_nat_high, inv_nat_high, inv_nat_low], axis=1)
    twist = 2.0 * math.pi / (2 * LENGTH) * np.outer(half, np.arange(LANES))
    twist = np.stack([np.cos(twist), -np.sin(twist)]).astype(np.float32)
    grid = 2.0 * math.pi / LANES * np.outer(np.arange(LANES), np.arange(LANES))
    cos, sin = np.cos(grid), np.sin(grid)

    def stacked(table):
        high, low = halves(table)
        return np.concatenate([high, high, low], axis=0)

    forward = np.block([[cos, -sin], [sin, cos]])
    mirror = np.block([[cos, sin], [sin, -cos]])
    inverse = np.block([[cos, sin], [-sin, cos]])
    pair = np.concatenate([stacked(forward), stacked(mirror)], axis=0)
    both = np.concatenate([stacked(inverse), stacked(np.block([[cos, sin], [sin, -cos]]))], axis=1)
    return {
        "first_split": first_split, "first_nat": first_nat, "twist": twist, "forward": stacked(forward), "pair": pair,
        "inverse": stacked(inverse), "both": both, "last_split": last_split, "last_nat": last_nat,
    }


def cut(value):
    high = value.astype(jnp.bfloat16)
    low = (value - high.astype(jnp.float32)).astype(jnp.bfloat16)
    return high, low


def store_parts(ref, row, col, real, imag):
    real_high, real_low = cut(real)
    imag_high, imag_low = cut(imag)
    parts = (real_high, imag_high, real_low, imag_low, real_high, imag_high)
    for at, part in enumerate(parts):
        ref[row:row + ROWS, col + at * LANES:col + (at + 1) * LANES] = part


def shifted(early, late, step):
    if step == 0:
        return early, late
    lane = lax.broadcasted_iota(jnp.int32, early.shape, 1)
    row = lax.broadcasted_iota(jnp.int32, early.shape, 0)
    count = early.shape[0]
    turned_early = pltpu.roll(early, (-step) % LANES, 1)
    turned_late = pltpu.roll(late, (-step) % LANES, 1)
    if step > 0:
        keep = lane < LANES - step
        beyond = jnp.where(row == count - 1, 0.0, pltpu.roll(turned_early, count - 1, 0))
        return jnp.where(keep, turned_early, turned_late), jnp.where(keep, turned_late, beyond)
    keep = lane >= -step
    before = jnp.where(row == 0, 0.0, pltpu.roll(turned_late, 1, 0))
    return jnp.where(keep, turned_early, before), jnp.where(keep, turned_late, turned_early)


def dot(left, right):
    return jnp.dot(left, right, preferred_element_type=jnp.float32)


Y_OF = ((1, 2), (0, 3))
QUADS = [[(x * 4 + Y_OF[odd][pair]) * 2 + z for pair in range(2) for z in range(2)] for x in range(4) for odd in range(2)]
LEAGUES = [[quad[2 * pair + z] for quad in QUADS for z in range(2)] for pair in range(2)]
PLANES = [[2 * j + z for j in range(16)] for z in range(2)]
MATE = 6


def twisted(array, col, twist_ref):
    real = array[:ROWS, col * LANES:(col + 1) * LANES]
    imag = array[ROWS:, col * LANES:(col + 1) * LANES]
    return real * twist_ref[0] - imag * twist_ref[1], real * twist_ref[1] + imag * twist_ref[0]


def untwisted(array, twist_ref):
    real, imag = array[:, :LANES], array[:, LANES:]
    return jnp.concatenate(
        [real * twist_ref[0] + imag * twist_ref[1], imag * twist_ref[0] - real * twist_ref[1]], axis=0)


def finish(table_ref, one, two):
    high, low = cut(jnp.concatenate([one, two], axis=1))
    return dot(table_ref[...], jnp.concatenate([high, low, high], axis=0))


def spectra_kernel(filters_ref, first_nat_ref, twist_ref, pair_ref, out_ref, kernel_buf):
    for q in range(BATCH):
        at = (pl.program_id(0) % (8 // BATCH)) * BATCH + q
        plus = filters_ref[0, 0, pl.ds(at, ROWS, stride=8), :]
        minus = filters_ref[1, 0, pl.ds(at, ROWS, stride=8), :]
        high, low = cut(jnp.concatenate([plus, minus], axis=1))
        section = dot(first_nat_ref[...], jnp.concatenate([high, high, low, low], axis=0))
        store_parts(kernel_buf, q * ROWS, 0, *twisted(section, 0, twist_ref))
        store_parts(kernel_buf, q * ROWS, 6 * LANES, *twisted(section, 1, twist_ref))
    out_ref[...] = dot(kernel_buf[...], pair_ref[...])


def lag_kernel(lag_one_ref, lag_two_ref, twist_ref, both_ref, last_nat_ref, out_ref):
    parts = jnp.where(pl.program_id(0) < pl.num_programs(0) // 2, lag_one_ref[...], lag_two_ref[...])
    unmixed = dot(jnp.concatenate([parts, parts[:, :2 * LANES]], axis=1), both_ref[...])
    for q in range(BATCH):
        at = (pl.program_id(0) % (8 // BATCH)) * BATCH + q
        rows = slice(q * ROWS, (q + 1) * ROWS)
        pair = finish(last_nat_ref, untwisted(unmixed[rows, :2 * LANES], twist_ref),
                      untwisted(unmixed[rows, 2 * LANES:], twist_ref))
        out_ref[0, 0, pl.ds(at, ROWS, stride=8), :] = pair[:, :LANES]
        out_ref[1, 0, pl.ds(at, ROWS, stride=8), :] = pair[:, LANES:]


def mixer_kernel(
    first, taps_ref, arrived_ref, spectra_ref, first_split_ref, twist_ref, forward_ref, inverse_ref, last_split_ref,
    back_ref, lag_ref, taps_out_ref,
    values_buf, slopes_buf, back_buf, mixed_buf, taps_buf, extra_buf, signal_buf, product_buf,
):
    blocks, total, width = arrived_ref.shape[0], arrived_ref.shape[1] // 2, back_ref.shape[1]
    step = pl.program_id(0)

    @pl.when(step == 0)
    def _():
        for h in range(2):
            part = slice(h * LANES, (h + 1) * LANES)
            for buf, at in ((values_buf, first), (slopes_buf, total + first)):
                buf[h] = arrived_ref[:, at:at + width, part].astype(jnp.float32).reshape(blocks * width, LANES)

    pooled = {}

    def start(g):
        for q in range(g * GROUP, (g + 1) * GROUP):
            c = step * GROUP * GROUPS + q
            early = values_buf[0, pl.ds(c, blocks, stride=width), :]
            late = values_buf[1, pl.ds(c, blocks, stride=width), :]
            sum_early, sum_late = None, None
            for k in range(TAPS):
                one, two = shifted(early, late, k - REACH)
                tap = taps_ref[k, first + c]
                sum_early = tap * one if k == 0 else sum_early + tap * one
                sum_late = tap * two if k == 0 else sum_late + tap * two
            short = jnp.concatenate([sum_early, sum_late], axis=0).astype(jnp.bfloat16)
            conv = short.astype(jnp.float32)
            slope = jnp.concatenate(
                [slopes_buf[h, pl.ds(c, blocks, stride=width), :] for h in range(2)], axis=0)
            sig = jax.nn.sigmoid(conv)
            pooled[q] = jnp.sum(conv * sig, keepdims=True) / LENGTH
            mean_grad = jnp.sum(slope, keepdims=True) / LENGTH
            extra_buf[q] = mean_grad * (sig * (1.0 + conv * (1.0 - sig)))
            both = jnp.concatenate([short, slope.astype(jnp.bfloat16)], axis=1)
            section = dot(first_split_ref[...], jnp.concatenate([both, both], axis=0))
            store_parts(signal_buf, 2 * q * ROWS, 0, *twisted(section, 0, twist_ref))
            store_parts(signal_buf, (2 * q + 1) * ROWS, 0, *twisted(section, 1, twist_ref))

    def multiply(g):
        base = 2 * g * GROUP * ROWS
        spec = dot(signal_buf[base:base + 2 * GROUP * ROWS], forward_ref[...])
        for q in range(GROUP):
            short, slope = spec[2 * q * ROWS:(2 * q + 1) * ROWS], spec[(2 * q + 1) * ROWS:(2 * q + 2) * ROWS]
            rows = slice((g * GROUP + q) * ROWS, (g * GROUP + q + 1) * ROWS)
            short_re, short_im = short[:, :LANES], short[:, LANES:]
            slope_re, slope_im = slope[:, :LANES], slope[:, LANES:]
            filt_re, filt_im = spectra_ref[rows, :LANES], spectra_ref[rows, LANES:]
            store_parts(product_buf, base + 2 * q * ROWS, 0,
                        short_re * filt_re - short_im * filt_im, short_re * filt_im + short_im * filt_re)
            store_parts(product_buf, base + (2 * q + 1) * ROWS, 0,
                        slope_re * filt_re + slope_im * filt_im, slope_im * filt_re - slope_re * filt_im)
            real_high, real_low = cut(slope_re * short_re + slope_im * short_im)
            imag_high, imag_low = cut(slope_im * short_re - slope_re * short_im)
            for at, part in enumerate((real_high, imag_high, real_low, imag_low)):
                lag_ref[rows, at * LANES:(at + 1) * LANES] = part

    def end(g):
        base = 2 * g * GROUP * ROWS
        unmixed = dot(product_buf[base:base + 2 * GROUP * ROWS], inverse_ref[...])
        for q in range(GROUP):
            c = step * GROUP * GROUPS + g * GROUP + q
            rows = 2 * q * ROWS
            long_pair = finish(last_split_ref, untwisted(unmixed[rows:rows + ROWS], twist_ref),
                               untwisted(unmixed[rows + ROWS:rows + 2 * ROWS], twist_ref))
            mixed = long_pair[:, :LANES] + pooled[g * GROUP + q]
            slope_back = long_pair[:, LANES:] + extra_buf[g * GROUP + q]
            slope_back = slope_back.astype(jnp.bfloat16).astype(jnp.float32)
            early = values_buf[0, pl.ds(c, blocks, stride=width), :]
            late = values_buf[1, pl.ds(c, blocks, stride=width), :]
            sum_early, sum_late = None, None
            for k in range(TAPS):
                one, two = shifted(slope_back[:blocks], slope_back[blocks:], REACH - k)
                tap = taps_ref[k, first + c]
                sum_early = tap * one if k == 0 else sum_early + tap * one
                sum_late = tap * two if k == 0 else sum_late + tap * two
                taps_buf[k, pl.ds(c, 1), :] = jnp.sum(one * early + two * late, axis=0, keepdims=True)
            for h, part in enumerate((sum_early, sum_late)):
                back_buf[h, pl.ds(c, blocks, stride=width), :] = part
                mixed_buf[h, pl.ds(c, blocks, stride=width), :] = mixed[h * blocks:(h + 1) * blocks]

    for turn in range(GROUPS + 2):
        if turn >= 2:
            end(turn - 2)
        if 1 <= turn <= GROUPS:
            multiply(turn - 1)
        if turn < GROUPS:
            start(turn)

    @pl.when(step == pl.num_programs(0) - 1)
    def _():
        for q, quad in enumerate(QUADS):
            for place, s in enumerate(quad):
                rows = slice(s * width, (s + 1) * width)
                for h in range(2):
                    part = back_buf[h, rows, :].astype(jnp.bfloat16)
                    lanes = slice((2 * place + h) * LANES, (2 * place + h + 1) * LANES)
                    back_ref[2 * q, :, lanes] = part
                    back_ref[2 * q + 1, :, lanes] = part
                    at = 8 + 2 * (place // 2) + h
                    back_ref[2 * q + place % 2, :, at * LANES:(at + 1) * LANES] = (
                        mixed_buf[h, rows, :].astype(jnp.bfloat16))
        lane = lax.broadcasted_iota(jnp.int32, (width, LANES), 1)
        packed = jnp.zeros((width, LANES), jnp.float32)
        for k in range(TAPS):
            rest = jnp.sum(taps_buf[k], axis=1, keepdims=True)
            for p in range(3):
                piece = rest.astype(jnp.bfloat16).astype(jnp.float32)
                packed = jnp.where(lane == 8 * p + k, piece, packed)
                rest = rest - piece
        packed = jnp.concatenate([packed, jnp.zeros((LANES - width, LANES), jnp.float32)], axis=0).T
        rows = pltpu.roll(packed[8:16], total + first, 1) + pltpu.roll(packed[16:24], 2 * total + first, 1)
        rows = rows + (pltpu.roll(packed[:8], first, 1) if first else packed[:8])
        taps_out_ref[...] = jnp.concatenate([rows, jnp.zeros_like(rows)], axis=0).astype(jnp.bfloat16)


def whole(shape):
    return pl.BlockSpec(shape, lambda *_: (0,) * len(shape))


def call(kernel, name, flops, nbytes, vmem=16, **kwargs):
    return pl.pallas_call(
        kernel, name=name,
        compiler_params=pltpu.CompilerParams(vmem_limit_bytes=vmem * 1024 * 1024),
        cost_estimate=pl.CostEstimate(flops=flops, bytes_accessed=nbytes, transcendentals=0), **kwargs)


def tables_of(names, blocks=LENGTH // 256):
    chosen = [jnp.asarray(tables(blocks)[name]) for name in names]
    return chosen, [whole(table.shape) for table in chosen]


PER_TILE = pl.BlockSpec((2, 1, ROWS * 8, LANES), lambda i: (0, i // (8 // BATCH), 0, 0))


def spectra_of(filters):
    width = filters.shape[1]
    tiles = width // 8
    view = filters.reshape(2, tiles, 8, ROWS, LANES).transpose(0, 1, 3, 2, 4).reshape(2, tiles, ROWS * 8, LANES)
    consts, specs = tables_of(("first_nat", "twist", "pair"))
    return call(
        spectra_kernel, "spectra", 3_000_000_000, 5_000_000, vmem=56,
        grid=(width // BATCH,), in_specs=[PER_TILE] + specs,
        out_specs=pl.BlockSpec((BATCH * ROWS, 2 * LANES), lambda i: (i, 0)),
        out_shape=jax.ShapeDtypeStruct((width * ROWS, 2 * LANES), jnp.float32),
        scratch_shapes=[pltpu.VMEM((BATCH * ROWS, 12 * LANES), jnp.bfloat16)],
    )(view, *consts)


def filter_grads(lag_one, lag_two):
    width = 2 * lag_one.shape[0] // ROWS
    tiles, steps = width // 8, width // BATCH // 2
    consts, specs = tables_of(("twist", "both", "last_nat"))
    out = call(
        lag_kernel, "filter_grads", 3_000_000_000, 5_000_000,
        grid=(width // BATCH,),
        in_specs=[pl.BlockSpec((BATCH * ROWS, 4 * LANES), lambda i: (jnp.minimum(i, steps - 1), 0)),
                  pl.BlockSpec((BATCH * ROWS, 4 * LANES), lambda i: (jnp.maximum(i - steps, 0), 0))] + specs,
        out_specs=PER_TILE,
        out_shape=jax.ShapeDtypeStruct((2, tiles, ROWS * 8, LANES), jnp.float32),
    )(lag_one, lag_two, *consts)
    return out.reshape(2, tiles, ROWS, 8, LANES).transpose(0, 1, 3, 2, 4).reshape(2, width, LENGTH)


def mixer(own_taps, arrived, spectra, half):
    blocks, width, span = arrived.shape[0], arrived.shape[1] // 4, arrived.shape[2]
    consts, specs = tables_of(("first_split", "twist", "forward", "inverse", "last_split"))
    back_shape = (blocks // 2, width, 6 * span)
    rows, batch = (2, blocks * width, LANES), GROUP * GROUPS
    return call(
        functools.partial(mixer_kernel, half * width), "mixer", 9_000_000_000, 4_000_000, vmem=56,
        grid=(width // batch,),
        in_specs=[pl.BlockSpec(memory_space=pltpu.SMEM), whole(arrived.shape),
                  pl.BlockSpec((batch * ROWS, 2 * LANES), lambda i: (half * (width // batch) + i, 0))] + specs,
        out_specs=[whole(back_shape), pl.BlockSpec((batch * ROWS, 4 * LANES), lambda i: (i, 0)), whole((16, LANES))],
        out_shape=[
            jax.ShapeDtypeStruct(back_shape, jnp.bfloat16),
            jax.ShapeDtypeStruct((width * ROWS, 4 * LANES), jnp.bfloat16),
            jax.ShapeDtypeStruct((16, LANES), jnp.bfloat16),
        ],
        scratch_shapes=[
            pltpu.VMEM(rows, jnp.float32),
            pltpu.VMEM(rows, jnp.float32),
            pltpu.VMEM(rows, jnp.float32),
            pltpu.VMEM(rows, jnp.float32),
            pltpu.VMEM((TAPS, width, LANES), jnp.float32),
            pltpu.VMEM((batch, ROWS, LANES), jnp.float32),
            pltpu.VMEM((2 * batch * ROWS, 6 * LANES), jnp.bfloat16),
            pltpu.VMEM((2 * batch * ROWS, 6 * LANES), jnp.bfloat16),
        ],
    )(own_taps, arrived, spectra, *consts)


STREAMS = 8


def send_kernel(rows_ref, *refs):
    weight_refs, (gate_ref, grad_ref, out_ref, total_ref) = refs[:STREAMS], refs[STREAMS:]
    blocks, width, span = out_ref.shape[0], out_ref.shape[1] // 2, out_ref.shape[2]
    step, steps = pl.program_id(0), pl.num_programs(0)
    count = blocks * gate_ref.shape[1] // total_ref.shape[1]
    sig = jax.nn.sigmoid(gate_ref[...].astype(jnp.float32))
    slopes = (grad_ref[...].astype(jnp.float32) * sig).T.astype(jnp.bfloat16)
    out_ref[pl.ds(step * count, count), width:, :] = slopes.reshape(count, width, span)
    part = weight_refs[0].shape[0]
    sides = []
    for side in range(2):
        refs = weight_refs[side::2]
        term = dot(rows_ref[:, :part], refs[0][...])
        for j in range(1, len(refs)):
            term = term + dot(rows_ref[:, j * part:(j + 1) * part], refs[j][...])
        sides.append(term)
    term = jnp.concatenate(sides, axis=1)

    @pl.when(step == 0)
    def _():
        total_ref[...] = term

    @pl.when((step > 0) & (step < steps - 1))
    def _():
        total_ref[...] += term

    @pl.when(step == steps - 1)
    def _():
        total = total_ref[...] + term
        out_ref[:, :width, :] = total.T.astype(jnp.bfloat16).reshape(blocks, width, span)


def sends(layer_in, w_value, gate, grads, count, steps=4):
    span, depth = layer_in.shape
    channels = w_value.shape[1]
    width = channels // count
    block = pl.BlockSpec((span, channels // steps), lambda i: (0, i))
    streams = [pl.BlockSpec((2 * depth // (steps * STREAMS), channels // 2),
                            functools.partial(lambda j, i: (STREAMS // 2 * i + j // 2, j % 2), j))
               for j in range(STREAMS)]
    return call(
        send_kernel, "sends", 2 * span * depth * channels, 12_500_000, vmem=56, grid=(steps,),
        in_specs=[pl.BlockSpec((span, depth // steps), lambda i: (0, i))] + streams + [block, block],
        out_specs=whole((count, 2 * width, span)),
        out_shape=jax.ShapeDtypeStruct((count, 2 * width, span), jnp.bfloat16),
        scratch_shapes=[pltpu.VMEM((span, channels), jnp.float32)],
    )(layer_in, *[w_value] * STREAMS, gate, grads)


def quarter_kernel(place_ref, rows_ref, others_ref, same_ref, cross_ref, other_ref):
    z = place_ref[0] % 2
    for y in range(4):
        to = slice(y * LANES, (y + 1) * LANES)
        own = pl.ds(pl.multiple_of((2 * y + z) * LANES, LANES), LANES)
        same_ref[:, to] = rows_ref[:, own]
        other_ref[:, to] = others_ref[:, own]
        cross_ref[:, to] = rows_ref[:, pl.ds(pl.multiple_of((2 * y + 1 - z) * LANES, LANES), LANES)]


def quarters_of(place, layer_in):
    span, depth = layer_in.shape
    quarter = jax.ShapeDtypeStruct((span, depth // 4), jnp.bfloat16)
    return call(
        quarter_kernel, "quarters", 0, 5_000_000,
        grid_spec=pltpu.PrefetchScalarGridSpec(
            num_scalar_prefetch=1, grid=(2,),
            in_specs=[pl.BlockSpec((span, depth // 4), lambda i, place: (0, 2 * (place[1] % 2) + i)),
                      pl.BlockSpec((span, depth // 4), lambda i, place: (0, 2 - 2 * (place[1] % 2) + i))],
            out_specs=[pl.BlockSpec((span, 4 * LANES), lambda i, place: (0, i))] * 3),
        out_shape=[quarter] * 3,
    )(place, layer_in, layer_in)


def quad_place():
    seq_at = lax.axis_index("seq")
    return seq_at // 4 % 2 * 2 + seq_at % 2


def share_kernel(half, back_ref, *refs):
    parts, refs = refs[:8], refs[8:]
    if half:
        taps_ref, partner_ref, _, out_ref, back_buf, rows_buf, out_buf, in_sem, out_sem = refs
    else:
        out_ref, back_buf, rows_buf, out_buf, in_sem, out_sem = refs
    span, rows, sent = rows_buf.shape[1], back_buf.shape[0], out_buf.shape[1]
    if half:
        taps = [ref[...].astype(jnp.float32)[:8] for ref in (taps_ref, partner_ref)]
        taps = jnp.concatenate(taps, axis=0).astype(jnp.bfloat16)
    loads = [pltpu.make_async_copy(back_ref.at[:, pl.ds(0, 4 * span)], back_buf, in_sem.at[8])]
    loads += [pltpu.make_async_copy(part, rows_buf.at[n], in_sem.at[n]) for n, part in enumerate(parts)]
    for load in loads:
        load.start()
    loads[0].wait()
    stores = []
    for side in range(2):
        for load in loads[1 + 4 * side:5 + 4 * side]:
            load.wait()
        first = 8 * (side ^ (lax.axis_index("tp") % 2))
        for two in range(4):
            lanes = slice(two * 256, (two + 1) * 256)
            product = None
            for j in range(4):
                at = pl.multiple_of((quad_place() ^ j) * span, span)
                term = dot(back_buf[:, pl.ds(at, span)], rows_buf[4 * side + j, :, lanes])
                product = term if product is None else product + term
            product = product.astype(jnp.bfloat16)
            n = 4 * side + two
            for m in range(2):
                out_buf[2 * n + m, :rows] = product[:, m * LANES:(m + 1) * LANES]
                if half:
                    out_buf[2 * n + m, rows:] = taps
            store = pltpu.make_async_copy(
                out_buf.at[pl.ds(2 * n, 2)],
                out_ref.at[pl.ds(first + 2 * two, 2), pl.ds(half * rows, sent)], out_sem.at[n])
            store.start()
            stores.append(store)
    for store in stores:
        store.wait()


def shares(back, mine, other, taps=None, before=None):
    span, depth = mine[0].shape
    rows = back.shape[0]
    half = 0 if before is None else 1
    operands = [back, *mine, *other] + ([*taps, before] if half else [])
    anywhere = pl.BlockSpec(memory_space=pl.ANY)
    return call(
        functools.partial(share_kernel, half), "shares", 16 * rows * span * depth, 7_000_000, vmem=60,
        in_specs=[anywhere] * 9 + ([pl.BlockSpec(memory_space=pltpu.VMEM)] * 2 + [anywhere] if half else []),
        out_specs=anywhere,
        out_shape=jax.ShapeDtypeStruct((16, 2 * rows + 16, LANES), jnp.bfloat16),
        input_output_aliases={11: 0} if half else {},
        scratch_shapes=[
            pltpu.VMEM((rows, 4 * span), jnp.bfloat16), pltpu.VMEM((8, span, depth), jnp.bfloat16),
            pltpu.VMEM((16, rows + 16 * half, LANES), jnp.bfloat16),
            pltpu.SemaphoreType.DMA((9,)), pltpu.SemaphoreType.DMA((8,))],
    )(*operands)


def merge(pair, mine, mate):
    leagues = [[jnp.where(pair == 0, one, two) for one, two in zip(mine, mate)],
               [jnp.where(pair == 0, two, one) for one, two in zip(mine, mate)]]
    size = mine[0].shape[0] // 4
    pieces = []
    for y in range(4):
        league, odd = y // 2, Y_OF[0][y // 2] != y
        for z in range(2):
            at = (2 * odd + z) * size
            pieces += [leagues[league][half][at:at + size] for half in range(2)]
    return jnp.concatenate(pieces, axis=0)


def weight_kernel(*refs):
    share_refs, (taps_ref, weight_ref, tap_sums_ref) = refs[:8], refs[8:]
    for x in range(4):
        totals = [[], []]
        for pair in range(2):
            for half in range(2):
                ref = share_refs[4 * half + x]
                terms = [ref[j].astype(jnp.float32) for j in range(16) if j % 4 // 2 == pair]
                totals[pair].append(sum(terms[1:], terms[0]))
        weight_ref[:, x * 2 * LANES:(x + 1) * 2 * LANES] = merge(0, *totals).T
    z = lax.axis_index("seq") % 2
    lane = lax.broadcasted_iota(jnp.int32, (8, LANES), 1)
    for x in range(8):
        row = jnp.zeros((8, LANES), jnp.float32)
        for n in range(4):
            packed = taps_ref[2 * x + n // 2].astype(jnp.float32)
            packed = jnp.where(z == n % 2, packed[:8], packed[8:])
            packed = packed + pltpu.roll(packed, LANES - 32, 1) + pltpu.roll(packed, LANES - 64, 1)
            row = jnp.where(lane // 32 == n, packed if n == 0 else pltpu.roll(packed, 32 * n, 1), row)
        tap_sums_ref[:, x * LANES:(x + 1) * LANES] = row[:TAPS]


def close_weight(parts):
    count, rows, span = parts.shape
    rows -= 16
    channels = 2 * rows
    return call(
        weight_kernel, "close_weight", 2_000_000, 3_000_000, grid=(1,),
        in_specs=[pl.BlockSpec((count, 64, span), functools.partial(lambda n, i: (0, n, 0), n)) for n in range(8)]
        + [pl.BlockSpec((count, 16, span), lambda i: (0, rows // 16, 0))],
        out_specs=[whole((span, channels)), whole((TAPS, channels))],
        out_shape=[jax.ShapeDtypeStruct((span, channels), jnp.float32),
                   jax.ShapeDtypeStruct((TAPS, channels), jnp.float32)],
    )(*[parts] * 9)


def input_kernel(place_ref, *refs):
    back_refs, mate_refs, (weight_ref, send_ref, keep_ref, own_buf) = refs[:2], refs[2:4], refs[4:]

    @pl.when(pl.program_id(0) == 0)
    def _():
        pair = place_ref[0] // 2
        for half in range(2):
            for x in range(4):
                for odd, mine, other in ((0, 1 + pair, 2 - pair), (1, 3 * pair, 3 - 3 * pair)):
                    for z in range(2):
                        at = ((2 * x + odd) * 2 + z) * 16
                        for ref, y in ((back_refs[half], mine), (mate_refs[half], other)):
                            to = pl.multiple_of(((4 * x + y) * 2 + z) * 32 + half * 16, 16)
                            own_buf[pl.ds(to, 16), :] = ref[at:at + 16, :]

    term = dot(weight_ref[...], own_buf[...])

    @pl.when(pl.program_id(0) < 2)
    def _():
        send_ref[0] = term.astype(jnp.bfloat16)

    @pl.when(pl.program_id(0) >= 2)
    def _():
        keep_ref[0] = term


def input_terms(place, backs, mates, w_value):
    depth, channels = w_value.shape
    rows, span = depth // 4, 256
    return call(
        input_kernel, "input_terms", 2 * span * depth * channels, 12_000_000, vmem=24,
        grid_spec=pltpu.PrefetchScalarGridSpec(
            num_scalar_prefetch=1, grid=(4,),
            in_specs=[pl.BlockSpec((channels // 4, span), lambda i, place: (0, place[0]))] * 2
            + [pl.BlockSpec((channels // 4, span), lambda i, place: (0, 0))] * 2
            + [pl.BlockSpec((rows, channels), lambda i, place: (place[1] ^ ((2 * i + 1 - i // 2) % 4), 0))],
            out_specs=[pl.BlockSpec((1, rows, span), lambda i, place: (jnp.minimum(i, 1), 0, 0)),
                       pl.BlockSpec((1, rows, span), lambda i, place: (jnp.maximum(i - 2, 0), 0, 0))],
            scratch_shapes=[pltpu.VMEM((channels, span), jnp.bfloat16)]),
        out_shape=[jax.ShapeDtypeStruct((2, rows, span), jnp.bfloat16),
                   jax.ShapeDtypeStruct((2, rows, span), jnp.float32)],
    )(place, *backs, *mates, w_value)


def close_kernel(keep_ref, core_ref, chip_ref, out_ref):
    total = keep_ref[0] + core_ref[0].astype(jnp.float32) + chip_ref[...].astype(jnp.float32)
    out_ref[...] = total.T.astype(jnp.bfloat16)


def close_input(keep, core, chip):
    rows, span = chip.shape
    first = pl.BlockSpec((1, 512, span), lambda i: (0, i, 0))
    return call(
        close_kernel, "close_input", 1_000_000, 3_000_000, grid=(rows // 512,),
        in_specs=[first, first, pl.BlockSpec((512, span), lambda i: (i, 0))],
        out_specs=pl.BlockSpec((span, 512), lambda i: (0, i)),
        out_shape=jax.ShapeDtypeStruct((span, rows), jnp.bfloat16))(keep, core, chip)


def gate_kernel(place_ref, one_ref, two_ref, mate_one_ref, mate_two_ref, gate_ref, grad_ref, out_ref):
    mine = [ref[...].astype(jnp.float32) for ref in (one_ref, two_ref)]
    mate = [ref[...].astype(jnp.float32) for ref in (mate_one_ref, mate_two_ref)]
    mixed = merge(place_ref[0] // 2, mine, mate).T
    sig = jax.nn.sigmoid(gate_ref[...].astype(jnp.float32))
    out_ref[...] = (grad_ref[...].astype(jnp.float32) * mixed * sig * (1.0 - sig)).astype(jnp.bfloat16)


def gate_grad(place, backs, mates, gate, grads):
    span, channels = gate.shape
    block = pl.BlockSpec((span, channels // 4), lambda i, place: (0, i))
    return call(
        gate_kernel, "gate_grad", 2_000_000, 2_500_000,
        grid_spec=pltpu.PrefetchScalarGridSpec(
            num_scalar_prefetch=1, grid=(4,),
            in_specs=[pl.BlockSpec((64, span), lambda i, place: (i, 4 + place[0] // 2))] * 2
            + [pl.BlockSpec((64, span), lambda i, place: (i, 1))] * 2 + [block, block],
            out_specs=block),
        out_shape=jax.ShapeDtypeStruct(gate.shape, jnp.bfloat16))(place, *backs, *mates, gate, grads)


def local(layer_in, w_value, short_taps, long_filters, gate_proj, grad_out):
    seq_count = lax.axis_size("seq")
    seq_at, tp_at = lax.axis_index("seq"), lax.axis_index("tp")
    span, depth = layer_in.shape
    channels = w_value.shape[1]
    width = channels // seq_count
    quad_at = quad_place()
    place = jnp.stack([quad_at, tp_at]).astype(jnp.int32)
    cores, chips = [(0, 1), (1, 0), (2, 3), (3, 2)], [(0, 2), (2, 0), (1, 3), (3, 1)]

    def exchange(value, index_groups=None):
        return lax.all_to_all(
            value, "seq", split_axis=0, concat_axis=0, axis_index_groups=index_groups, tiled=True)

    def mates(value):
        return lax.ppermute(value, "seq", [(s, s ^ MATE) for s in range(seq_count)])

    outgoing = sends(layer_in, w_value, gate_proj, grad_out, seq_count)
    rows_in, outgoing = lax.optimization_barrier((layer_in, outgoing))
    arrived = exchange(outgoing)
    same, cross, other = quarters_of(place, rows_in)

    def across(value, flip):
        return lax.ppermute(
            value, ("seq", "tp"), [(4 * s + t, 4 * (s ^ flip) + (t ^ 2)) for s in range(seq_count) for t in range(4)])

    first = across(cross, 1)
    spectra = spectra_of(long_filters)
    same, cross, spectra = lax.optimization_barrier((same, cross, spectra))
    mine = [same, first, mates(same), across(cross, 1 ^ MATE)]

    own_taps = lax.dynamic_slice_in_dim(short_taps, seq_at * width, width, 1)
    def league(value):
        return exchange(value, LEAGUES).reshape(channels // 4, value.shape[2])

    def for_mate(back):
        return mates(jnp.concatenate([
            lax.dynamic_slice_in_dim(back, (quad_at ^ 2) * span, span, 1),
            lax.dynamic_slice_in_dim(back, 4 * span + (1 - quad_at // 2) * span, span, 1)], axis=1))

    back_one, lag_one, taps_one = mixer(own_taps, arrived, spectra, 0)
    arrived, back_one = lax.optimization_barrier((arrived, back_one))
    back_two, lag_two, taps_two = mixer(own_taps, arrived, spectra, 1)
    back_one = league(back_one)
    back_one, back_two, mine = lax.optimization_barrier((back_one, back_two, mine))
    other = [other] + [lax.ppermute(part, "tp", cores) for part in mine[1:]]
    back_two = league(back_two)
    mate_one = for_mate(back_one)
    taps = taps_one + taps_two
    partner = lax.ppermute(taps, "seq", [(s, s ^ 1) for s in range(seq_count)])
    outgoing = shares(back_one, mine, other)
    back_two, outgoing, mate_one, partner = lax.optimization_barrier((back_two, outgoing, mate_one, partner))
    mate_two = for_mate(back_two)
    outgoing, mate_two = lax.optimization_barrier((shares(back_two, mine, other, (taps, partner), outgoing), mate_two))
    parts = exchange(outgoing, PLANES)
    backs, their = [back_one, back_two], [mate_one, mate_two]

    send, keep = input_terms(place, backs, their, w_value)
    core = lax.ppermute(send, "tp", cores)
    send = (keep[1] + core[1].astype(jnp.float32)).astype(jnp.bfloat16)
    send, lag_one, lag_two = lax.optimization_barrier((send, lag_one, lag_two))
    chip = lax.ppermute(send, "tp", chips)
    grad_filters = filter_grads(lag_one, lag_two)
    grad_input = close_input(keep, core, chip)
    grad_gate = gate_grad(place, backs, their, gate_proj, grad_out)
    parts, grad_input, grad_gate = lax.optimization_barrier((parts, grad_input, grad_gate))
    grad_weight, grad_taps = close_weight(parts)
    return (grad_input, grad_weight, grad_taps, grad_filters, grad_gate)


def solution(mesh):
    in_specs = (
        P("seq", None),
        P(None, "tp"),
        P(None, "tp"),
        P(None, ("tp", "seq"), None),
        P("seq", "tp"),
        P("seq", "tp"),
    )
    out_specs = (
        P("seq", "tp"),
        P("seq", "tp"),
        P(None, "tp"),
        P(None, ("tp", "seq"), None),
        P("seq", "tp"),
    )
    return jax.shard_map(local, mesh=mesh, in_specs=in_specs, out_specs=out_specs, check_vma=False)
```
